512 devices in a mesh: rollout: 16 (over z), ctx: 32 (over y, x, core).
Axes of the slice: x: 4, y: 4, z: 16, core: 2. Of those that a mesh axis runs over, the one named last changes fastest.
Arguments:
- queries: bfloat16 [16, 4096, 4096], P('rollout', 'ctx'), may hold values from -6 to 6
- keys_values: bfloat16 [16, 2, 4096, 1024], P('rollout', None, 'ctx'), may hold values from -6 to 6
- image_rows: bfloat16 [16, 256, 6144], P('rollout', 'ctx'), may hold values from -6 to 6
- cotangent: bfloat16 [16, 4096, 4096], P('rollout', 'ctx'), may hold values from -96 to 96
- seq_image: int32 [16], replicated, may hold values from 0 to 15, as said below
- vis_start: int32 [16], P('rollout'), may hold values from 1 to 63
- comp_lengths: int32 [16, 16], P('rollout'), may hold values from 1 to 314, 3776 in all within a row
Outputs:
- grad_queries: bfloat16 [16, 4096, 4096], P('rollout', 'ctx')
- grad_keys_values: bfloat16 [16, 2, 4096, 1024], P('rollout', None, 'ctx')
- grad_image: bfloat16 [16, 256, 6144], P('rollout', 'ctx')
The draws below stay inside these ranges and needn't reach their ends.
Inputs may be any that keep to these rules, and one draw needn't show every extreme that they name: `seq_image`: each image belongs to exactly one group. The image's rows take positions vis_start to vis_start + 255 of the group's sequence. `comp_lengths`: each group's lengths sum to 3776.
All inputs are finite; a program needn't handle non-finite values.
Results may differ from the reference program's by a relative error of at most 0.0068.
Values may be sent and summed in bfloat16 or wider, within the bound.
A program may use at most 128 MiB of HBM per device.

```python
import math
import jax
import jax.numpy as jnp
import numpy as np
from jax import lax

HEADS = 32
KV_HEADS = 8
HEAD_DIM = 128
VIS = 256
PROMPT = 64
NCOMP = 16
SEQ = 4096
GROUPS = 16
MOST = 314


def draw_seq_image(key, part):
    key = jax.random.fold_in(key, 7)
    rotation = jax.random.randint(key, (), 0, GROUPS).astype(jnp.int32)
    group_ids = jnp.arange(GROUPS, dtype=jnp.int32)
    moved = (group_ids - rotation) % GROUPS
    half_count = GROUPS // 2
    base_map = jnp.where(moved < half_count, 2 * moved + 1, 2 * moved - GROUPS)
    return ((base_map + rotation) % GROUPS).astype(jnp.int32)


def draw_queries(key, part):
    key = jax.random.fold_in(key, 3)
    noise_shape = (GROUPS, SEQ, HEADS, HEAD_DIM)
    noise_base = jnp.clip(jax.random.normal(key, noise_shape, jnp.float32), -6.0, 6.0)
    return noise_base.reshape(GROUPS, SEQ, HEADS * HEAD_DIM).astype(jnp.bfloat16)


def draw_keys_values(key, part):
    key = jax.random.fold_in(key, 5)
    kv_shape = (GROUPS, 2, SEQ, KV_HEADS, HEAD_DIM)
    noise_base = jnp.clip(jax.random.normal(key, kv_shape, jnp.float32), -6.0, 6.0)
    return noise_base.reshape(GROUPS, 2, SEQ, KV_HEADS * HEAD_DIM).astype(jnp.bfloat16)


def place_ends(values, rng, smallest, high):
    index_at = [jax.random.randint(jax.random.fold_in(rng, axis), (), 0, length) for axis, length in enumerate(values.shape)]
    widest = values.shape.index(max(values.shape))
    beside = index_at[:widest] + [(index_at[widest] + 1) % values.shape[widest]] + index_at[widest + 1:]
    return values.at[tuple(index_at)].set(smallest).at[tuple(beside)].set(high)


def shard_levels(key, extent, cuts, low, largest):
    def one(axis_at, blocks):
        heights = jax.random.uniform(jax.random.fold_in(jax.random.fold_in(key, 6), axis_at), (blocks,), jnp.float32, low / len(cuts), largest / len(cuts))
        return jnp.repeat(jnp.exp(heights), extent[axis_at] // blocks).reshape((-1,) + (1,) * (len(extent) - axis_at - 1))

    factor_of = one(*cuts[0])
    for cut in cuts[1:]:
        factor_of = factor_of * one(*cut)
    return factor_of


def length_profile(amount, total, reach, lean):
    loads = [(1 << 20) // math.isqrt(grade ** lean) + 1 for grade in range(2, amount + 1)]
    spare, given = total - reach - (amount - 1), [1] * (amount - 1)
    while spare > 0:
        free = [i for i in range(amount - 1) if given[i] < reach]
        mass, budget = sum([loads[i] for i in free]), spare
        for i in free:
            more = min(reach - given[i], max(1, budget * loads[i] // mass), spare)
            given[i] = given[i] + more
            spare = spare - more
    return np.array([reach] + given)


def uneven_parts(key, amount, total, reach, lean):
    if amount == 2:
        one = jax.random.randint(key, (), max(1, total - reach), min(reach, total - 1) + 1)
        return jnp.stack([one, total - one])
    sizes = jnp.asarray(length_profile(amount, total, reach, lean), jnp.int32)
    couples = (amount - 1) // 2
    source_of, sink = sizes[1:1 + 2 * couples:2], sizes[2:2 + 2 * couples:2]
    slack = jnp.minimum(source_of - 1, reach - sink)
    moved = jax.random.randint(jax.random.fold_in(key, 1), (couples,), 0, 1 << 20) % (slack + 1)
    sizes = sizes.at[1:1 + 2 * couples:2].set(source_of - moved).at[2:2 + 2 * couples:2].set(sink + moved)
    return sizes[jax.random.permutation(jax.random.fold_in(key, 2), amount)]


def scatter_about(own_key, shape, spread, most, shards=(), held_as=jnp.bfloat16):
    factor_of = shard_levels(own_key, shape, shards, -0.22, 0.18) if shards else 1.0
    entries = jax.random.normal(own_key, shape, jnp.float32) * spread * factor_of
    return jnp.minimum(jnp.maximum(entries, -most), most).astype(held_as)


def setup_inputs(seed: int = 0) -> dict:
    key_list = jax.random.split(jax.random.key(seed), 8)
    queries = draw_queries(jax.random.fold_in(key_list[7], 71), 0)
    keys_values = draw_keys_values(jax.random.fold_in(key_list[7], 71), 0)
    image_rows = scatter_about(key_list[2], (GROUPS, VIS, (HEADS + 2 * KV_HEADS) * HEAD_DIM), 1.0, 6.0, ((0, 16), (1, 32)))
    cotangent = scatter_about(key_list[3], (GROUPS, SEQ, HEADS * HEAD_DIM), 16.0, 96.0, ((0, 16), (1, 32)))
    seq_image = draw_seq_image(jax.random.fold_in(key_list[7], 71), 0)
    vis_start = place_ends(jax.random.randint(key_list[5], (GROUPS,), 1, PROMPT), jax.random.fold_in(key_list[5], 1), 1, PROMPT - 1).astype(jnp.int32)
    comp_lengths = jax.vmap(lambda own: uneven_parts(own, NCOMP, SEQ - VIS - PROMPT, MOST, 2))(jax.random.split(key_list[6], GROUPS)).reshape((GROUPS, NCOMP)).astype(jnp.int32)
    return {"queries": queries, "keys_values": keys_values, "image_rows": image_rows, "cotangent": cotangent, "seq_image": seq_image, "vis_start": vis_start, "comp_lengths": comp_lengths}


neg_large = -1e+30

def segment_table(lengths):
    prefix_len = VIS + PROMPT
    seg_ends = jnp.cumsum(lengths).astype(jnp.int32)
    positions = jnp.arange(SEQ, dtype=jnp.int32)
    later_ends = lax.optimization_barrier(jnp.sum((seg_ends[None, :] <= (positions - prefix_len)[:, None]).astype(jnp.int32), axis=1))
    return jnp.where(positions < prefix_len, 0, 1 + later_ends).astype(jnp.int32)

def rounded(value):
    return lax.optimization_barrier(value.astype(jnp.bfloat16)).astype(jnp.float32)

def head_grads(q_head, k_head, v_head, d_head, visible):
    score_scale = 1.0 / math.sqrt(HEAD_DIM)
    q_float = q_head.astype(jnp.float32)
    k_float = k_head.astype(jnp.float32)
    v_float = v_head.astype(jnp.float32)
    d_float = d_head.astype(jnp.float32)
    scores = jnp.dot(q_float, k_float.T, preferred_element_type=jnp.float32) * score_scale
    scores = jnp.where(visible, scores, neg_large)
    row_top = lax.optimization_barrier(jnp.max(scores, axis=1, keepdims=True))
    exp_terms = jnp.where(visible, jnp.exp(scores - row_top), 0.0)
    weights = exp_terms / lax.optimization_barrier(jnp.sum(exp_terms, axis=1, keepdims=True))
    d_weights = jnp.dot(d_float, v_float.T, preferred_element_type=jnp.float32)
    row_delta = lax.optimization_barrier(jnp.sum(weights * d_weights, axis=1, keepdims=True))
    d_scores = rounded(weights * (d_weights - row_delta))
    head_dq = (jnp.dot(d_scores, k_float, preferred_element_type=jnp.float32) * score_scale).astype(jnp.bfloat16)
    head_dk = jnp.dot(d_scores.T, q_float, preferred_element_type=jnp.float32) * score_scale
    head_dv = jnp.dot(rounded(weights).T, d_float, preferred_element_type=jnp.float32)
    return (head_dq, head_dk, head_dv)

def one_group(group_items):
    q_rows, kv_rows, d_rows, image_view, vis_begin, lengths = group_items
    query_width = HEADS * HEAD_DIM
    kv_width = KV_HEADS * HEAD_DIM
    head_ratio = HEADS // KV_HEADS
    vis_begin = vis_begin.astype(jnp.int32)
    q_full = lax.dynamic_update_slice_in_dim(q_rows, image_view[:, :query_width], vis_begin, 0)
    k_full = lax.dynamic_update_slice_in_dim(kv_rows[0], image_view[:, query_width:query_width + kv_width], vis_begin, 0)
    v_full = lax.dynamic_update_slice_in_dim(kv_rows[1], image_view[:, query_width + kv_width:], vis_begin, 0)
    segment_ids = segment_table(lengths)
    positions = jnp.arange(SEQ, dtype=jnp.int32)
    visible = (positions[None, :] <= positions[:, None]) & ((segment_ids[None, :] == 0) | (segment_ids[None, :] == segment_ids[:, None]))

    def per_head(head_index):
        kv_index = head_index // head_ratio
        q_head = lax.dynamic_slice_in_dim(q_full, head_index * HEAD_DIM, HEAD_DIM, 1)
        d_head = lax.dynamic_slice_in_dim(d_rows, head_index * HEAD_DIM, HEAD_DIM, 1)
        k_head = lax.dynamic_slice_in_dim(k_full, kv_index * HEAD_DIM, HEAD_DIM, 1)
        v_head = lax.dynamic_slice_in_dim(v_full, kv_index * HEAD_DIM, HEAD_DIM, 1)
        return head_grads(q_head, k_head, v_head, d_head, visible)
    head_dq, head_dk, head_dv = lax.map(per_head, jnp.arange(HEADS, dtype=jnp.int32))
    sum_keys = lax.optimization_barrier(jnp.sum(head_dk.reshape(KV_HEADS, head_ratio, SEQ, HEAD_DIM), axis=1)).astype(jnp.bfloat16)
    sum_values = lax.optimization_barrier(jnp.sum(head_dv.reshape(KV_HEADS, head_ratio, SEQ, HEAD_DIM), axis=1)).astype(jnp.bfloat16)
    grad_q = jnp.transpose(head_dq, (1, 0, 2)).reshape(SEQ, query_width)
    grad_k = jnp.transpose(sum_keys, (1, 0, 2)).reshape(SEQ, kv_width)
    grad_v = jnp.transpose(sum_values, (1, 0, 2)).reshape(SEQ, kv_width)
    image_grad = jnp.concatenate([lax.dynamic_slice_in_dim(grad_q, vis_begin, VIS, 0), lax.dynamic_slice_in_dim(grad_k, vis_begin, VIS, 0), lax.dynamic_slice_in_dim(grad_v, vis_begin, VIS, 0)], axis=1)
    inside = (positions >= vis_begin) & (positions < vis_begin + VIS)
    zero_value = jnp.zeros((), jnp.bfloat16)
    grad_q = jnp.where(inside[:, None], zero_value, grad_q)
    grad_kv = jnp.where(inside[None, :, None], zero_value, jnp.stack([grad_k, grad_v]))
    return (grad_q, grad_kv, image_grad)

def reference(queries, keys_values, image_rows, cotangent, seq_image, vis_start, comp_lengths):
    image_views = image_rows[seq_image]
    grad_queries, grad_keys_values, image_grads = lax.map(one_group, (queries, keys_values, cotangent, image_views, vis_start, comp_lengths))
    grad_image = jnp.zeros_like(image_rows).at[seq_image].set(image_grads)
    return (grad_queries, grad_keys_values, grad_image)
```

```python
import functools
import math

import jax
import jax.numpy as jnp
from jax import lax
from jax.experimental import pallas as pl
from jax.experimental.pallas import tpu as pltpu
from jax.sharding import PartitionSpec as P

HEADS = 32
KV_HEADS = 8
HEAD_DIM = 128
VIS = 256
PROMPT = 64
PREFIX = VIS + PROMPT
GROUPS = 16
SHARDS = 32
CHIPS = 16
ROWS = 128
CHIP_ROWS = 256
HALO = 320
LOCAL = HALO + CHIP_ROWS
KEYS = PREFIX + LOCAL
QW = HEADS * HEAD_DIM // 2
KW = KV_HEADS * HEAD_DIM // 2
MESH = pl.DeviceIdType.MESH
BF = jnp.bfloat16
F32 = jnp.float32
NEG = -1e30


def remote(src, dst, send, recv, z, c):
    return pltpu.make_async_remote_copy(
        src_ref=src, dst_ref=dst, send_sem=send, recv_sem=recv, device_id=(z, c), device_id_type=MESH
    )


def arrived(ref, sem):
    pltpu.make_async_copy(ref, ref, sem).wait()


def each(count, body):
    def step(k, carry):
        body(k)
        return carry

    lax.fori_loop(0, count, step, 0)


def send_all(count, me, copy, local):
    def body(k):
        @pl.when(k != me)
        def _():
            copy(k).start()

        @pl.when(k == me)
        def _():
            local(k).start()

    each(count, body)


def sent_all(count, me, copy):
    def body(k):
        @pl.when(k != me)
        def _():
            copy(k).wait_send()

    each(count, body)


def greet(z, c):
    barrier = pltpu.get_barrier_semaphore()
    i = c // 2

    def plane(k):
        @pl.when(k != c)
        def _():
            pl.semaphore_signal(barrier, inc=1, device_id=(z, k), device_id_type=MESH)

    def column(k):
        @pl.when(k != z)
        def _():
            pl.semaphore_signal(barrier, inc=1, device_id=(k, 2 * i), device_id_type=MESH)
            pl.semaphore_signal(barrier, inc=1, device_id=(k, 2 * i + 1), device_id_type=MESH)

    each(SHARDS, plane)
    each(GROUPS, column)
    pl.semaphore_wait(barrier, SHARDS - 1 + 2 * (GROUPS - 1))


def gather_kernel(
    seq_ref, vis_ref, q, d, kv, img,
    q2, d2, kvloc, kvimg, kvtxt, imgq, imgd,
    z1buf, stage, z2buf, kvp, qp, ta, tb, tm, dv, ds,
    z1s, z2s, txs, sws, has, ags, ats, dss,
    z1r, z2r, tar, tbr, q2r, d2r, klr, kir, ktr, d0r, d1r, lcr,
):
    z = lax.axis_index("rollout")
    c = lax.axis_index("ctx")
    i = c // 2
    h = c % 2
    sib = 2 * i + 1 - h
    greet(z, c)

    def z1(j):
        return remote(img.at[j], z1buf.at[z], z1s.at[j], z1r, j, c)

    send_all(GROUPS, z, z1, lambda j: pltpu.make_async_copy(img.at[j], z1buf.at[z], z1r))

    def text_src(k):
        ii, hh = k // 2, k % 2
        b = ii % 8
        return kv.at[
            b // 4,
            pl.ds(pl.multiple_of(32 * (ii // 8), 32), 32),
            pl.ds(pl.multiple_of(KW * hh + 128 * (b % 4), 128), 128),
        ]

    for place, buf, sem in ((0, ta, tar), (2, tb, tbr)):
        @pl.when(c == place)
        def _():
            send_all(
                SHARDS, c,
                lambda k: remote(text_src(k), buf, txs.at[k], sem, z, k),
                lambda k: pltpu.make_async_copy(text_src(k), buf, sem),
            )

    def cols(core, width):
        return pl.ds(pl.multiple_of(width * core, width), width)

    my_rows = pl.ds(pl.multiple_of(ROWS * h, ROWS), ROWS)
    own_rows = pl.ds(pl.multiple_of(HALO + ROWS * h, 64), ROWS)
    near_rows = pl.ds(pl.multiple_of(64 + ROWS * h, 64), ROWS)
    swaps = [
        remote(d.at[:, cols(1 - h, QW)], d2.at[my_rows, :], sws.at[0], d2r, z, sib),
        remote(q.at[:, cols(1 - h, QW)], q2.at[my_rows, :], sws.at[1], q2r, z, sib),
        remote(kv.at[:, :, cols(1 - h, KW)], kvloc.at[:, own_rows, :], sws.at[2], klr, z, sib),
    ]
    one = lax.rem(i + 1, CHIPS)
    two = lax.rem(i + 2, CHIPS)
    swaps += [
        remote(kv.at[:, :, pl.ds(KW * hh, KW)], kvloc.at[:, near_rows, :], has.at[hh], klr, z, 2 * one + hh)
        for hh in (0, 1)
    ]
    far = [
        remote(
            kv.at[:, pl.ds(64, 64), pl.ds(KW * hh, KW)], kvloc.at[:, pl.ds(0, 64), :], has.at[2 + hh], klr, z,
            2 * two + hh,
        )
        for hh in (0, 1)
    ]
    for copy in swaps:
        copy.start()

    @pl.when(h == 1)
    def _():
        for copy in far:
            copy.start()

    pltpu.make_async_copy(d.at[:, cols(h, QW)], d2.at[my_rows, :], d2r).start()
    pltpu.make_async_copy(q.at[:, cols(h, QW)], q2.at[my_rows, :], q2r).start()
    pltpu.make_async_copy(kv.at[:, :, cols(h, KW)], kvloc.at[:, own_rows, :], klr).start()

    arrived(z1buf, z1r)

    def pick(g):
        stage[g] = z1buf[seq_ref[g]]

    each(GROUPS, pick)
    to_core = z % 2
    slot = 8 * h + z // 2
    here = jnp.where(to_core == h, z, GROUPS)

    def z2(g):
        return remote(stage.at[g], z2buf.at[slot], z2s.at[g], z2r, g, 2 * i + to_core)

    send_all(GROUPS, here, z2, lambda g: pltpu.make_async_copy(stage.at[g], z2buf.at[slot], z2r))

    arrived(ta, tar)
    arrived(tb, tbr)
    b = i % 8
    half = pl.ds(pl.multiple_of(32 * (i // 8), 32), 32)
    t = 32 * (i // 8) + lax.broadcasted_iota(jnp.int32, (32, 128), 0)
    tm[...] = jnp.where(t < vis_ref[0], ta[...].astype(F32), tb[...].astype(F32)).astype(BF)

    def atx(k):
        return remote(tm, kvtxt.at[b, half, :], ats.at[k], ktr, z, 2 * k + h)

    send_all(CHIPS, i, atx, lambda k: pltpu.make_async_copy(tm, kvtxt.at[b, half, :], ktr))

    def dsend(k):
        return remote(ds.at[pl.ds(pl.multiple_of(16 * k, 16), 16), :], imgd.at[0], dss.at[k], d0r, z, 2 * k + h)

    def dsend1(k):
        return remote(
            ds.at[pl.ds(pl.multiple_of(192 + 16 * k, 16), 16), :], imgd.at[1], dss.at[k], d1r, z, 2 * (12 + k) + h
        )

    @pl.when(i < 2)
    def _():
        arrived(d2, d2r)
        load = pltpu.make_async_copy(d2, dv, lcr)
        load.start()
        load.wait()
        r = lax.broadcasted_iota(jnp.int32, (VIS, CHIP_ROWS), 0)
        p = lax.broadcasted_iota(jnp.int32, (VIS, CHIP_ROWS), 1)
        pick_rows = jnp.where(p + CHIP_ROWS * i == r + vis_ref[0], 1.0, 0.0).astype(BF)
        for part in range(4):
            w = pl.ds(part * 512, 512)
            ds[:, w] = jnp.dot(pick_rows, dv[:, w], preferred_element_type=F32).astype(BF)

    @pl.when(i == 0)
    def _():
        send_all(CHIPS, i, dsend, lambda k: pltpu.make_async_copy(ds.at[pl.ds(0, 16), :], imgd.at[0], d0r))

    @pl.when(i == 1)
    def _():
        each(4, lambda k: dsend1(k).start())

    arrived(z2buf, z2r)
    o = lax.broadcasted_iota(jnp.int32, (384, 512), 0)
    n = lax.broadcasted_iota(jnp.int32, (384, 512), 1)
    perm = jnp.where(n == (o % 16) * 32 + o // 16, 1.0, 0.0).astype(BF)
    by_head = jnp.dot(perm, z2buf[...].reshape(512, 128), preferred_element_type=F32).astype(BF).reshape(24, 16, 128)
    qp[...] = by_head[:16]
    kvp[...] = by_head[16:]
    mine = pl.ds(pl.multiple_of(16 * i, 16), 16)

    def aim(k):
        return remote(kvp, kvimg.at[:, mine, :], ags.at[k], kir, z, 2 * k + h)

    send_all(CHIPS, i, aim, lambda k: pltpu.make_async_copy(kvp, kvimg.at[:, mine, :], kir))
    out_q = pltpu.make_async_copy(qp, imgq, lcr)
    out_q.start()

    arrived(q2, q2r)

    @pl.when(i >= 2)
    def _():
        arrived(d2, d2r)

    arrived(kvloc, klr)
    arrived(kvtxt, ktr)
    arrived(imgd.at[0], d0r)

    @pl.when(i >= 12)
    def _():
        arrived(imgd.at[1], d1r)

    arrived(kvimg, kir)
    out_q.wait()

    sent_all(GROUPS, z, z1)
    sent_all(GROUPS, here, z2)
    for place, buf, sem in ((0, ta, tar), (2, tb, tbr)):
        @pl.when(c == place)
        def _():
            sent_all(SHARDS, c, lambda k: remote(text_src(k), buf, txs.at[k], sem, z, k))

    for copy in swaps:
        copy.wait_send()

    @pl.when(h == 1)
    def _():
        for copy in far:
            copy.wait_send()

    sent_all(CHIPS, i, atx)
    sent_all(CHIPS, i, aim)

    @pl.when(i == 0)
    def _():
        sent_all(CHIPS, i, dsend)

    @pl.when(i == 1)
    def _():
        each(4, lambda k: dsend1(k).wait_send())


def attend_kernel(
    vis_ref, len_ref, q, d, kvloc, kvimg, kvtxt, imgq, imgd,
    dq, dkvloc, dkvimg, dkvtxt, dimgq,
    bias, ibias, valid, kall, vall, kt, dk, dv,
):
    i = lax.axis_index("ctx") // 2
    scale = 1.0 / math.sqrt(HEAD_DIM)
    to_log2 = scale * math.log2(math.e)
    vis = vis_ref[0]

    @pl.when(pl.program_id(0) == 0)
    def _():
        def slot_positions(lanes):
            r = lax.broadcasted_iota(jnp.int32, (PREFIX, lanes), 0)
            text = r - VIS
            return jnp.where(r < VIS, vis + r, jnp.where(text < vis, text, r))

        pos = CHIP_ROWS * i + lax.broadcasted_iota(jnp.int32, (1, CHIP_ROWS), 1)
        begin = jnp.full((1, CHIP_ROWS), PREFIX, jnp.int32)
        edge = jnp.int32(PREFIX)
        for k in range(16):
            edge = edge + len_ref[0, k]
            begin = jnp.where(pos >= edge, edge, begin)
        begin = jnp.where(pos < PREFIX, pos + 1, begin)
        valid[...] = jnp.where((pos >= vis) & (pos < vis + VIS), 0.0, 1.0)
        bias[:PREFIX, :] = jnp.where(slot_positions(CHIP_ROWS) <= pos, 0.0, NEG)
        at = CHIP_ROWS * i - HALO + lax.broadcasted_iota(jnp.int32, (LOCAL, CHIP_ROWS), 0)
        bias[PREFIX:, :] = jnp.where((at >= begin) & (at <= pos), 0.0, NEG)
        ipos = vis + 16 * i + lax.broadcasted_iota(jnp.int32, (1, 64), 1) % 16
        ibias[...] = jnp.where(slot_positions(64) <= ipos, 0.0, NEG)

    for whole, index in ((kall, 0), (vall, 1)):
        whole[:VIS, :] = kvimg[index, 0]
        whole[VIS:PREFIX, :] = kvtxt[index, 0]
        whole[PREFIX:, :] = kvloc[index]
    kt[...] = kall[...].T
    nt = (((1,), (1,)), ((), ()))

    def grads(k_rows, v_rows, q_rows, d_rows, mask, live):
        top = lax.dot_general(k_rows, q_rows, nt, preferred_element_type=F32) * to_log2 + mask
        e = jnp.exp2(top - jnp.max(top, axis=0, keepdims=True))
        dw = lax.dot_general(v_rows, d_rows, nt, preferred_element_type=F32)
        inv = 1.0 / jnp.sum(e, axis=0, keepdims=True)
        delta = jnp.sum(e * dw, axis=0, keepdims=True) * inv
        if live is not None:
            inv = inv * live
        w = e * inv
        s = (w * (dw - delta)).astype(BF)
        return s, w.astype(BF)

    qi = imgq[...].reshape(64, 128)
    di0 = imgd[0].astype(F32)
    di1 = jnp.where(i >= 12, imgd[1].astype(F32), 0.0)
    di = (di0 + di1).astype(BF)
    di = jnp.concatenate([di[:, 128 * k : 128 * (k + 1)] for k in range(4)], axis=0)
    s, w = grads(kall[:PREFIX, :], vall[:PREFIX, :], qi, di, ibias[...], None)
    dk[:PREFIX, :] = jnp.dot(s, qi, preferred_element_type=F32)
    dv[:PREFIX, :] = jnp.dot(w, di, preferred_element_type=F32)
    dk[PREFIX:, :] = jnp.zeros((LOCAL, 128), F32)
    dv[PREFIX:, :] = jnp.zeros((LOCAL, 128), F32)
    dqi = jnp.dot(kt[:, :PREFIX], s, preferred_element_type=F32) * scale
    dimgq[...] = dqi.T.astype(BF).reshape(4, 16, 128)

    for k in range(4):
        w128 = pl.ds(128 * k, 128)
        qh = q[:, w128]
        dh = d[:, w128]
        s, w = grads(kall[...], vall[...], qh, dh, bias[...], valid[...])
        dk[...] += jnp.dot(s, qh, preferred_element_type=F32)
        dv[...] += jnp.dot(w, dh, preferred_element_type=F32)
        dqt = jnp.dot(kt[...], s, preferred_element_type=F32) * scale
        dq[:, w128] = dqt.T.astype(BF)

    for index, part, factor in ((0, dk, scale), (1, dv, 1.0)):
        total = (part[...] * factor).astype(BF)
        dkvimg[index, 0] = total[:VIS]
        dkvtxt[index, 0] = total[VIS:PREFIX]
        dkvloc[index] = total[PREFIX:]


def scatter_kernel(
    inv_ref, vis_ref, dq2, dkvloc, dkvimg, dkvtxt, dimgq,
    gq, gkv, gimg,
    rsi, rst, hb0, hb1, hb2, dtx, heads, rows, zb, stage, tx, kvo,
    ris, rts, hs, qs, xs, z1s, z2s,
    rir, rtr, h0r, h1r, h2r, gqr, xr, z1r, z2r, lcr,
):
    z = lax.axis_index("rollout")
    c = lax.axis_index("ctx")
    i = c // 2
    h = c % 2
    sib = 2 * i + 1 - h
    greet(z, c)

    def block(k):
        return pl.ds(pl.multiple_of(16 * k, 16), 16)

    def half_of(k):
        return pl.ds(pl.multiple_of(32 * (k // 8), 32), 32)

    load = pltpu.make_async_copy(dimgq, heads.at[pl.ds(0, 16)], lcr)
    load.start()

    def rimg(k):
        return remote(dkvimg.at[:, block(k), :], rsi.at[i], ris.at[k], rir, z, 2 * k + h)

    def rtxt(k):
        return remote(dkvtxt.at[k % 8, half_of(k), :], rst.at[i], rts.at[k], rtr, z, 2 * k + h)

    send_all(CHIPS, i, rimg, lambda k: pltpu.make_async_copy(dkvimg.at[:, block(k), :], rsi.at[i], rir))
    send_all(CHIPS, i, rtxt, lambda k: pltpu.make_async_copy(dkvtxt.at[k % 8, half_of(k), :], rst.at[i], rtr))

    one = lax.rem(i + CHIPS - 1, CHIPS)
    two = lax.rem(i + CHIPS - 2, CHIPS)

    def rows_of(core, first):
        return pl.ds(pl.multiple_of(first + ROWS * core, 64), ROWS)

    my_cols = pl.ds(pl.multiple_of(QW * h, QW), QW)
    copies = [
        remote(dkvloc.at[:, rows_of(s, 64), :], hb1.at[h], hs.at[s], h1r, z, 2 * one + s) for s in (0, 1)
    ] + [
        remote(dkvloc.at[:, pl.ds(0, 64), :], hb2.at[h], hs.at[2], h2r, z, 2 * two + 1),
        remote(dkvloc.at[:, rows_of(1 - h, HALO), :], hb0.at[h], hs.at[3], h0r, z, sib),
        remote(dq2.at[rows_of(1 - h, 0), :], gq.at[:, my_cols], qs, gqr, z, sib),
    ]
    for copy in copies:
        copy.start()
    pltpu.make_async_copy(dkvloc.at[:, rows_of(h, HALO), :], hb0.at[h], h0r).start()
    pltpu.make_async_copy(dq2.at[rows_of(h, 0), :], gq.at[:, my_cols], gqr).start()

    arrived(rst, rtr)
    total = rst[0].astype(F32)
    for k in range(1, CHIPS):
        total = total + rst[k].astype(F32)
    tx[...] = total.astype(BF)
    txt_slot = dtx.at[h, i % 8, half_of(i), :]

    for n, place in ((0, 0), (1, 2)):
        @pl.when(c != place)
        def _():
            remote(tx, txt_slot, xs.at[n], xr, z, place).start()

        @pl.when(c == place)
        def _():
            pltpu.make_async_copy(tx, txt_slot, xr).start()

    arrived(rsi, rir)
    total = rsi[0].astype(F32)
    for k in range(1, CHIPS):
        total = total + rsi[k].astype(F32)
    load.wait()
    heads[16:] = total.astype(BF)

    o = lax.broadcasted_iota(jnp.int32, (512, 384), 0)
    n = lax.broadcasted_iota(jnp.int32, (512, 384), 1)
    perm = jnp.where(n == (o % 32) * 16 + o // 32, 1.0, 0.0).astype(BF)
    rows[...] = (
        jnp.dot(perm, heads[...].reshape(384, 128), preferred_element_type=F32).astype(BF).reshape(16, 32, 128)
    )
    here = jnp.where(z % 2 == h, 8 * h + z // 2, GROUPS)

    def z1(r):
        return remote(rows.at[r], zb.at[z], z1s.at[r], z1r, 2 * (r % 8) + h, 2 * i + r // 8)

    send_all(16, here, z1, lambda r: pltpu.make_async_copy(rows.at[r], zb.at[z], z1r))
    arrived(zb, z1r)

    def pick(g):
        stage[g] = zb[inv_ref[g]]

    each(GROUPS, pick)

    def z2(g):
        return remote(stage.at[g], gimg.at[z], z2s.at[g], z2r, g, c)

    send_all(GROUPS, z, z2, lambda g: pltpu.make_async_copy(stage.at[g], gimg.at[z], z2r))

    arrived(hb0, h0r)
    arrived(hb1, h1r)

    @pl.when(h == 1)
    def _():
        arrived(hb2, h2r)

    for hh in (0, 1):
        for n in (0, 1):
            w = pl.ds(KW * hh, KW)
            near = hb0[hh, n].astype(F32) + hb1[hh, n].astype(F32)
            kvo[n, :64, w] = near[:64].astype(BF)
            more = jnp.where(h == 1, hb2[hh, n].astype(F32), 0.0)
            kvo[n, 64:, w] = (near[64:] + more).astype(BF)

    t = lax.broadcasted_iota(jnp.int32, (PROMPT, 128), 0)
    vis = vis_ref[0]
    for place in (0, 2):
        @pl.when(c == place)
        def _():
            arrived(dtx, xr)
            keep = t < vis if place == 0 else t >= vis
            for hh in (0, 1):
                for b in range(8):
                    kvo[b // 4, :64, pl.ds(KW * hh + 128 * (b % 4), 128)] = jnp.where(
                        keep, dtx[hh, b].astype(F32), 0.0
                    ).astype(BF)

    out = pltpu.make_async_copy(kvo, gkv, lcr)
    out.start()
    arrived(gq, gqr)
    arrived(gimg, z2r)
    out.wait()

    sent_all(CHIPS, i, rimg)
    sent_all(CHIPS, i, rtxt)
    for copy in copies:
        copy.wait_send()
    for n, place in ((0, 0), (1, 2)):
        @pl.when(c != place)
        def _():
            remote(tx, txt_slot, xs.at[n], xr, z, place).wait_send()

    sent_all(16, here, z1)
    sent_all(GROUPS, z, z2)


ANY = pl.BlockSpec(memory_space=pl.ANY)
SMEM = pl.BlockSpec(memory_space=pltpu.SMEM)
DMA = pltpu.SemaphoreType.DMA


def sds(*shape):
    return jax.ShapeDtypeStruct(shape, BF)


def vm(*shape, dtype=BF):
    return pltpu.VMEM(shape, dtype)


def per_device(queries, keys_values, image_rows, cotangent, seq_image, vis_start, comp_lengths):
    rows = image_rows[0]
    q_part = rows[:, : 2 * QW].reshape(8, 2, 16, 128)
    k_part = rows[:, 2 * QW : 2 * QW + 2 * KW].reshape(8, 2, 4, 128)
    v_part = rows[:, 2 * QW + 2 * KW :].reshape(8, 2, 4, 128)
    pieces = jnp.concatenate([q_part, k_part, v_part, jnp.zeros((8, 2, 8, 128), BF)], axis=2)
    pieces = pieces.reshape(16, 32, 128)

    q2, d2, kvloc, kvimg, kvtxt, imgq, imgd = pl.pallas_call(
        gather_kernel,
        out_shape=[
            sds(CHIP_ROWS, QW), sds(CHIP_ROWS, QW), sds(2, LOCAL, KW), sds(8, VIS, 128), sds(8, PROMPT, 128),
            sds(16, 16, 128), sds(2, 16, QW),
        ],
        in_specs=[SMEM, SMEM, ANY, ANY, ANY, ANY],
        out_specs=[ANY] * 7,
        scratch_shapes=[
            vm(16, 32, 128), vm(16, 32, 128), vm(16, 32, 128), vm(8, 16, 128), vm(16, 16, 128),
            vm(32, 128), vm(32, 128), vm(32, 128), vm(CHIP_ROWS, QW), vm(CHIP_ROWS, QW),
            DMA((16,)), DMA((16,)), DMA((32,)), DMA((3,)), DMA((4,)), DMA((16,)), DMA((16,)), DMA((16,)),
        ] + [DMA(())] * 12,
        compiler_params=pltpu.CompilerParams(
            collective_id=0, has_side_effects=True, vmem_limit_bytes=32 * 2**20
        ),
        name="gather_in",
    )(seq_image, vis_start, queries[0], cotangent[0], keys_values[0], pieces)

    dq2, dkvloc, dkvimg, dkvtxt, dimgq = pl.pallas_call(
        attend_kernel,
        grid=(4,),
        out_shape=[
            sds(CHIP_ROWS, QW), sds(2, LOCAL, KW), sds(2, 4, VIS, 128), sds(2, 4, PROMPT, 128), sds(16, 16, 128),
        ],
        in_specs=[
            SMEM, SMEM,
            pl.BlockSpec((CHIP_ROWS, 512), lambda e: (0, e)),
            pl.BlockSpec((CHIP_ROWS, 512), lambda e: (0, e)),
            pl.BlockSpec((2, LOCAL, 128), lambda e: (0, 0, e)),
            pl.BlockSpec((2, 1, VIS, 128), lambda e: (0, e, 0, 0)),
            pl.BlockSpec((2, 1, PROMPT, 128), lambda e: (0, e, 0, 0)),
            pl.BlockSpec((4, 16, 128), lambda e: (e, 0, 0)),
            pl.BlockSpec((2, 16, 512), lambda e: (0, 0, e)),
        ],
        out_specs=[
            pl.BlockSpec((CHIP_ROWS, 512), lambda e: (0, e)),
            pl.BlockSpec((2, LOCAL, 128), lambda e: (0, 0, e)),
            pl.BlockSpec((2, 1, VIS, 128), lambda e: (0, e, 0, 0)),
            pl.BlockSpec((2, 1, PROMPT, 128), lambda e: (0, e, 0, 0)),
            pl.BlockSpec((4, 16, 128), lambda e: (e, 0, 0)),
        ],
        scratch_shapes=[
            vm(KEYS, CHIP_ROWS, dtype=F32), vm(PREFIX, 64, dtype=F32), vm(1, CHIP_ROWS, dtype=F32),
            vm(KEYS, 128), vm(KEYS, 128), vm(128, KEYS), vm(KEYS, 128, dtype=F32), vm(KEYS, 128, dtype=F32),
        ],
        compiler_params=pltpu.CompilerParams(vmem_limit_bytes=48 * 2**20),
        name="attend",
    )(
        vis_start, comp_lengths, q2, d2, kvloc, kvimg.reshape(2, 4, VIS, 128), kvtxt.reshape(2, 4, PROMPT, 128),
        imgq, imgd,
    )

    groups = jnp.arange(GROUPS, dtype=jnp.int32)
    user = jnp.sum(jnp.where(seq_image[None, :] == groups[:, None], groups[None, :], 0), axis=1, dtype=jnp.int32)
    gq, gkv, gimg = pl.pallas_call(
        scatter_kernel,
        out_shape=[sds(ROWS, 2 * QW), sds(2, ROWS, 2 * KW), sds(16, 32, 128)],
        in_specs=[SMEM, SMEM] + [ANY] * 5,
        out_specs=[ANY] * 3,
        scratch_shapes=[
            vm(16, 8, 16, 128), vm(16, 32, 128), vm(2, 2, ROWS, KW), vm(2, 2, ROWS, KW), vm(2, 2, 64, KW),
            vm(2, 8, 64, 128), vm(24, 16, 128), vm(16, 32, 128), vm(16, 32, 128), vm(16, 32, 128), vm(32, 128),
            vm(2, ROWS, 2 * KW),
            DMA((16,)), DMA((16,)), DMA((4,)), DMA(()), DMA((2,)), DMA((16,)), DMA((16,)),
        ] + [DMA(())] * 10,
        compiler_params=pltpu.CompilerParams(
            collective_id=1, has_side_effects=True, vmem_limit_bytes=32 * 2**20
        ),
        name="scatter_out",
    )(user, vis_start, dq2, dkvloc, dkvimg.reshape(8, VIS, 128), dkvtxt.reshape(8, PROMPT, 128), dimgq)

    gimg = gimg.reshape(8, 2, 32, 128)
    own = jnp.concatenate(
        [
            gimg[:, :, :16].reshape(8, 2 * QW),
            gimg[:, :, 16:20].reshape(8, 2 * KW),
            gimg[:, :, 20:24].reshape(8, 2 * KW),
        ],
        axis=1,
    )
    return (gq[None], gkv[None], own[None])


def solution(mesh):
    placed = (
        P("rollout", "ctx", None),
        P("rollout", None, "ctx", None),
        P("rollout", "ctx", None),
        P("rollout", "ctx", None),
        P(),
        P("rollout"),
        P("rollout", None),
    )
    return jax.shard_map(
        per_device,
        mesh=mesh,
        in_specs=placed,
        out_specs=(
            P("rollout", "ctx", None),
            P("rollout", None, "ctx", None),
            P("rollout", "ctx", None),
        ),
        check_vma=False,
    )
```

```python
import functools
import math

import jax
import jax.numpy as jnp
from jax import lax
from jax.experimental import pallas as pl
from jax.experimental.pallas import tpu as pltpu
from jax.sharding import PartitionSpec as P

HEADS = 32
KV_HEADS = 8
HEAD_DIM = 128
VIS = 256
PROMPT = 64
PREFIX = VIS + PROMPT
GROUPS = 16
SHARDS = 32
CHIPS = 16
ROWS = 128
CHIP_ROWS = 256
HALO = 320
LOCAL = HALO + CHIP_ROWS
KEYS = PREFIX + LOCAL
QW = HEADS * HEAD_DIM // 2
KW = KV_HEADS * HEAD_DIM // 2
MESH = pl.DeviceIdType.MESH
BF = jnp.bfloat16
F32 = jnp.float32
NEG = -1e30
RS_AT = 2


def remote(src, dst, send, recv, z, c):
    return pltpu.make_async_remote_copy(
        src_ref=src, dst_ref=dst, send_sem=send, recv_sem=recv, device_id=(z, c), device_id_type=MESH
    )


def arrived(ref, sem):
    pltpu.make_async_copy(ref, ref, sem).wait()


def each(count, body):
    def step(k, carry):
        body(k)
        return carry

    lax.fori_loop(0, count, step, 0)


def send_all(count, me, copy, local):
    def body(k):
        @pl.when(k != me)
        def _():
            copy(k).start()

        @pl.when(k == me)
        def _():
            local(k).start()

    each(count, body)


def sent_all(count, me, copy):
    def body(k):
        @pl.when(k != me)
        def _():
            copy(k).wait_send()

    each(count, body)


def greet(z, c):
    barrier = pltpu.get_barrier_semaphore()
    i = c // 2

    def plane(k):
        @pl.when(k != c)
        def _():
            pl.semaphore_signal(barrier, inc=1, device_id=(z, k), device_id_type=MESH)

    def column(k):
        @pl.when(k != z)
        def _():
            pl.semaphore_signal(barrier, inc=1, device_id=(k, 2 * i), device_id_type=MESH)
            pl.semaphore_signal(barrier, inc=1, device_id=(k, 2 * i + 1), device_id_type=MESH)

    each(SHARDS, plane)
    each(GROUPS, column)


def greeted():
    pl.semaphore_wait(pltpu.get_barrier_semaphore(), SHARDS - 1 + 2 * (GROUPS - 1))


def one_hot(rows, cols, source):
    o = lax.broadcasted_iota(jnp.int32, (rows, cols), 0)
    n = lax.broadcasted_iota(jnp.int32, (rows, cols), 1)
    return jnp.where(n == source(o), 1.0, 0.0).astype(BF)


def piece_source(o):
    s = o % 32
    r = o // 64
    hh = (o // 32) % 2
    block = jnp.where(s < 16, 16 * hh + s, jnp.where(s < 20, 16 + 4 * hh + s, 20 + 4 * hh + s))
    return jnp.where(s < 24, 8 * block + r, -1)


def kernel(
    seq_ref, inv_ref, vis_ref, len_ref, q, d, kv, img,
    gq, gkv, gimg,
    pieces, z1buf, stage, z2buf, kvp, qi, ta, tb, tm, ds, gather_p, spread_p,
    q2, d2, kvloc, kvimg, kvtxt, imgd,
    bias, ibias, valid, el, dwl, stat, sp, kp, vp, dkl, dvl,
    dq2, dkvloc, dkvimg, dkvtxt, heads,
    rsi, rst, hb0, hb1, hb2, dtx, rows, zb, stage2, tx, kvo,
    z1s, z2s, txs, sws, has, ags, ats, dss, ris, rts, hrs, qrs, xs, y1s, y2s,
    z1r, z2r, tar, tbr, q2r, d2r, klr, kir, ktr, d0r, d1r,
    rir, rtr, h0r, h1r, h2r, gqr, xr, y1r, y2r, lcr,
):
    z = lax.axis_index("rollout")
    c = lax.axis_index("ctx")
    i = c // 2
    h = c % 2
    sib = 2 * i + 1 - h
    scale = 1.0 / math.sqrt(HEAD_DIM)
    to_log2 = scale * math.log2(math.e)
    vis = vis_ref[0]
    nt = (((1,), (1,)), ((), ()))
    greet(z, c)

    blocks = jnp.concatenate([img[:, 128 * k : 128 * (k + 1)].astype(F32) for k in range(48)], axis=0).astype(BF)
    pieces[...] = (
        jnp.dot(one_hot(512, 384, piece_source), blocks, preferred_element_type=F32).astype(BF).reshape(16, 32, 128)
    )
    greeted()

    def z1(j):
        return remote(pieces.at[j], z1buf.at[z], z1s.at[j], z1r, j, c)

    send_all(GROUPS, z, z1, lambda j: pltpu.make_async_copy(pieces.at[j], z1buf.at[z], z1r))

    def text_src(k):
        ii, hh = k // 2, k % 2
        b = ii % 8
        return kv.at[
            b // 4,
            pl.ds(pl.multiple_of(32 * (ii // 8), 32), 32),
            pl.ds(pl.multiple_of(KW * hh + 128 * (b % 4), 128), 128),
        ]

    for place, buf, sem in ((0, ta, tar), (2, tb, tbr)):
        @pl.when(c == place)
        def _():
            send_all(
                SHARDS, c,
                lambda k: remote(text_src(k), buf, txs.at[k], sem, z, k),
                lambda k: pltpu.make_async_copy(text_src(k), buf, sem),
            )

    def cols(core, width):
        return pl.ds(pl.multiple_of(width * core, width), width)

    def rows_of(core, first):
        return pl.ds(pl.multiple_of(first + ROWS * core, 64), ROWS)

    def block(k):
        return pl.ds(pl.multiple_of(16 * k, 16), 16)

    def half_of(k):
        return pl.ds(pl.multiple_of(32 * (k // 8), 32), 32)

    def ahead(n):
        return lax.rem(i + n, CHIPS)

    my_rows = rows_of(h, 0)
    own_rows = rows_of(h, HALO)
    near_rows = rows_of(h, 64)
    swaps = [
        remote(d.at[:, cols(1 - h, QW)], d2.at[my_rows, :], sws.at[0], d2r, z, sib),
        remote(q.at[:, cols(1 - h, QW)], q2.at[my_rows, :], sws.at[1], q2r, z, sib),
        remote(kv.at[:, :, cols(1 - h, KW)], kvloc.at[:, own_rows, :], sws.at[2], klr, z, sib),
    ] + [
        remote(kv.at[:, :, pl.ds(KW * hh, KW)], kvloc.at[:, near_rows, :], has.at[hh], klr, z, 2 * ahead(1) + hh)
        for hh in (0, 1)
    ]
    far = [
        remote(
            kv.at[:, pl.ds(64, 64), pl.ds(KW * hh, KW)], kvloc.at[:, pl.ds(0, 64), :], has.at[2 + hh], klr, z,
            2 * ahead(2) + hh,
        )
        for hh in (0, 1)
    ]
    for copy in swaps:
        copy.start()

    @pl.when(h == 1)
    def _():
        for copy in far:
            copy.start()

    pltpu.make_async_copy(d.at[:, cols(h, QW)], d2.at[my_rows, :], d2r).start()
    pltpu.make_async_copy(q.at[:, cols(h, QW)], q2.at[my_rows, :], q2r).start()
    pltpu.make_async_copy(kv.at[:, :, cols(h, KW)], kvloc.at[:, own_rows, :], klr).start()

    gather_p[...] = one_hot(384, 512, lambda o: (o % 16) * 32 + o // 16)
    spread_p[...] = one_hot(512, 384, lambda o: (o % 32) * 16 + o // 32)

    def slot_positions(lanes):
        r = lax.broadcasted_iota(jnp.int32, (PREFIX, lanes), 0)
        text = r - VIS
        return jnp.where(r < VIS, vis + r, jnp.where(text < vis, text, r))

    pos = CHIP_ROWS * i + lax.broadcasted_iota(jnp.int32, (1, CHIP_ROWS), 1)
    begin = jnp.full((1, CHIP_ROWS), PREFIX, jnp.int32)
    edge = jnp.int32(PREFIX)
    for k in range(16):
        edge = edge + len_ref[0, k]
        begin = jnp.where(pos >= edge, edge, begin)
    begin = jnp.where(pos < PREFIX, pos + 1, begin)
    valid[...] = jnp.where((pos >= vis) & (pos < vis + VIS), 0.0, 1.0)
    bias[:PREFIX, :] = jnp.where(slot_positions(CHIP_ROWS) <= pos, 0.0, NEG)
    at = CHIP_ROWS * i - HALO + lax.broadcasted_iota(jnp.int32, (LOCAL, CHIP_ROWS), 0)
    bias[PREFIX:, :] = jnp.where((at >= begin) & (at <= pos), 0.0, NEG)
    ipos = vis + 16 * i + lax.broadcasted_iota(jnp.int32, (1, 64), 1) % 16
    ibias[...] = jnp.where(slot_positions(64) <= ipos, 0.0, NEG)

    arrived(z1buf, z1r)

    def pick(g):
        stage[g] = z1buf[seq_ref[g]]

    each(GROUPS, pick)
    to_core = z % 2
    slot = 8 * h + z // 2
    here = jnp.where(to_core == h, z, GROUPS)
    here_back = jnp.where(to_core == h, slot, GROUPS)

    def z2(g):
        return remote(stage.at[g], z2buf.at[slot], z2s.at[g], z2r, g, 2 * i + to_core)

    send_all(GROUPS, here, z2, lambda g: pltpu.make_async_copy(stage.at[g], z2buf.at[slot], z2r))

    arrived(ta, tar)
    arrived(tb, tbr)
    t = 32 * (i // 8) + lax.broadcasted_iota(jnp.int32, (32, 128), 0)
    tm[...] = jnp.where(t < vis, ta[...].astype(F32), tb[...].astype(F32)).astype(BF)
    txt_part = kvtxt.at[i % 8, half_of(i), :]

    def atx(k):
        return remote(tm, txt_part, ats.at[k], ktr, z, 2 * k + h)

    send_all(CHIPS, i, atx, lambda k: pltpu.make_async_copy(tm, txt_part, ktr))

    def dsend(k):
        return remote(ds.at[block(k), :], imgd.at[0], dss.at[k], d0r, z, 2 * k + h)

    def dsend1(k):
        return remote(ds.at[block(12 + k), :], imgd.at[1], dss.at[k], d1r, z, 2 * (12 + k) + h)

    arrived(d2, d2r)

    @pl.when(i < 2)
    def _():
        shift = one_hot(VIS, CHIP_ROWS, lambda r: r + vis - CHIP_ROWS * i)
        for part in range(4):
            w = pl.ds(part * 512, 512)
            ds[:, w] = jnp.dot(shift, d2[:, w], preferred_element_type=F32).astype(BF)

    @pl.when(i == 0)
    def _():
        send_all(CHIPS, i, dsend, lambda k: pltpu.make_async_copy(ds.at[block(0), :], imgd.at[0], d0r))

    @pl.when(i == 1)
    def _():
        each(4, lambda k: dsend1(k).start())

    arrived(z2buf, z2r)
    by_head = jnp.dot(gather_p[...], z2buf[...].reshape(512, 128), preferred_element_type=F32).astype(BF)
    by_head = by_head.reshape(24, 16, 128)
    kvp[...] = by_head[16:]

    def aim(k):
        return remote(kvp, kvimg.at[:, block(i), :], ags.at[k], kir, z, 2 * k + h)

    send_all(CHIPS, i, aim, lambda k: pltpu.make_async_copy(kvp, kvimg.at[:, block(i), :], kir))
    qi[...] = by_head[:16]

    arrived(q2, q2r)
    arrived(kvloc, klr)

    def head_cols(e, k):
        return pl.ds(pl.multiple_of(512 * e + 128 * k, 128), 128)

    def key_cols(e):
        return pl.ds(pl.multiple_of(128 * e, 128), 128)

    def local_scores(e):
        k_rows = kvloc[0, :, key_cols(e)]
        v_rows = kvloc[1, :, key_cols(e)]
        for k in range(4):
            w128 = head_cols(e, k)
            n = 4 * e + k
            top = lax.dot_general(k_rows, q2[:, w128], nt, preferred_element_type=F32) * to_log2 + bias[PREFIX:, :]
            peak = jnp.max(top, axis=0, keepdims=True)
            ex = jnp.exp2(top - peak)
            dw = lax.dot_general(v_rows, d2[:, w128], nt, preferred_element_type=F32)
            el[n] = ex
            dwl[n] = dw
            stat[n, 0:1, :] = peak
            stat[n, 1:2, :] = jnp.sum(ex, axis=0, keepdims=True)
            stat[n, 2:3, :] = jnp.sum(ex * dw, axis=0, keepdims=True)

    each(4, local_scores)

    arrived(kvtxt, ktr)
    arrived(imgd.at[0], d0r)

    @pl.when(i >= 12)
    def _():
        arrived(imgd.at[1], d1r)

    arrived(kvimg, kir)

    def rimg(half, k):
        return remote(dkvimg.at[half, :, block(k), :], rsi.at[i, half], ris.at[half, k], rir, z, 2 * k + h)

    def rtxt(k):
        return remote(dkvtxt.at[k % 8, half_of(k), :], rst.at[i], rts.at[k], rtr, z, 2 * k + h)

    def prefix_grads(e):
        kp[:VIS, :] = kvimg[e]
        kp[VIS:, :] = kvtxt[e]
        vp[:VIS, :] = kvimg[4 + e]
        vp[VIS:, :] = kvtxt[4 + e]
        k_rows = kp[...]
        v_rows = vp[...]

        def scores(q_rows, d_rows, mask):
            top = lax.dot_general(k_rows, q_rows, nt, preferred_element_type=F32) * to_log2 + mask
            dw = lax.dot_general(v_rows, d_rows, nt, preferred_element_type=F32)
            return top, jnp.max(top, axis=0, keepdims=True), dw

        q_rows = qi[pl.ds(4 * e, 4)].reshape(64, 128)
        wide = pl.ds(pl.multiple_of(512 * e, 512), 512)
        d_rows = (imgd[0, :, wide].astype(F32) + jnp.where(i >= 12, imgd[1, :, wide].astype(F32), 0.0)).astype(BF)
        d_rows = jnp.concatenate([d_rows[:, 128 * k : 128 * (k + 1)] for k in range(4)], axis=0)
        top, peak, dw = scores(q_rows, d_rows, ibias[...])
        ex = jnp.exp2(top - peak)
        inv = 1.0 / jnp.sum(ex, axis=0, keepdims=True)
        delta = jnp.sum(ex * dw, axis=0, keepdims=True) * inv
        w = ex * inv
        s = (w * (dw - delta)).astype(BF)
        dk = jnp.dot(s, q_rows, preferred_element_type=F32)
        dv = jnp.dot(w.astype(BF), d_rows, preferred_element_type=F32)
        dqi = lax.dot_general(s, k_rows, (((0,), (0,)), ((), ())), preferred_element_type=F32) * scale
        heads[pl.ds(4 * e, 4)] = dqi.astype(BF).reshape(4, 16, 128)

        for k in range(4):
            n = 4 * e + k
            q_rows = q2[:, head_cols(e, k)]
            d_rows = d2[:, head_cols(e, k)]
            top, peak, dw = scores(q_rows, d_rows, bias[:PREFIX, :])
            low = stat[n, 0:1, :]
            peak = jnp.maximum(peak, low)
            ex = jnp.exp2(top - peak)
            shrink = jnp.exp2(low - peak)
            inv = 1.0 / (jnp.sum(ex, axis=0, keepdims=True) + stat[n, 1:2, :] * shrink)
            delta = (jnp.sum(ex * dw, axis=0, keepdims=True) + stat[n, 2:3, :] * shrink) * inv
            inv = inv * valid[...]
            w = ex * inv
            s = (w * (dw - delta)).astype(BF)
            dk = dk + jnp.dot(s, q_rows, preferred_element_type=F32)
            dv = dv + jnp.dot(w.astype(BF), d_rows, preferred_element_type=F32)
            sp[n] = s
            stat[n, 0:1, :] = shrink * inv
            stat[n, 1:2, :] = delta
        dk = (dk * scale).astype(BF)
        dv = dv.astype(BF)
        place = 2 * (e % 2)
        dkvimg[e // 2, place] = dk[:VIS]
        dkvimg[e // 2, place + 1] = dv[:VIS]
        dkvtxt[e] = dk[VIS:]
        dkvtxt[4 + e] = dv[VIS:]

        @pl.when(e % 2 == 1)
        def _():
            half = e // 2
            send_all(
                CHIPS, i,
                lambda k: rimg(half, k),
                lambda k: pltpu.make_async_copy(dkvimg.at[half, :, block(k), :], rsi.at[i, half], rir),
            )

    each(4, prefix_grads)
    send_all(CHIPS, i, rtxt, lambda k: pltpu.make_async_copy(dkvtxt.at[k % 8, half_of(k), :], rst.at[i], rtr))

    def halo_copies(e):
        near, more = 2 * ahead(CHIPS - 1), 2 * ahead(CHIPS - 2)
        return [
            remote(dkvloc.at[e, :, rows_of(s, 64), :], hb1.at[h, e], hrs.at[s, e], h1r, z, near + s) for s in (0, 1)
        ] + [
            remote(dkvloc.at[e, :, pl.ds(0, 64), :], hb2.at[h, e], hrs.at[2, e], h2r, z, more + 1),
            remote(dkvloc.at[e, :, rows_of(1 - h, HALO), :], hb0.at[h, e], hrs.at[3, e], h0r, z, sib),
            remote(dq2.at[e, rows_of(1 - h, 0), :], gq.at[:, out_cols(e)], qrs.at[e], gqr, z, sib),
        ]

    def out_cols(e):
        return pl.ds(pl.multiple_of(QW * h + 512 * e, 512), 512)

    def local_grads(e):
        k_rows = kvloc[0, :, key_cols(e)]
        kt = k_rows.T
        kp[:VIS, :] = kvimg[e]
        kp[VIS:, :] = kvtxt[e]
        kpt = kp[...].T
        for k in range(4):
            n = 4 * e + k
            q_rows = q2[:, head_cols(e, k)]
            d_rows = d2[:, head_cols(e, k)]
            w = el[n] * stat[n, 0:1, :]
            s = (w * (dwl[n] - stat[n, 1:2, :])).astype(BF)
            part = jnp.dot(s, q_rows, preferred_element_type=F32)
            dkl[...] = part if k == 0 else dkl[...] + part
            part = jnp.dot(w.astype(BF), d_rows, preferred_element_type=F32)
            dvl[...] = part if k == 0 else dvl[...] + part
            dqt = jnp.dot(kt, s, preferred_element_type=F32) + jnp.dot(kpt, sp[n], preferred_element_type=F32)
            dq2[e, :, 128 * k : 128 * (k + 1)] = (dqt * scale).T.astype(BF)
        dkvloc[e, 0] = (dkl[...] * scale).astype(BF)
        dkvloc[e, 1] = dvl[...].astype(BF)
        for copy in halo_copies(e):
            copy.start()
        pltpu.make_async_copy(dkvloc.at[e, :, rows_of(h, HALO), :], hb0.at[h, e], h0r).start()
        pltpu.make_async_copy(dq2.at[e, rows_of(h, 0), :], gq.at[:, out_cols(e)], gqr).start()

    def z1_back(r):
        return remote(rows.at[r], zb.at[z], y1s.at[r], y1r, 2 * (r % 8) + h, 2 * i + r // 8)

    txt_slot = dtx.at[h, i % 8, half_of(i), :]

    def reduce_prefix():
        arrived(rsi, rir)
        total = rsi[0].astype(F32)
        for k in range(1, CHIPS):
            total = total + rsi[k].astype(F32)
        total = total.astype(BF)
        for e in range(4):
            for n in range(2):
                heads[16 + 4 * n + e] = total[e // 2, 2 * (e % 2) + n]
        rows[...] = (
            jnp.dot(spread_p[...], heads[...].reshape(384, 128), preferred_element_type=F32)
            .astype(BF)
            .reshape(16, 32, 128)
        )
        send_all(16, here_back, z1_back, lambda r: pltpu.make_async_copy(rows.at[r], zb.at[z], y1r))
        arrived(rst, rtr)
        total = rst[0].astype(F32)
        for k in range(1, CHIPS):
            total = total + rst[k].astype(F32)
        tx[...] = total.astype(BF)
        for n, place in ((0, 0), (1, 2)):
            @pl.when(c != place)
            def _():
                remote(tx, txt_slot, xs.at[n], xr, z, place).start()

            @pl.when(c == place)
            def _():
                pltpu.make_async_copy(tx, txt_slot, xr).start()

    def rest(e):
        local_grads(e)

        @pl.when(e == RS_AT)
        def _():
            reduce_prefix()

    each(4, rest)

    sent_all(GROUPS, z, z1)
    sent_all(GROUPS, here, z2)
    for place, buf, sem in ((0, ta, tar), (2, tb, tbr)):
        @pl.when(c == place)
        def _():
            sent_all(SHARDS, c, lambda k: remote(text_src(k), buf, txs.at[k], sem, z, k))

    for copy in swaps:
        copy.wait_send()

    @pl.when(h == 1)
    def _():
        for copy in far:
            copy.wait_send()

    sent_all(CHIPS, i, atx)
    sent_all(CHIPS, i, aim)

    @pl.when(i == 0)
    def _():
        sent_all(CHIPS, i, dsend)

    @pl.when(i == 1)
    def _():
        each(4, lambda k: dsend1(k).wait_send())

    arrived(zb, y1r)

    def pick_back(g):
        stage2[g] = zb[inv_ref[g]]

    each(GROUPS, pick_back)

    def z2_back(g):
        return remote(stage2.at[g], gimg.at[z], y2s.at[g], y2r, g, c)

    send_all(GROUPS, z, z2_back, lambda g: pltpu.make_async_copy(stage2.at[g], gimg.at[z], y2r))

    for half in (0, 1):
        sent_all(CHIPS, i, lambda k: rimg(half, k))
    sent_all(CHIPS, i, rtxt)
    sent_all(16, here_back, z1_back)
    for n, place in ((0, 0), (1, 2)):
        @pl.when(c != place)
        def _():
            remote(tx, txt_slot, xs.at[n], xr, z, place).wait_send()

    arrived(hb0, h0r)
    arrived(hb1, h1r)

    @pl.when(h == 1)
    def _():
        arrived(hb2, h2r)

    for hh in (0, 1):
        for e in range(4):
            for n in (0, 1):
                w = pl.ds(KW * hh + 128 * e, 128)
                near = hb0[hh, e, n].astype(F32) + hb1[hh, e, n].astype(F32)
                kvo[n, :64, w] = near[:64].astype(BF)
                more = jnp.where(h == 1, hb2[hh, e, n].astype(F32), 0.0)
                kvo[n, 64:, w] = (near[64:] + more).astype(BF)

    t64 = lax.broadcasted_iota(jnp.int32, (PROMPT, 128), 0)
    for place in (0, 2):
        @pl.when(c == place)
        def _():
            arrived(dtx, xr)
            keep = t64 < vis if place == 0 else t64 >= vis
            for hh in (0, 1):
                for b in range(8):
                    kvo[b // 4, :64, pl.ds(KW * hh + 128 * (b % 4), 128)] = jnp.where(
                        keep, dtx[hh, b].astype(F32), 0.0
                    ).astype(BF)

    out = pltpu.make_async_copy(kvo, gkv, lcr)
    out.start()
    each(4, lambda e: [copy.wait_send() for copy in halo_copies(e)] and None)
    arrived(gq, gqr)
    out.wait()
    arrived(gimg, y2r)
    sent_all(GROUPS, z, z2_back)


ANY = pl.BlockSpec(memory_space=pl.ANY)
SMEM = pl.BlockSpec(memory_space=pltpu.SMEM)
DMA = pltpu.SemaphoreType.DMA


def sds(*shape):
    return jax.ShapeDtypeStruct(shape, BF)


def vm(*shape, dtype=BF):
    return pltpu.VMEM(shape, dtype)


def per_device(queries, keys_values, image_rows, cotangent, seq_image, vis_start, comp_lengths):
    groups = jnp.arange(GROUPS, dtype=jnp.int32)
    user = jnp.sum(jnp.where(seq_image[None, :] == groups[:, None], groups[None, :], 0), axis=1, dtype=jnp.int32)
    gq, gkv, gimg = pl.pallas_call(
        kernel,
        out_shape=[sds(ROWS, 2 * QW), sds(2, ROWS, 2 * KW), sds(16, 32, 128)],
        in_specs=[SMEM] * 4 + [ANY] * 3 + [pl.BlockSpec(memory_space=pltpu.VMEM)],
        out_specs=[ANY] * 3,
        scratch_shapes=[
            vm(16, 32, 128), vm(16, 32, 128), vm(16, 32, 128), vm(16, 32, 128), vm(8, 16, 128), vm(16, 16, 128),
            vm(32, 128), vm(32, 128), vm(32, 128), vm(VIS, QW), vm(384, 512), vm(512, 384),
            vm(CHIP_ROWS, QW), vm(CHIP_ROWS, QW), vm(2, LOCAL, KW), vm(8, VIS, 128), vm(8, PROMPT, 128),
            vm(2, 16, QW),
            vm(KEYS, CHIP_ROWS, dtype=F32), vm(PREFIX, 64, dtype=F32), vm(1, CHIP_ROWS, dtype=F32),
            vm(16, LOCAL, CHIP_ROWS, dtype=F32), vm(16, LOCAL, CHIP_ROWS, dtype=F32),
            vm(16, 8, CHIP_ROWS, dtype=F32), vm(16, PREFIX, CHIP_ROWS),
            vm(PREFIX, 128), vm(PREFIX, 128), vm(LOCAL, 128, dtype=F32), vm(LOCAL, 128, dtype=F32),
            vm(4, CHIP_ROWS, 512), vm(4, 2, LOCAL, 128), vm(2, 4, VIS, 128), vm(8, PROMPT, 128), vm(24, 16, 128),
            vm(16, 2, 4, 16, 128), vm(16, 32, 128), vm(2, 4, 2, ROWS, 128), vm(2, 4, 2, ROWS, 128),
            vm(2, 4, 2, 64, 128), vm(2, 8, 64, 128), vm(16, 32, 128), vm(16, 32, 128), vm(16, 32, 128), vm(32, 128),
            vm(2, ROWS, 2 * KW),
            DMA((16,)), DMA((16,)), DMA((32,)), DMA((3,)), DMA((4,)), DMA((16,)), DMA((16,)), DMA((16,)),
            DMA((2, 16)), DMA((16,)), DMA((4, 4)), DMA((4,)), DMA((2,)), DMA((16,)), DMA((16,)),
        ] + [DMA(())] * 21,
        compiler_params=pltpu.CompilerParams(
            collective_id=0, has_side_effects=True, vmem_limit_bytes=56 * 2**20
        ),
        name="grads",
    )(seq_image, user, vis_start, comp_lengths, queries[0], cotangent[0], keys_values[0], image_rows[0])

    gimg = gimg.reshape(8, 2, 32, 128)
    own = jnp.concatenate(
        [
            gimg[:, :, :16].reshape(8, 2 * QW),
            gimg[:, :, 16:20].reshape(8, 2 * KW),
            gimg[:, :, 20:24].reshape(8, 2 * KW),
        ],
        axis=1,
    )
    return (gq[None], gkv[None], own[None])


def solution(mesh):
    placed = (
        P("rollout", "ctx", None),
        P("rollout", None, "ctx", None),
        P("rollout", "ctx", None),
        P("rollout", "ctx", None),
        P(),
        P("rollout"),
        P("rollout", None),
    )
    return jax.shard_map(
        per_device,
        mesh=mesh,
        in_specs=placed,
        out_specs=(
            P("rollout", "ctx", None),
            P("rollout", None, "ctx", None),
            P("rollout", "ctx", None),
        ),
        check_vma=False,
    )
```

```python
import functools
import math

import jax
import jax.numpy as jnp
from jax import lax
from jax.experimental import pallas as pl
from jax.experimental.pallas import tpu as pltpu
from jax.sharding import PartitionSpec as P

HEADS = 32
KV_HEADS = 8
HEAD_DIM = 128
VIS = 256
PROMPT = 64
PREFIX = VIS + PROMPT
GROUPS = 16
SHARDS = 32
CHIPS = 16
ROWS = 128
CHIP_ROWS = 256
HALO = 320
LOCAL = HALO + CHIP_ROWS
KEYS = PREFIX + LOCAL
QW = HEADS * HEAD_DIM // 2
KW = KV_HEADS * HEAD_DIM // 2
MESH = pl.DeviceIdType.MESH
BF = jnp.bfloat16
F32 = jnp.float32
NEG = -1e30
NEAR = 4
PARTS = 2 * NEAR
LIMIT = 56
RS_AT = 2


def remote(src, dst, send, recv, z, c):
    return pltpu.make_async_remote_copy(
        src_ref=src, dst_ref=dst, send_sem=send, recv_sem=recv, device_id=(z, c), device_id_type=MESH
    )


def arrived(ref, sem):
    pltpu.make_async_copy(ref, ref, sem).wait()


def each(count, body):
    def step(k, carry):
        body(k)
        return carry

    lax.fori_loop(0, count, step, 0)


def send_all(count, me, copy, local):
    each(count - 1, lambda k: copy(lax.rem(me + 1 + k, count)).start())
    local(me).start()


def sent_all(count, me, copy):
    each(count - 1, lambda k: copy(lax.rem(me + 1 + k, count)).wait_send())


def send_but(count, me, copy, local):
    def body(k):
        @pl.when(k != me)
        def _():
            copy(k).start()

        @pl.when(k == me)
        def _():
            local(k).start()

    each(count, body)


def sent_but(count, me, copy):
    def body(k):
        @pl.when(k != me)
        def _():
            copy(k).wait_send()

    each(count, body)


def greet(z, c):
    barrier = pltpu.get_barrier_semaphore()
    i = c // 2

    def column(k):
        for to in (lax.rem(z + 1 + k, GROUPS), lax.rem(z + GROUPS - 1 - k, GROUPS)):
            for core in (0, 1):
                pl.semaphore_signal(barrier, inc=1, device_id=(to, 2 * i + core), device_id_type=MESH)

    def plane(k):
        pl.semaphore_signal(
            barrier, inc=1, device_id=(z, lax.rem(c + 1 + k, SHARDS)), device_id_type=MESH
        )

    each(NEAR, column)
    each(SHARDS - 1, plane)


def greeted():
    pl.semaphore_wait(pltpu.get_barrier_semaphore(), SHARDS - 1 + 4 * NEAR)


def one_hot(rows, cols, source):
    o = lax.broadcasted_iota(jnp.int32, (rows, cols), 0)
    n = lax.broadcasted_iota(jnp.int32, (rows, cols), 1)
    return jnp.where(n == source(o), 1.0, 0.0).astype(BF)


def piece_rows():
    shape = (8, 48, 384)
    piece = lax.broadcasted_iota(jnp.int32, shape, 0)
    y = lax.broadcasted_iota(jnp.int32, shape, 1)
    n = lax.broadcasted_iota(jnp.int32, shape, 2)
    half = piece % 2
    of_kv = y < 16
    y = jnp.where(of_kv, y, y - 16)
    row = 2 * (piece // 2) + jnp.where(of_kv, y // 8, y // 16)
    block = jnp.where(of_kv, 32 + 8 * ((y // 4) % 2) + 4 * half + y % 4, 16 * half + y % 16)
    return jnp.where(n == 8 * block + row, 1.0, 0.0).astype(BF).reshape(384, 384)


def kv_order(o):
    y = o // 16
    return (o % 16) * 8 + 4 * (y % 2) + 2 * (y // 4) + (y // 2) % 2


def kv_order_back(o):
    x = o % 8
    return ((x % 4) // 2 * 4 + x % 2 * 2 + x // 4) * 16 + o // 8


def q_order(o):
    return (o % 16) * 16 + o // 16


def kernel(
    seq_ref, vis_ref, len_ref, q, d, kv, img,
    gq, gkv, gimg,
    inv_ref, pieces, z1k, z1q, stage, z2k, z2q, kvp, qi, ta, tb, tm, ds, to_rows, kv_p, kv_pb, q_p,
    q2, d2, kvloc, kvimg, kvtxt, imgd,
    bias, ibias, valid, el, dwl, stat, sp, kp, vp, dkl, dvl,
    dq2, dkvloc, dkvimg, dkvtxt, heads,
    rsi, rst, hb0, hb1, hb2, dtx, rows, zbk, zbq, stage2, stage3, fin, tx, kvo, io,
    z1s, z2s, txs, sws, has, ags, ats, dss, ris, rts, hrs, qrs, xs, y1s, y2s,
    z1r, z2r, kir, y1r, y2r,
    tar, tbr, q2r, d2r, klr, ktr, d0r, d1r, rir, rtr, h0r, h1r, h2r, gqr, xr, lcr, far_sem,
):
    z = lax.axis_index("rollout")
    c = lax.axis_index("ctx")
    i = c // 2
    h = c % 2
    sib = 2 * i + 1 - h
    scale = 1.0 / math.sqrt(HEAD_DIM)
    to_log2 = scale * math.log2(math.e)
    vis = vis_ref[0]
    nt = (((1,), (1,)), ((), ()))
    greet(z, c)

    blocks = jnp.concatenate([img[:, 128 * k : 128 * (k + 1)].astype(F32) for k in range(48)], axis=0).astype(BF)
    in_pieces = piece_rows()
    pieces[...] = jnp.dot(in_pieces, blocks, preferred_element_type=F32).astype(BF).reshape(8, 48, 128)
    greeted()
    for to in (lax.rem(z + NEAR, GROUPS), lax.rem(z + GROUPS - NEAR, GROUPS)):
        for core in (0, 1):
            pl.semaphore_signal(far_sem, inc=1, device_id=(to, 2 * i + core), device_id_type=MESH)

    spans = (pl.ds(0, 16), pl.ds(16, 32))
    z1b, z2b, zbs = (z1k, z1q), (z2k, z2q), (zbk, zbq)

    def z1(p, n):
        j = lax.rem(z + GROUPS + 1 - NEAR + p, GROUPS)
        return remote(pieces.at[p // 2 * 2 + j % 2, spans[n]], z1b[n].at[p], z1s.at[n, p], z1r.at[n], j, c)

    def z1_here(n):
        p = NEAR - 1
        return pltpu.make_async_copy(
            pieces.at[p // 2 * 2 + z % 2, spans[n]], z1b[n].at[p], z1r.at[n]
        )

    others = [p for p in range(PARTS) if p != NEAR - 1]
    for n in (0, 1):
        for p in others:
            z1(p, n).start()
        z1_here(n).start()

    def text_src(k):
        ii, hh = k // 2, k % 2
        b = ii % 8
        return kv.at[
            b // 4,
            pl.ds(pl.multiple_of(32 * (ii // 8), 32), 32),
            pl.ds(pl.multiple_of(KW * hh + 128 * (b % 4), 128), 128),
        ]

    for place, buf, sem in ((0, ta, tar), (2, tb, tbr)):
        @pl.when(c == place)
        def _():
            send_all(
                SHARDS, c,
                lambda k: remote(text_src(k), buf, txs.at[k], sem, z, k),
                lambda k: pltpu.make_async_copy(text_src(k), buf, sem),
            )

    def cols(core, width):
        return pl.ds(pl.multiple_of(width * core, width), width)

    def rows_of(core, first):
        return pl.ds(pl.multiple_of(first + ROWS * core, 64), ROWS)

    def block(k):
        return pl.ds(pl.multiple_of(16 * k, 16), 16)

    def half_of(k):
        return pl.ds(pl.multiple_of(32 * (k // 8), 32), 32)

    def ahead(n):
        return lax.rem(i + n, CHIPS)

    my_rows = rows_of(h, 0)
    own_rows = rows_of(h, HALO)
    near_rows = rows_of(h, 64)
    swaps = [
        remote(d.at[:, cols(1 - h, QW)], d2.at[my_rows, :], sws.at[0], d2r, z, sib),
        remote(q.at[:, cols(1 - h, QW)], q2.at[my_rows, :], sws.at[1], q2r, z, sib),
        remote(kv.at[:, :, cols(1 - h, KW)], kvloc.at[:, own_rows, :], sws.at[2], klr, z, sib),
    ] + [
        remote(kv.at[:, :, pl.ds(KW * hh, KW)], kvloc.at[:, near_rows, :], has.at[hh], klr, z, 2 * ahead(1) + hh)
        for hh in (0, 1)
    ]
    far = [
        remote(
            kv.at[:, pl.ds(64, 64), pl.ds(KW * hh, KW)], kvloc.at[:, pl.ds(0, 64), :], has.at[2 + hh], klr, z,
            2 * ahead(2) + hh,
        )
        for hh in (0, 1)
    ]
    for copy in swaps:
        copy.start()

    @pl.when(h == 1)
    def _():
        for copy in far:
            copy.start()

    pltpu.make_async_copy(d.at[:, cols(h, QW)], d2.at[my_rows, :], d2r).start()
    pltpu.make_async_copy(q.at[:, cols(h, QW)], q2.at[my_rows, :], q2r).start()
    pltpu.make_async_copy(kv.at[:, :, cols(h, KW)], kvloc.at[:, own_rows, :], klr).start()

    to_rows[...] = in_pieces.T
    kv_p[...] = one_hot(128, 128, kv_order)
    kv_pb[...] = one_hot(128, 128, kv_order_back)
    q_p[...] = one_hot(256, 256, q_order)
    for o in range(GROUPS):
        user = jnp.int32(0)
        for g in range(GROUPS):
            user = jnp.where(seq_ref[g] == o, g, user)
        inv_ref[o] = user

    def slot_positions(lanes):
        r = lax.broadcasted_iota(jnp.int32, (PREFIX, lanes), 0)
        text = r - VIS
        return jnp.where(r < VIS, vis + r, jnp.where(text < vis, text, r))

    pos = CHIP_ROWS * i + lax.broadcasted_iota(jnp.int32, (1, CHIP_ROWS), 1)
    begin = jnp.full((1, CHIP_ROWS), PREFIX, jnp.int32)
    edge = jnp.int32(PREFIX)
    for k in range(16):
        edge = edge + len_ref[0, k]
        begin = jnp.where(pos >= edge, edge, begin)
    begin = jnp.where(pos < PREFIX, pos + 1, begin)
    valid[...] = jnp.where((pos >= vis) & (pos < vis + VIS), 0.0, 1.0)
    bias[:PREFIX, :] = jnp.where(slot_positions(CHIP_ROWS) <= pos, 0.0, NEG)
    at = CHIP_ROWS * i - HALO + lax.broadcasted_iota(jnp.int32, (LOCAL, CHIP_ROWS), 0)
    bias[PREFIX:, :] = jnp.where((at >= begin) & (at <= pos), 0.0, NEG)
    ipos = vis + 16 * i + lax.broadcasted_iota(jnp.int32, (1, 64), 1) % 16
    ibias[...] = jnp.where(slot_positions(64) <= ipos, 0.0, NEG)

    to_core = z % 2
    slot = 8 * h + z // 2
    here = jnp.where(to_core == h, z, GROUPS)
    here_back = jnp.where(to_core == h, slot, GROUPS)

    def part_of(o, j):
        return jnp.minimum((j - o + NEAR - 1) & (GROUPS - 1), PARTS - 1)

    def z2(g, n):
        return remote(
            stage.at[g, spans[n]], z2b[n].at[slot], z2s.at[n, g], z2r.at[n], g, 2 * i + to_core
        )

    def z2_here(g, n):
        return pltpu.make_async_copy(stage.at[g, spans[n]], z2b[n].at[slot], z2r.at[n])

    for n in (0, 1):
        arrived(z1b[n], z1r.at[n])

        def pick(g):
            stage[g, spans[n]] = z1b[n][part_of(seq_ref[g], z)]

        each(GROUPS, pick)
        if n == 0:
            pl.semaphore_wait(far_sem, 4)
        send_but(GROUPS, here, lambda g: z2(g, n), lambda g: z2_here(g, n))

    arrived(ta, tar)
    arrived(tb, tbr)
    t = 32 * (i // 8) + lax.broadcasted_iota(jnp.int32, (32, 128), 0)
    tm[...] = jnp.where(t < vis, ta[...].astype(F32), tb[...].astype(F32)).astype(BF)
    txt_part = kvtxt.at[i % 8, half_of(i), :]

    def atx(k):
        return remote(tm, txt_part, ats.at[k], ktr, z, 2 * k + h)

    send_all(CHIPS, i, atx, lambda k: pltpu.make_async_copy(tm, txt_part, ktr))

    def dsend(k):
        return remote(ds.at[block(k), :], imgd.at[0], dss.at[k], d0r, z, 2 * k + h)

    def dsend1(k):
        return remote(ds.at[block(12 + k), :], imgd.at[1], dss.at[k], d1r, z, 2 * (12 + k) + h)

    arrived(d2, d2r)

    @pl.when(i < 2)
    def _():
        shift = one_hot(VIS, CHIP_ROWS, lambda r: r + vis - CHIP_ROWS * i)
        for part in range(4):
            w = pl.ds(part * 512, 512)
            ds[:, w] = jnp.dot(shift, d2[:, w], preferred_element_type=F32).astype(BF)

    @pl.when(i == 0)
    def _():
        send_all(CHIPS, i, dsend, lambda k: pltpu.make_async_copy(ds.at[block(0), :], imgd.at[0], d0r))

    @pl.when(i == 1)
    def _():
        each(4, lambda k: dsend1(k).start())

    image = seq_ref[z]

    def slot_of(s, rp):
        even = (image + 1 - NEAR + 2 * rp) & (GROUPS - 1)
        j = jnp.where((even & 1) == h, even, (even + 1) & (GROUPS - 1))
        return 8 * s + j // 2

    def come(n):
        return jnp.concatenate([z2b[n][slot_of(s, rp)] for s in (0, 1) for rp in range(4)], axis=0)

    arrived(z2b[0], z2r.at[0])
    kvp[...] = jnp.dot(kv_p[...], come(0), preferred_element_type=F32).astype(BF).reshape(2, 4, 16, 128)

    def aim(half, k):
        return remote(kvp.at[half], kvimg.at[half, :, block(i), :], ags.at[half, k], kir.at[half], z, 2 * k + h)

    for half in (0, 1):
        send_all(
            CHIPS, i, lambda k: aim(half, k),
            lambda k: pltpu.make_async_copy(kvp.at[half], kvimg.at[half, :, block(i), :], kir.at[half]),
        )

    arrived(q2, q2r)
    arrived(kvloc, klr)

    def head_cols(e, k):
        return pl.ds(pl.multiple_of(512 * e + 128 * k, 128), 128)

    def key_cols(e):
        return pl.ds(pl.multiple_of(128 * e, 128), 128)

    def local_scores(e):
        k_rows = kvloc[0, :, key_cols(e)]
        v_rows = kvloc[1, :, key_cols(e)]
        for k in range(4):
            w128 = head_cols(e, k)
            n = 4 * e + k
            top = lax.dot_general(k_rows, q2[:, w128], nt, preferred_element_type=F32) * to_log2 + bias[PREFIX:, :]
            peak = jnp.max(top, axis=0, keepdims=True)
            ex = jnp.exp2(top - peak)
            dw = lax.dot_general(v_rows, d2[:, w128], nt, preferred_element_type=F32)
            el[n] = ex
            dwl[n] = dw
            lanes = pl.ds(CHIP_ROWS * k, CHIP_ROWS)
            stat[e, 0:1, lanes] = peak
            stat[e, 1:2, lanes] = jnp.sum(ex, axis=0, keepdims=True)
            stat[e, 2:3, lanes] = jnp.sum(ex * dw, axis=0, keepdims=True)

    each(4, local_scores)

    arrived(z2b[1], z2r.at[1])
    qi[...] = jnp.dot(q_p[...], come(1), preferred_element_type=F32).astype(BF).reshape(16, 16, 128)
    arrived(kvtxt, ktr)
    arrived(imgd.at[0], d0r)

    @pl.when(i >= 12)
    def _():
        arrived(imgd.at[1], d1r)

    def rimg(half, k):
        return remote(dkvimg.at[half, :, block(k), :], rsi.at[i, half], ris.at[half, k], rir, z, 2 * k + h)

    def rtxt(k):
        return remote(dkvtxt.at[k % 8, half_of(k), :], rst.at[i], rts.at[k], rtr, z, 2 * k + h)

    def four(x):
        return jnp.concatenate([x] * 4, axis=1)

    def prefix_grads(e):
        place = 2 * (e % 2)

        @pl.when(e % 2 == 0)
        def _():
            arrived(kvimg.at[e // 2], kir.at[e // 2])

        kp[:VIS, :] = kvimg[e // 2, place]
        kp[VIS:, :] = kvtxt[e]
        vp[:VIS, :] = kvimg[e // 2, place + 1]
        vp[VIS:, :] = kvtxt[4 + e]
        k_rows = kp[...]
        v_rows = vp[...]

        def scores(q_rows, d_rows, mask):
            top = lax.dot_general(k_rows, q_rows, nt, preferred_element_type=F32) * to_log2 + mask
            dw = lax.dot_general(v_rows, d_rows, nt, preferred_element_type=F32)
            return top, jnp.max(top, axis=0, keepdims=True), dw

        q_rows = qi[pl.ds(4 * e, 4)].reshape(64, 128)
        wide = pl.ds(pl.multiple_of(512 * e, 512), 512)
        d_rows = (imgd[0, :, wide].astype(F32) + jnp.where(i >= 12, imgd[1, :, wide].astype(F32), 0.0)).astype(BF)
        d_rows = jnp.concatenate([d_rows[:, 128 * k : 128 * (k + 1)] for k in range(4)], axis=0)
        top, peak, dw = scores(q_rows, d_rows, ibias[...])
        ex = jnp.exp2(top - peak)
        inv = 1.0 / jnp.sum(ex, axis=0, keepdims=True)
        delta = jnp.sum(ex * dw, axis=0, keepdims=True) * inv
        w = ex * inv
        s = (w * (dw - delta)).astype(BF)
        dk = jnp.dot(s, q_rows, preferred_element_type=F32)
        dv = jnp.dot(w.astype(BF), d_rows, preferred_element_type=F32)
        dqi = lax.dot_general(s, k_rows, (((0,), (0,)), ((), ())), preferred_element_type=F32) * scale
        heads[pl.ds(4 * e, 4)] = dqi.astype(BF).reshape(4, 16, 128)

        q_rows = jnp.concatenate([q2[:, head_cols(e, k)] for k in range(4)], axis=0)
        d_rows = jnp.concatenate([d2[:, head_cols(e, k)] for k in range(4)], axis=0)
        top, peak, dw = scores(q_rows, d_rows, four(bias[:PREFIX, :]))
        low = stat[e, 0:1, :]
        peak = jnp.maximum(peak, low)
        ex = jnp.exp2(top - peak)
        shrink = jnp.exp2(low - peak)
        inv = 1.0 / (jnp.sum(ex, axis=0, keepdims=True) + stat[e, 1:2, :] * shrink)
        delta = (jnp.sum(ex * dw, axis=0, keepdims=True) + stat[e, 2:3, :] * shrink) * inv
        inv = inv * four(valid[...])
        w = ex * inv
        s = (w * (dw - delta)).astype(BF)
        dk = dk + jnp.dot(s, q_rows, preferred_element_type=F32)
        dv = dv + jnp.dot(w.astype(BF), d_rows, preferred_element_type=F32)
        sp[e] = s
        stat[e, 0:1, :] = shrink * inv
        stat[e, 1:2, :] = delta
        dk = (dk * scale).astype(BF)
        dv = dv.astype(BF)
        dkvimg[e // 2, place] = dk[:VIS]
        dkvimg[e // 2, place + 1] = dv[:VIS]
        dkvtxt[e] = dk[VIS:]
        dkvtxt[4 + e] = dv[VIS:]

        @pl.when(e % 2 == 1)
        def _():
            half = e // 2
            send_all(
                CHIPS, i,
                lambda k: rimg(half, k),
                lambda k: pltpu.make_async_copy(dkvimg.at[half, :, block(k), :], rsi.at[i, half], rir),
            )

    def z1_back(t, n):
        return remote(
            stage2.at[t, spans[n]], zbs[n].at[z], y1s.at[n, t], y1r.at[n], 2 * (t % 8) + h, 2 * i + t // 8
        )

    def back_to_rows(n, value):
        rows[:, spans[n]] = value.astype(BF).reshape(8, 16 * (n + 1), 128)

        def pick(t):
            stage2[t, spans[n]] = rows[4 * (t // 8) + part_of(image, 2 * (t % 8) + h) // 2, spans[n]]

        each(16, pick)
        send_but(
            16, here_back, lambda t: z1_back(t, n),
            lambda t: pltpu.make_async_copy(stage2.at[t, spans[n]], zbs[n].at[z], y1r.at[n]),
        )

    def z2_back(p, n):
        o = lax.rem(z + GROUPS + NEAR - 1 - p, GROUPS)
        return remote(
            stage3.at[p, spans[n]], fin.at[p // 2 * 2 + z % 2, spans[n]], y2s.at[n, p], y2r.at[n], o, c
        )

    def second_back(n):
        arrived(zbs[n], y1r.at[n])

        def pick(p):
            stage3[p, spans[n]] = zbs[n][inv_ref[lax.rem(z + GROUPS + NEAR - 1 - p, GROUPS)]]

        each(PARTS, pick)
        for p in others:
            z2_back(p, n).start()
        p = NEAR - 1
        pltpu.make_async_copy(
            stage3.at[p, spans[n]], fin.at[p // 2 * 2 + z % 2, spans[n]], y2r.at[n]
        ).start()

    each(4, prefix_grads)
    back_to_rows(1, jnp.dot(q_p[...], heads[...].reshape(256, 128), preferred_element_type=F32))
    send_all(CHIPS, i, rtxt, lambda k: pltpu.make_async_copy(dkvtxt.at[k % 8, half_of(k), :], rst.at[i], rtr))

    def halo_copies(e):
        near, more = 2 * ahead(CHIPS - 1), 2 * ahead(CHIPS - 2)
        return [
            remote(dkvloc.at[e, :, rows_of(s, 64), :], hb1.at[h, e], hrs.at[s, e], h1r, z, near + s) for s in (0, 1)
        ] + [
            remote(dkvloc.at[e, :, pl.ds(0, 64), :], hb2.at[h, e], hrs.at[2, e], h2r, z, more + 1),
            remote(dkvloc.at[e, :, rows_of(1 - h, HALO), :], hb0.at[h, e], hrs.at[3, e], h0r, z, sib),
            remote(dq2.at[e, rows_of(1 - h, 0), :], gq.at[:, out_cols(e)], qrs.at[e], gqr, z, sib),
        ]

    def out_cols(e):
        return pl.ds(pl.multiple_of(QW * h + 512 * e, 512), 512)

    def local_grads(e):
        k_rows = kvloc[0, :, key_cols(e)]
        kt = k_rows.T
        kp[:VIS, :] = kvimg[e // 2, 2 * (e % 2)]
        kp[VIS:, :] = kvtxt[e]
        kpt = kp[...].T
        for k in range(4):
            n = 4 * e + k
            q_rows = q2[:, head_cols(e, k)]
            d_rows = d2[:, head_cols(e, k)]
            lanes = pl.ds(CHIP_ROWS * k, CHIP_ROWS)
            w = el[n] * stat[e, 0:1, lanes]
            s = (w * (dwl[n] - stat[e, 1:2, lanes])).astype(BF)
            part = jnp.dot(s, q_rows, preferred_element_type=F32)
            dkl[...] = part if k == 0 else dkl[...] + part
            part = jnp.dot(w.astype(BF), d_rows, preferred_element_type=F32)
            dvl[...] = part if k == 0 else dvl[...] + part
            dqt = jnp.dot(kt, s, preferred_element_type=F32) + jnp.dot(kpt, sp[e, :, lanes], preferred_element_type=F32)
            dq2[e, :, 128 * k : 128 * (k + 1)] = (dqt * scale).T.astype(BF)
        dkvloc[e, 0] = (dkl[...] * scale).astype(BF)
        dkvloc[e, 1] = dvl[...].astype(BF)
        for copy in halo_copies(e):
            copy.start()
        pltpu.make_async_copy(dkvloc.at[e, :, rows_of(h, HALO), :], hb0.at[h, e], h0r).start()
        pltpu.make_async_copy(dq2.at[e, rows_of(h, 0), :], gq.at[:, out_cols(e)], gqr).start()

    txt_slot = dtx.at[h, i % 8, half_of(i), :]

    def reduce_prefix():
        arrived(rsi, rir)
        total = rsi[0].astype(F32)
        for k in range(1, CHIPS):
            total = total + rsi[k].astype(F32)
        total = total.astype(BF).reshape(128, 128)
        back_to_rows(0, jnp.dot(kv_pb[...], total, preferred_element_type=F32))
        arrived(rst, rtr)
        total = rst[0].astype(F32)
        for k in range(1, CHIPS):
            total = total + rst[k].astype(F32)
        tx[...] = total.astype(BF)
        for n, place in ((0, 0), (1, 2)):
            @pl.when(c != place)
            def _():
                remote(tx, txt_slot, xs.at[n], xr, z, place).start()

            @pl.when(c == place)
            def _():
                pltpu.make_async_copy(tx, txt_slot, xr).start()

    def rest(e):
        local_grads(e)

        @pl.when(e == RS_AT)
        def _():
            reduce_prefix()

    each(4, rest)

    second_back(1)

    for n in (0, 1):
        for p in others:
            z1(p, n).wait_send()
        sent_but(GROUPS, here, lambda g: z2(g, n))
    for place, buf, sem in ((0, ta, tar), (2, tb, tbr)):
        @pl.when(c == place)
        def _():
            sent_all(SHARDS, c, lambda k: remote(text_src(k), buf, txs.at[k], sem, z, k))

    for copy in swaps:
        copy.wait_send()

    @pl.when(h == 1)
    def _():
        for copy in far:
            copy.wait_send()

    sent_all(CHIPS, i, atx)
    for half in (0, 1):
        sent_all(CHIPS, i, lambda k: aim(half, k))

    @pl.when(i == 0)
    def _():
        sent_all(CHIPS, i, dsend)

    @pl.when(i == 1)
    def _():
        each(4, lambda k: dsend1(k).wait_send())

    second_back(0)

    for half in (0, 1):
        sent_all(CHIPS, i, lambda k: rimg(half, k))
    sent_all(CHIPS, i, rtxt)
    for n in (0, 1):
        sent_but(16, here_back, lambda t: z1_back(t, n))
    for n, place in ((0, 0), (1, 2)):
        @pl.when(c != place)
        def _():
            remote(tx, txt_slot, xs.at[n], xr, z, place).wait_send()

    arrived(hb0, h0r)
    arrived(hb1, h1r)

    @pl.when(h == 1)
    def _():
        arrived(hb2, h2r)

    for hh in (0, 1):
        for e in range(4):
            for n in (0, 1):
                w = pl.ds(KW * hh + 128 * e, 128)
                near = hb0[hh, e, n].astype(F32) + hb1[hh, e, n].astype(F32)
                kvo[n, :64, w] = near[:64].astype(BF)
                more = jnp.where(h == 1, hb2[hh, e, n].astype(F32), 0.0)
                kvo[n, 64:, w] = (near[64:] + more).astype(BF)

    t64 = lax.broadcasted_iota(jnp.int32, (PROMPT, 128), 0)
    for place in (0, 2):
        @pl.when(c == place)
        def _():
            arrived(dtx, xr)
            keep = t64 < vis if place == 0 else t64 >= vis
            for hh in (0, 1):
                for b in range(8):
                    kvo[b // 4, :64, pl.ds(KW * hh + 128 * (b % 4), 128)] = jnp.where(
                        keep, dtx[hh, b].astype(F32), 0.0
                    ).astype(BF)

    out = pltpu.make_async_copy(kvo, gkv, lcr)
    out.start()
    each(4, lambda e: [copy.wait_send() for copy in halo_copies(e)] and None)
    arrived(gq, gqr)
    out.wait()
    for n in (0, 1):
        arrived(fin.at[:, spans[n]], y2r.at[n])
    blocks = jnp.dot(to_rows[...], fin[...].reshape(384, 128), preferred_element_type=F32)
    for k in range(48):
        io[:, 128 * k : 128 * (k + 1)] = blocks[8 * k : 8 * (k + 1)].astype(BF)
    out = pltpu.make_async_copy(io, gimg, lcr)
    out.start()
    for n in (0, 1):
        for p in others:
            z2_back(p, n).wait_send()
    out.wait()


ANY = pl.BlockSpec(memory_space=pl.ANY)
HBM = pl.BlockSpec(memory_space=pltpu.HBM)
SMEM = pl.BlockSpec(memory_space=pltpu.SMEM)
DMA = pltpu.SemaphoreType.DMA


def sds(*shape):
    return jax.ShapeDtypeStruct(shape, BF)


def vm(*shape, dtype=BF):
    return pltpu.VMEM(shape, dtype)


def per_device(queries, keys_values, image_rows, cotangent, seq_image, vis_start, comp_lengths):
    gq, gkv, gimg = pl.pallas_call(
        kernel,
        out_shape=[sds(ROWS, 2 * QW), sds(2, ROWS, 2 * KW), sds(8, 2 * QW + 4 * KW)],
        in_specs=[SMEM] * 3 + [HBM] * 3 + [pl.BlockSpec(memory_space=pltpu.VMEM)],
        out_specs=[ANY] * 3,
        scratch_shapes=[
            pltpu.SMEM((16,), jnp.int32),
            vm(8, 48, 128), vm(8, 16, 128), vm(8, 32, 128), vm(16, 48, 128), vm(16, 16, 128), vm(16, 32, 128),
            vm(2, 4, 16, 128), vm(16, 16, 128),
            vm(32, 128), vm(32, 128), vm(32, 128), vm(VIS, QW), vm(384, 384), vm(128, 128), vm(128, 128), vm(256, 256),
            vm(CHIP_ROWS, QW), vm(CHIP_ROWS, QW), vm(2, LOCAL, KW), vm(2, 4, VIS, 128), vm(8, PROMPT, 128),
            vm(2, 16, QW),
            vm(KEYS, CHIP_ROWS, dtype=F32), vm(PREFIX, 64, dtype=F32), vm(1, CHIP_ROWS, dtype=F32),
            vm(16, LOCAL, CHIP_ROWS, dtype=F32), vm(16, LOCAL, CHIP_ROWS, dtype=F32),
            vm(4, 8, 4 * CHIP_ROWS, dtype=F32), vm(4, PREFIX, 4 * CHIP_ROWS),
            vm(PREFIX, 128), vm(PREFIX, 128), vm(LOCAL, 128, dtype=F32), vm(LOCAL, 128, dtype=F32),
            vm(4, CHIP_ROWS, 512), vm(4, 2, LOCAL, 128), vm(2, 4, VIS, 128), vm(8, PROMPT, 128), vm(16, 16, 128),
            vm(16, 2, 4, 16, 128), vm(16, 32, 128), vm(2, 4, 2, ROWS, 128), vm(2, 4, 2, ROWS, 128),
            vm(2, 4, 2, 64, 128), vm(2, 8, 64, 128), vm(8, 48, 128), vm(16, 16, 128), vm(16, 32, 128),
            vm(16, 48, 128), vm(8, 48, 128), vm(8, 48, 128), vm(32, 128), vm(2, ROWS, 2 * KW), vm(8, 2 * QW + 4 * KW),
            DMA((2, 8)), DMA((2, 16)), DMA((32,)), DMA((3,)), DMA((4,)), DMA((2, 16)), DMA((16,)), DMA((16,)),
            DMA((2, 16)), DMA((16,)), DMA((4, 4)), DMA((4,)), DMA((2,)), DMA((2, 16)), DMA((2, 8)),
            DMA((2,)), DMA((2,)), DMA((2,)), DMA((2,)), DMA((2,)),
        ] + [DMA(())] * 16 + [pltpu.SemaphoreType.REGULAR],
        compiler_params=pltpu.CompilerParams(
            collective_id=0, has_side_effects=True, vmem_limit_bytes=LIMIT * 2**20
        ),
        name="grads",
    )(seq_image, vis_start, comp_lengths, queries[0], cotangent[0], keys_values[0], image_rows[0])
    return (gq[None], gkv[None], gimg[None])


def solution(mesh):
    placed = (
        P("rollout", "ctx", None),
        P("rollout", None, "ctx", None),
        P("rollout", "ctx", None),
        P("rollout", "ctx", None),
        P(),
        P("rollout"),
        P("rollout", None),
    )
    return jax.shard_map(
        per_device,
        mesh=mesh,
        in_specs=placed,
        out_specs=(
            P("rollout", "ctx", None),
            P("rollout", None, "ctx", None),
            P("rollout", "ctx", None),
        ),
        check_vma=False,
    )
```

```python
import functools
import math

import jax
import jax.numpy as jnp
from jax import lax
from jax.experimental import pallas as pl
from jax.experimental.pallas import tpu as pltpu
from jax.sharding import PartitionSpec as P

HEADS = 32
KV_HEADS = 8
HEAD_DIM = 128
VIS = 256
PROMPT = 64
PREFIX = VIS + PROMPT
GROUPS = 16
SHARDS = 32
CHIPS = 16
ROWS = 128
CHIP_ROWS = 256
HALO = 320
LOCAL = HALO + CHIP_ROWS
KEYS = PREFIX + LOCAL
QW = HEADS * HEAD_DIM // 2
KW = KV_HEADS * HEAD_DIM // 2
MESH = pl.DeviceIdType.MESH
BF = jnp.bfloat16
F32 = jnp.float32
NEG = -1e30
NEAR = 4
PARTS = 2 * NEAR
LIMIT = 40
RS_AT = 2


def remote(src, dst, send, recv, z, c):
    return pltpu.make_async_remote_copy(
        src_ref=src, dst_ref=dst, send_sem=send, recv_sem=recv, device_id=(z, c), device_id_type=MESH
    )


def arrived(ref, sem):
    pltpu.make_async_copy(ref, ref, sem).wait()


def each(count, body):
    def step(k, carry):
        body(k)
        return carry

    lax.fori_loop(0, count, step, 0)


def send_all(count, me, copy, local):
    each(count - 1, lambda k: copy(lax.rem(me + 1 + k, count)).start())
    local(me).start()


def sent_all(count, me, copy):
    each(count - 1, lambda k: copy(lax.rem(me + 1 + k, count)).wait_send())


def send_but(count, me, copy, local):
    def body(k):
        @pl.when(k != me)
        def _():
            copy(k).start()

        @pl.when(k == me)
        def _():
            local(k).start()

    each(count, body)


def sent_but(count, me, copy):
    def body(k):
        @pl.when(k != me)
        def _():
            copy(k).wait_send()

    each(count, body)


def greet(z, c):
    barrier = pltpu.get_barrier_semaphore()
    i = c // 2

    def column(k):
        for to in (lax.rem(z + 1 + k, GROUPS), lax.rem(z + GROUPS - 1 - k, GROUPS)):
            for core in (0, 1):
                pl.semaphore_signal(barrier, inc=1, device_id=(to, 2 * i + core), device_id_type=MESH)

    def plane(k):
        pl.semaphore_signal(
            barrier, inc=1, device_id=(z, lax.rem(c + 1 + k, SHARDS)), device_id_type=MESH
        )

    each(NEAR, column)
    each(SHARDS - 1, plane)


def greeted():
    pl.semaphore_wait(pltpu.get_barrier_semaphore(), SHARDS - 1 + 4 * NEAR)


def one_hot(rows, cols, source):
    o = lax.broadcasted_iota(jnp.int32, (rows, cols), 0)
    n = lax.broadcasted_iota(jnp.int32, (rows, cols), 1)
    return jnp.where(n == source(o), 1.0, 0.0).astype(BF)


def piece_rows():
    shape = (8, 48, 384)
    piece = lax.broadcasted_iota(jnp.int32, shape, 0)
    y = lax.broadcasted_iota(jnp.int32, shape, 1)
    n = lax.broadcasted_iota(jnp.int32, shape, 2)
    half = piece % 2
    of_kv = y < 16
    y = jnp.where(of_kv, y, y - 16)
    row = 2 * (piece // 2) + jnp.where(of_kv, y // 8, y // 16)
    block = jnp.where(of_kv, 32 + 8 * ((y // 4) % 2) + 4 * half + y % 4, 16 * half + y % 16)
    return jnp.where(n == 8 * block + row, 1.0, 0.0)


def kv_order(o):
    y = o // 16
    return (o % 16) * 8 + 4 * (y % 2) + 2 * (y // 4) + (y // 2) % 2


def kv_order_back(o):
    x = o % 8
    return ((x % 4) // 2 * 4 + x % 2 * 2 + x // 4) * 16 + o // 8


def q_order(o):
    return (o % 16) * 16 + o // 16


def kernel(
    seq_ref, vis_ref, len_ref, q, d, kv, img,
    gq, gkv, gimg,
    inv_ref, pieces, z1k, z1q, stage, z2k, z2q, kvp, qi, ta, tb, tm, ds, dnext, to_kv, to_q, kv_p, kv_pb, q_p,
    q2, d2, kvloc, kvimg, kvtxt, imgd,
    bias, ibias, valid, el, dwl, stat, sp, kp, vp, dkl, dvl,
    dq2, dkvloc, dkvimg, dkvtxt, heads,
    rsi, rst, hb0, hb1, hb2, dtx, rows, zbk, zbq, stage2, stage3, fin, tx, kvo, io,
    z1s, z2s, txs, sws, has, ags, ats, dss, dns, ris, rts, hrs, qrs, xs, y1s, y2s, ims,
    z1r, z2r, kir, y1r, y2r, klr, kfr,
    tar, tbr, q2r, d2r, ktr, d0r, dnr, rir, rtr, h0r, h1r, h2r, gqr, xr, lcr, far_sem,
):
    z = lax.axis_index("rollout")
    c = lax.axis_index("ctx")
    i = c // 2
    h = c % 2
    sib = 2 * i + 1 - h
    scale = 1.0 / math.sqrt(HEAD_DIM)
    to_log2 = scale * math.log2(math.e)
    vis = vis_ref[0]
    nt = (((1,), (1,)), ((), ()))
    load = pltpu.make_async_copy(img, io, lcr)
    load.start()
    greet(z, c)

    in_pieces = piece_rows()
    load.wait()
    blocks = jnp.concatenate([io[:, 128 * k : 128 * (k + 1)].astype(F32) for k in range(48)], axis=0).astype(BF)
    pieces[...] = jnp.dot(in_pieces.astype(BF).reshape(384, 384), blocks, preferred_element_type=F32).astype(BF).reshape(8, 48, 128)
    greeted()
    for to in (lax.rem(z + NEAR, GROUPS), lax.rem(z + GROUPS - NEAR, GROUPS)):
        for core in (0, 1):
            pl.semaphore_signal(far_sem, inc=1, device_id=(to, 2 * i + core), device_id_type=MESH)

    spans = (pl.ds(0, 16), pl.ds(16, 32))
    z1b, z2b, zbs = (z1k, z1q), (z2k, z2q), (zbk, zbq)

    def z1(p, n):
        j = lax.rem(z + GROUPS + 1 - NEAR + p, GROUPS)
        return remote(pieces.at[p // 2 * 2 + j % 2, spans[n]], z1b[n].at[p], z1s.at[n, p], z1r.at[n], j, c)

    def z1_here(n):
        p = NEAR - 1
        return pltpu.make_async_copy(
            pieces.at[p // 2 * 2 + z % 2, spans[n]], z1b[n].at[p], z1r.at[n]
        )

    others = [p for p in range(PARTS) if p != NEAR - 1]
    for n in (0, 1):
        for p in others:
            z1(p, n).start()
        z1_here(n).start()

    def text_src(k):
        ii, hh = k // 2, k % 2
        b = ii % 8
        return kv.at[
            b // 4,
            pl.ds(pl.multiple_of(32 * (ii // 8), 32), 32),
            pl.ds(pl.multiple_of(KW * hh + 128 * (b % 4), 128), 128),
        ]

    for place, buf, sem in ((0, ta, tar), (2, tb, tbr)):
        @pl.when(c == place)
        def _():
            send_all(
                SHARDS, c,
                lambda k: remote(text_src(k), buf, txs.at[k], sem, z, k),
                lambda k: pltpu.make_async_copy(text_src(k), buf, sem),
            )

    def cols(core, width):
        return pl.ds(pl.multiple_of(width * core, width), width)

    def rows_of(core, first):
        return pl.ds(pl.multiple_of(first + ROWS * core, 64), ROWS)

    def block(k):
        return pl.ds(pl.multiple_of(16 * k, 16), 16)

    def half_of(k):
        return pl.ds(pl.multiple_of(32 * (k // 8), 32), 32)

    def ahead(n):
        return lax.rem(i + n, CHIPS)

    my_rows = rows_of(h, 0)
    own_rows = rows_of(h, HALO)
    near_rows = rows_of(h, 64)

    def kv_cols(core, e):
        return pl.ds(pl.multiple_of(KW * core + 128 * e, 128), 128)

    sends_near = (i >= 1) & (i < CHIPS - 1)
    sends_far = (i >= 2) & (i < CHIPS - 1)
    has_near = i >= 2
    has_far = i >= 3
    far_rows = pl.ds(0, 64)

    def own_in(e):
        return remote(
            kv.at[:, :, kv_cols(1 - h, e)], kvloc.at[e, :, own_rows, :], has.at[2, e], klr.at[e], z, sib
        )

    def near_in(e):
        return [
            remote(
                kv.at[:, :, kv_cols(hh, e)], kvloc.at[e, :, near_rows, :], has.at[hh, e], klr.at[e], z,
                2 * ahead(1) + hh,
            )
            for hh in (0, 1)
        ]

    def far_in(e):
        return remote(
            kvloc.at[e, :, pl.ds(HALO - 64, 64), :], kvloc.at[e, :, far_rows, :], has.at[3, e], kfr.at[e], z,
            2 * ahead(1) + h,
        )

    def halo_start(e):
        @pl.when(sends_near)
        def _():
            for copy in near_in(e):
                copy.start()

        own_in(e).start()
        pltpu.make_async_copy(kv.at[:, :, kv_cols(h, e)], kvloc.at[e, :, own_rows, :], klr.at[e]).start()

    def near_come(e):
        @pl.when(has_near)
        def _():
            arrived(kvloc.at[e, :, pl.ds(64, LOCAL - 64), :], klr.at[e])

        @pl.when(i < 2)
        def _():
            arrived(kvloc.at[e, :, pl.ds(HALO, CHIP_ROWS), :], klr.at[e])
            kvloc[e, :, 64:HALO, :] = jnp.zeros((2, HALO - 64, 128), BF)

        @pl.when(sends_far)
        def _():
            far_in(e).start()

    def far_come(e):
        @pl.when(has_far)
        def _():
            arrived(kvloc.at[e, :, far_rows, :], kfr.at[e])

        @pl.when(i < 3)
        def _():
            kvloc[e, :, 0:64, :] = jnp.zeros((2, 64, 128), BF)

    swaps = [
        remote(d.at[:, cols(1 - h, QW)], d2.at[my_rows, :], sws.at[0], d2r, z, sib),
        remote(q.at[:, cols(1 - h, QW)], q2.at[my_rows, :], sws.at[1], q2r, z, sib),
    ]
    halo_start(0)
    for copy in swaps:
        copy.start()
    pltpu.make_async_copy(d.at[:, cols(h, QW)], d2.at[my_rows, :], d2r).start()
    pltpu.make_async_copy(q.at[:, cols(h, QW)], q2.at[my_rows, :], q2r).start()
    halo_start(1)

    def dnear(hh):
        return remote(d.at[pl.ds(0, 64), pl.ds(QW * hh, QW)], dnext, dns.at[hh], dnr, z, hh)

    def dsend(k):
        return remote(ds.at[block(k), :], imgd, dss.at[k], d0r, z, 2 * k + h)

    @pl.when(c == 2)
    def _():
        for hh in (0, 1):
            dnear(hh).start()

    def rest_of_image():
        arrived(dnext, dnr)
        shift = one_hot(64, CHIP_ROWS, lambda r: r + 192 + vis)
        more = one_hot(64, 64, lambda r: r + 192 + vis - CHIP_ROWS)
        for part in range(4):
            w = pl.ds(part * 512, 512)
            rows_d = jnp.dot(shift, d2[:, w], preferred_element_type=F32)
            rows_d = rows_d + jnp.dot(more, dnext[:, w], preferred_element_type=F32)
            ds[192:, w] = rows_d.astype(BF)
        each(4, lambda k: dsend(k + 12).start())

    to_kv[...] = in_pieces[:, :16, 256:].astype(BF).reshape(128, 128).T
    to_q[...] = in_pieces[:, 16:, :256].astype(BF).reshape(256, 256).T
    kv_p[...] = one_hot(128, 128, kv_order)
    kv_pb[...] = one_hot(128, 128, kv_order_back)
    q_p[...] = one_hot(256, 256, q_order)
    for o in range(GROUPS):
        user = jnp.int32(0)
        for g in range(GROUPS):
            user = jnp.where(seq_ref[g] == o, g, user)
        inv_ref[o] = user

    def slot_positions(lanes):
        r = lax.broadcasted_iota(jnp.int32, (PREFIX, lanes), 0)
        text = r - VIS
        return jnp.where(r < VIS, vis + r, jnp.where(text < vis, text, r))

    pos = CHIP_ROWS * i + lax.broadcasted_iota(jnp.int32, (1, CHIP_ROWS), 1)
    begin = jnp.full((1, CHIP_ROWS), PREFIX, jnp.int32)
    edge = jnp.int32(PREFIX)
    for k in range(16):
        edge = edge + len_ref[0, k]
        begin = jnp.where(pos >= edge, edge, begin)
    begin = jnp.where(pos < PREFIX, pos + 1, begin)
    valid[...] = jnp.where((pos >= vis) & (pos < vis + VIS), 0.0, 1.0)
    bias[:PREFIX, :] = jnp.where(slot_positions(CHIP_ROWS) <= pos, 0.0, NEG)
    at = CHIP_ROWS * i - HALO + lax.broadcasted_iota(jnp.int32, (LOCAL, CHIP_ROWS), 0)
    bias[PREFIX:, :] = jnp.where((at >= begin) & (at <= pos), 0.0, NEG)
    ipos = vis + 16 * i + lax.broadcasted_iota(jnp.int32, (1, 64), 1) % 16
    ibias[...] = jnp.where(slot_positions(64) <= ipos, 0.0, NEG)

    to_core = z % 2
    slot = 8 * h + z // 2
    here = jnp.where(to_core == h, z, GROUPS)
    here_back = jnp.where(to_core == h, slot, GROUPS)

    def part_of(o, j):
        return jnp.minimum((j - o + NEAR - 1) & (GROUPS - 1), PARTS - 1)

    def z2(g, n):
        return remote(
            stage.at[g, spans[n]], z2b[n].at[slot], z2s.at[n, g], z2r.at[n], g, 2 * i + to_core
        )

    def z2_here(g, n):
        return pltpu.make_async_copy(stage.at[g, spans[n]], z2b[n].at[slot], z2r.at[n])

    for n in (0, 1):
        arrived(z1b[n], z1r.at[n])

        def pick(g):
            stage[g, spans[n]] = z1b[n][part_of(seq_ref[g], z)]

        each(GROUPS, pick)
        if n == 0:
            pl.semaphore_wait(far_sem, 4)
        send_but(GROUPS, here, lambda g: z2(g, n), lambda g: z2_here(g, n))

    @pl.when(i == 0)
    def _():
        arrived(d2, d2r)
        shift = one_hot(192, CHIP_ROWS, lambda r: r + vis)
        for part in range(4):
            w = pl.ds(part * 512, 512)
            ds[:192, w] = jnp.dot(shift, d2[:, w], preferred_element_type=F32).astype(BF)
        pltpu.make_async_copy(ds.at[block(0), :], imgd, d0r).start()
        each(11, lambda k: dsend(k + 1).start())

    halo_start(2)
    halo_start(3)

    image = seq_ref[z]

    def slot_of(s, rp):
        even = (image + 1 - NEAR + 2 * rp) & (GROUPS - 1)
        j = jnp.where((even & 1) == h, even, (even + 1) & (GROUPS - 1))
        return 8 * s + j // 2

    def come(n):
        return jnp.concatenate([z2b[n][slot_of(s, rp)] for s in (0, 1) for rp in range(4)], axis=0)

    def aim(half, k):
        return remote(kvp.at[half], kvimg.at[half, :, block(i), :], ags.at[half, k], kir.at[half], z, 2 * k + h)

    def hand_round():
        arrived(z2b[0], z2r.at[0])
        kvp[...] = jnp.dot(kv_p[...], come(0), preferred_element_type=F32).astype(BF).reshape(2, 4, 16, 128)

        for half in (0, 1):
            send_all(
                CHIPS, i, lambda k: aim(half, k),
                lambda k: pltpu.make_async_copy(kvp.at[half], kvimg.at[half, :, block(i), :], kir.at[half]),
            )

    arrived(q2, q2r)

    @pl.when(i > 0)
    def _():
        arrived(d2, d2r)


    def head_cols(e, k):
        return pl.ds(pl.multiple_of(512 * e + 128 * k, 128), 128)

    def local_scores(e):
        far_come(e)
        k_rows = kvloc[e, 0]
        v_rows = kvloc[e, 1]
        for k in range(4):
            w128 = head_cols(e, k)
            n = 4 * e + k
            top = lax.dot_general(k_rows, q2[:, w128], nt, preferred_element_type=F32) * to_log2 + bias[PREFIX:, :]
            peak = jnp.max(top, axis=0, keepdims=True)
            ex = jnp.exp2(top - peak)
            dw = lax.dot_general(v_rows, d2[:, w128], nt, preferred_element_type=F32)
            el[n] = ex
            dwl[n] = dw
            lanes = pl.ds(CHIP_ROWS * k, CHIP_ROWS)
            stat[e, 0:1, lanes] = peak
            stat[e, 1:2, lanes] = jnp.sum(ex, axis=0, keepdims=True)
            stat[e, 2:3, lanes] = jnp.sum(ex * dw, axis=0, keepdims=True)

    def prefix_come():
        arrived(z2b[1], z2r.at[1])
        qi[...] = jnp.dot(q_p[...], come(1), preferred_element_type=F32).astype(BF).reshape(16, 16, 128)
        arrived(kvtxt, ktr)
        arrived(imgd, d0r)

    def rimg(half, k):
        return remote(dkvimg.at[half, :, block(k), :], rsi.at[i, half], ris.at[half, k], rir, z, 2 * k + h)

    def rtxt(k):
        return remote(dkvtxt.at[k % 8, half_of(k), :], rst.at[i], rts.at[k], rtr, z, 2 * k + h)

    def four(x):
        return jnp.concatenate([x] * 4, axis=1)

    def prefix_grads(e):
        place = 2 * (e % 2)

        @pl.when(e == 0)
        def _():
            prefix_come()

        @pl.when(e % 2 == 0)
        def _():
            arrived(kvimg.at[e // 2], kir.at[e // 2])

        kp[:VIS, :] = kvimg[e // 2, place]
        kp[VIS:, :] = kvtxt[e]
        vp[:VIS, :] = kvimg[e // 2, place + 1]
        vp[VIS:, :] = kvtxt[4 + e]
        k_rows = kp[...]
        v_rows = vp[...]

        def scores(q_rows, d_rows, mask):
            top = lax.dot_general(k_rows, q_rows, nt, preferred_element_type=F32) * to_log2 + mask
            dw = lax.dot_general(v_rows, d_rows, nt, preferred_element_type=F32)
            return top, jnp.max(top, axis=0, keepdims=True), dw

        q_rows = qi[pl.ds(4 * e, 4)].reshape(64, 128)
        wide = pl.ds(pl.multiple_of(512 * e, 512), 512)
        d_rows = imgd[:, wide]
        d_rows = jnp.concatenate([d_rows[:, 128 * k : 128 * (k + 1)] for k in range(4)], axis=0)
        top, peak, dw = scores(q_rows, d_rows, ibias[...])
        ex = jnp.exp2(top - peak)
        inv = 1.0 / jnp.sum(ex, axis=0, keepdims=True)
        delta = jnp.sum(ex * dw, axis=0, keepdims=True) * inv
        w = ex * inv
        s = (w * (dw - delta)).astype(BF)
        dk = jnp.dot(s, q_rows, preferred_element_type=F32)
        dv = jnp.dot(w.astype(BF), d_rows, preferred_element_type=F32)
        dqi = lax.dot_general(s, k_rows, (((0,), (0,)), ((), ())), preferred_element_type=F32) * scale
        heads[pl.ds(4 * e, 4)] = dqi.astype(BF).reshape(4, 16, 128)

        q_rows = jnp.concatenate([q2[:, head_cols(e, k)] for k in range(4)], axis=0)
        d_rows = jnp.concatenate([d2[:, head_cols(e, k)] for k in range(4)], axis=0)
        top, peak, dw = scores(q_rows, d_rows, four(bias[:PREFIX, :]))
        low = stat[e, 0:1, :]
        peak = jnp.maximum(peak, low)
        ex = jnp.exp2(top - peak)
        shrink = jnp.exp2(low - peak)
        inv = 1.0 / (jnp.sum(ex, axis=0, keepdims=True) + stat[e, 1:2, :] * shrink)
        delta = (jnp.sum(ex * dw, axis=0, keepdims=True) + stat[e, 2:3, :] * shrink) * inv
        inv = inv * four(valid[...])
        w = ex * inv
        s = (w * (dw - delta)).astype(BF)
        dk = dk + jnp.dot(s, q_rows, preferred_element_type=F32)
        dv = dv + jnp.dot(w.astype(BF), d_rows, preferred_element_type=F32)
        sp[e] = s
        stat[e, 0:1, :] = shrink * inv
        stat[e, 1:2, :] = delta
        dk = (dk * scale).astype(BF)
        dv = dv.astype(BF)
        dkvimg[e // 2, place] = dk[:VIS]
        dkvimg[e // 2, place + 1] = dv[:VIS]
        dkvtxt[e] = dk[VIS:]
        dkvtxt[4 + e] = dv[VIS:]

        @pl.when(e % 2 == 1)
        def _():
            half = e // 2
            send_all(
                CHIPS, i,
                lambda k: rimg(half, k),
                lambda k: pltpu.make_async_copy(dkvimg.at[half, :, block(k), :], rsi.at[i, half], rir),
            )

    def z1_back(t, n):
        return remote(
            stage2.at[t, spans[n]], zbs[n].at[z], y1s.at[n, t], y1r.at[n], 2 * (t % 8) + h, 2 * i + t // 8
        )

    def back_to_rows(n, value):
        rows[:, spans[n]] = value.astype(BF).reshape(8, 16 * (n + 1), 128)

        def pick(t):
            stage2[t, spans[n]] = rows[4 * (t // 8) + part_of(image, 2 * (t % 8) + h) // 2, spans[n]]

        each(16, pick)
        send_but(
            16, here_back, lambda t: z1_back(t, n),
            lambda t: pltpu.make_async_copy(stage2.at[t, spans[n]], zbs[n].at[z], y1r.at[n]),
        )

    def z2_back(p, n):
        o = lax.rem(z + GROUPS + NEAR - 1 - p, GROUPS)
        return remote(
            stage3.at[p, spans[n]], fin.at[p // 2 * 2 + z % 2, spans[n]], y2s.at[n, p], y2r.at[n], o, c
        )

    def second_back(n):
        arrived(zbs[n], y1r.at[n])

        def pick(p):
            stage3[p, spans[n]] = zbs[n][inv_ref[lax.rem(z + GROUPS + NEAR - 1 - p, GROUPS)]]

        each(PARTS, pick)
        for p in others:
            z2_back(p, n).start()
        p = NEAR - 1
        pltpu.make_async_copy(
            stage3.at[p, spans[n]], fin.at[p // 2 * 2 + z % 2, spans[n]], y2r.at[n]
        ).start()

    near_come(0)

    @pl.when(i == 0)
    def _():
        rest_of_image()

    hand_round()

    arrived(ta, tar)
    arrived(tb, tbr)
    t = 32 * (i // 8) + lax.broadcasted_iota(jnp.int32, (32, 128), 0)
    tm[...] = jnp.where(t < vis, ta[...].astype(F32), tb[...].astype(F32)).astype(BF)
    txt_part = kvtxt.at[i % 8, half_of(i), :]

    def atx(k):
        return remote(tm, txt_part, ats.at[k], ktr, z, 2 * k + h)

    send_all(CHIPS, i, atx, lambda k: pltpu.make_async_copy(tm, txt_part, ktr))
    near_come(1)

    def step(n):
        @pl.when((n != 2) & (n < 4))
        def _():
            local_scores(n)

        @pl.when(n == 1)
        def _():
            near_come(2)
            near_come(3)

        @pl.when(n > 0)
        def _():
            prefix_grads(n - 1)

        @pl.when(n == 2)
        def _():
            local_scores(n)

    each(5, step)
    back_to_rows(1, jnp.dot(q_p[...], heads[...].reshape(256, 128), preferred_element_type=F32))
    send_all(CHIPS, i, rtxt, lambda k: pltpu.make_async_copy(dkvtxt.at[k % 8, half_of(k), :], rst.at[i], rtr))

    def near_back(e):
        return [
            remote(
                dkvloc.at[e, :, rows_of(s, 64), :], hb1.at[h, e], hrs.at[s, e], h1r, z, 2 * ahead(CHIPS - 1) + s
            )
            for s in (0, 1)
        ]

    def far_back(e):
        return remote(
            dkvloc.at[e, :, far_rows, :], hb2.at[h, e], hrs.at[2, e], h2r, z, 2 * ahead(CHIPS - 2) + 1
        )

    def own_back(e):
        return [
            remote(dkvloc.at[e, :, rows_of(1 - h, HALO), :], hb0.at[h, e], hrs.at[3, e], h0r, z, sib),
            remote(dq2.at[e, rows_of(1 - h, 0), :], gq.at[:, out_cols(e)], qrs.at[e], gqr, z, sib),
        ]

    def back_start(e):
        @pl.when(has_near)
        def _():
            for copy in near_back(e):
                copy.start()

        @pl.when(has_far)
        def _():
            far_back(e).start()

        for copy in own_back(e):
            copy.start()

    def back_left(e):
        @pl.when(has_near)
        def _():
            for copy in near_back(e):
                copy.wait_send()

        @pl.when(has_far)
        def _():
            far_back(e).wait_send()

        for copy in own_back(e):
            copy.wait_send()

    def out_cols(e):
        return pl.ds(pl.multiple_of(QW * h + 512 * e, 512), 512)

    def local_grads(e):
        k_rows = kvloc[e, 0]
        kt = k_rows.T
        kp[:VIS, :] = kvimg[e // 2, 2 * (e % 2)]
        kp[VIS:, :] = kvtxt[e]
        kpt = kp[...].T
        for k in range(4):
            n = 4 * e + k
            q_rows = q2[:, head_cols(e, k)]
            d_rows = d2[:, head_cols(e, k)]
            lanes = pl.ds(CHIP_ROWS * k, CHIP_ROWS)
            w = el[n] * stat[e, 0:1, lanes]
            s = (w * (dwl[n] - stat[e, 1:2, lanes])).astype(BF)
            part = jnp.dot(s, q_rows, preferred_element_type=F32)
            dkl[...] = part if k == 0 else dkl[...] + part
            part = jnp.dot(w.astype(BF), d_rows, preferred_element_type=F32)
            dvl[...] = part if k == 0 else dvl[...] + part
            dqt = jnp.dot(kt, s, preferred_element_type=F32) + jnp.dot(kpt, sp[e, :, lanes], preferred_element_type=F32)
            dq2[e, :, 128 * k : 128 * (k + 1)] = (dqt * scale).T.astype(BF)
        dkvloc[e, 0] = (dkl[...] * scale).astype(BF)
        dkvloc[e, 1] = dvl[...].astype(BF)
        back_start(e)
        pltpu.make_async_copy(dkvloc.at[e, :, rows_of(h, HALO), :], hb0.at[h, e], h0r).start()
        pltpu.make_async_copy(dq2.at[e, rows_of(h, 0), :], gq.at[:, out_cols(e)], gqr).start()

    txt_slot = dtx.at[h, i % 8, half_of(i), :]

    def reduce_prefix():
        arrived(rsi, rir)
        total = rsi[0].astype(F32)
        for k in range(1, CHIPS):
            total = total + rsi[k].astype(F32)
        total = total.astype(BF).reshape(128, 128)
        back_to_rows(0, jnp.dot(kv_pb[...], total, preferred_element_type=F32))
        arrived(rst, rtr)
        total = rst[0].astype(F32)
        for k in range(1, CHIPS):
            total = total + rst[k].astype(F32)
        tx[...] = total.astype(BF)
        for n, place in ((0, 0), (1, 2)):
            @pl.when(c != place)
            def _():
                remote(tx, txt_slot, xs.at[n], xr, z, place).start()

            @pl.when(c == place)
            def _():
                pltpu.make_async_copy(tx, txt_slot, xr).start()

    def rest(e):
        local_grads(e)

        @pl.when(e == RS_AT)
        def _():
            reduce_prefix()

    each(4, rest)

    second_back(1)

    for n in (0, 1):
        for p in others:
            z1(p, n).wait_send()
        sent_but(GROUPS, here, lambda g: z2(g, n))
    for place, buf, sem in ((0, ta, tar), (2, tb, tbr)):
        @pl.when(c == place)
        def _():
            sent_all(SHARDS, c, lambda k: remote(text_src(k), buf, txs.at[k], sem, z, k))

    for copy in swaps:
        copy.wait_send()

    def halo_left(e):
        own_in(e).wait_send()

        @pl.when(sends_near)
        def _():
            for copy in near_in(e):
                copy.wait_send()

        @pl.when(sends_far)
        def _():
            far_in(e).wait_send()

    each(4, halo_left)

    sent_all(CHIPS, i, atx)
    for half in (0, 1):
        sent_all(CHIPS, i, lambda k: aim(half, k))

    @pl.when(i == 0)
    def _():
        each(15, lambda k: dsend(k + 1).wait_send())

    @pl.when(c == 2)
    def _():
        for hh in (0, 1):
            dnear(hh).wait_send()

    second_back(0)

    def assemble(n, order):
        blocks = jnp.dot(order[...], fin[:, spans[n]].reshape(-1, 128), preferred_element_type=F32)
        begin, width = ((2 * QW, 4 * KW), (0, 2 * QW))[n]
        for k in range(width // 128):
            io[:, begin + 128 * k : begin + 128 * (k + 1)] = blocks[8 * k : 8 * (k + 1)].astype(BF)
        span = pl.ds(begin, width)
        copy = pltpu.make_async_copy(io.at[:, span], gimg.at[:, span], ims.at[n])
        copy.start()
        return copy

    arrived(fin.at[:, spans[1]], y2r.at[1])
    first = assemble(1, to_q)

    for half in (0, 1):
        sent_all(CHIPS, i, lambda k: rimg(half, k))
    sent_all(CHIPS, i, rtxt)
    for n in (0, 1):
        sent_but(16, here_back, lambda t: z1_back(t, n))
    for n, place in ((0, 0), (1, 2)):
        @pl.when(c != place)
        def _():
            remote(tx, txt_slot, xs.at[n], xr, z, place).wait_send()

    arrived(hb0, h0r)
    @pl.when(sends_near)
    def _():
        arrived(hb1, h1r)

    gives_far = (h == 1) & (i >= 1) & (i < CHIPS - 2)

    @pl.when(gives_far)
    def _():
        arrived(hb2, h2r)

    for hh in (0, 1):
        for e in range(4):
            for n in (0, 1):
                w = pl.ds(KW * hh + 128 * e, 128)
                near = hb0[hh, e, n].astype(F32) + jnp.where(sends_near, hb1[hh, e, n].astype(F32), 0.0)
                kvo[n, :64, w] = near[:64].astype(BF)
                more = jnp.where(gives_far, hb2[hh, e, n].astype(F32), 0.0)
                kvo[n, 64:, w] = (near[64:] + more).astype(BF)

    t64 = lax.broadcasted_iota(jnp.int32, (PROMPT, 128), 0)
    for place in (0, 2):
        @pl.when(c == place)
        def _():
            arrived(dtx, xr)
            keep = t64 < vis if place == 0 else t64 >= vis
            for hh in (0, 1):
                for b in range(8):
                    kvo[b // 4, :64, pl.ds(KW * hh + 128 * (b % 4), 128)] = jnp.where(
                        keep, dtx[hh, b].astype(F32), 0.0
                    ).astype(BF)

    out = pltpu.make_async_copy(kvo, gkv, lcr)
    out.start()
    each(4, back_left)
    arrived(gq, gqr)
    out.wait()
    arrived(fin.at[:, spans[0]], y2r.at[0])
    last = assemble(0, to_kv)
    for n in (0, 1):
        for p in others:
            z2_back(p, n).wait_send()
    first.wait()
    last.wait()


ANY = pl.BlockSpec(memory_space=pl.ANY)
SMEM = pl.BlockSpec(memory_space=pltpu.SMEM)
DMA = pltpu.SemaphoreType.DMA


def sds(*shape):
    return jax.ShapeDtypeStruct(shape, BF)


def vm(*shape, dtype=BF):
    return pltpu.VMEM(shape, dtype)


def per_device(queries, keys_values, image_rows, cotangent, seq_image, vis_start, comp_lengths):
    gq, gkv, gimg = pl.pallas_call(
        kernel,
        out_shape=[sds(ROWS, 2 * QW), sds(2, ROWS, 2 * KW), sds(8, 2 * QW + 4 * KW)],
        in_specs=[SMEM] * 3 + [ANY] * 4,
        out_specs=[ANY] * 3,
        scratch_shapes=[
            pltpu.SMEM((16,), jnp.int32),
            vm(8, 48, 128), vm(8, 16, 128), vm(8, 32, 128), vm(16, 48, 128), vm(16, 16, 128), vm(16, 32, 128),
            vm(2, 4, 16, 128), vm(16, 16, 128),
            vm(32, 128), vm(32, 128), vm(32, 128), vm(VIS, QW), vm(64, QW), vm(128, 128), vm(256, 256),
            vm(128, 128), vm(128, 128), vm(256, 256),
            vm(CHIP_ROWS, QW), vm(CHIP_ROWS, QW), vm(4, 2, LOCAL, 128), vm(2, 4, VIS, 128), vm(8, PROMPT, 128),
            vm(16, QW),
            vm(KEYS, CHIP_ROWS, dtype=F32), vm(PREFIX, 64, dtype=F32), vm(1, CHIP_ROWS, dtype=F32),
            vm(16, LOCAL, CHIP_ROWS, dtype=F32), vm(16, LOCAL, CHIP_ROWS, dtype=F32),
            vm(4, 8, 4 * CHIP_ROWS, dtype=F32), vm(4, PREFIX, 4 * CHIP_ROWS),
            vm(PREFIX, 128), vm(PREFIX, 128), vm(LOCAL, 128, dtype=F32), vm(LOCAL, 128, dtype=F32),
            vm(4, CHIP_ROWS, 512), vm(4, 2, LOCAL, 128), vm(2, 4, VIS, 128), vm(8, PROMPT, 128), vm(16, 16, 128),
            vm(16, 2, 4, 16, 128), vm(16, 32, 128), vm(2, 4, 2, ROWS, 128), vm(2, 4, 2, ROWS, 128),
            vm(2, 4, 2, 64, 128), vm(2, 8, 64, 128), vm(8, 48, 128), vm(16, 16, 128), vm(16, 32, 128),
            vm(16, 48, 128), vm(8, 48, 128), vm(8, 48, 128), vm(32, 128), vm(2, ROWS, 2 * KW), vm(8, 2 * QW + 4 * KW),
            DMA((2, 8)), DMA((2, 16)), DMA((32,)), DMA((2,)), DMA((4, 4)), DMA((2, 16)), DMA((16,)), DMA((16,)), DMA((2,)),
            DMA((2, 16)), DMA((16,)), DMA((4, 4)), DMA((4,)), DMA((2,)), DMA((2, 16)), DMA((2, 8)),
            DMA((2,)),
            DMA((2,)), DMA((2,)), DMA((2,)), DMA((2,)), DMA((2,)), DMA((4,)), DMA((4,)),
        ] + [DMA(())] * 15 + [pltpu.SemaphoreType.REGULAR],
        compiler_params=pltpu.CompilerParams(
            collective_id=0, has_side_effects=True, vmem_limit_bytes=LIMIT * 2**20
        ),
        name="grads",
    )(
        seq_image, vis_start, comp_lengths,
        *(pltpu.with_memory_space_constraint(x[0], pltpu.HBM) for x in (queries, cotangent, keys_values, image_rows)),
    )
    return (gq[None], gkv[None], gimg[None])


def solution(mesh):
    placed = (
        P("rollout", "ctx", None),
        P("rollout", None, "ctx", None),
        P("rollout", "ctx", None),
        P("rollout", "ctx", None),
        P(),
        P("rollout"),
        P("rollout", None),
    )
    return jax.shard_map(
        per_device,
        mesh=mesh,
        in_specs=placed,
        out_specs=(
            P("rollout", "ctx", None),
            P("rollout", None, "ctx", None),
            P("rollout", "ctx", None),
        ),
        check_vma=False,
    )
```

```python
import functools
import math

import jax
import jax.numpy as jnp
from jax import lax
from jax.experimental import pallas as pl
from jax.experimental.pallas import tpu as pltpu
from jax.sharding import PartitionSpec as P

HEADS = 32
KV_HEADS = 8
HEAD_DIM = 128
VIS = 256
PROMPT = 64
PREFIX = VIS + PROMPT
GROUPS = 16
SHARDS = 32
CHIPS = 16
ROWS = 128
CHIP_ROWS = 256
HALO = 320
LOCAL = HALO + CHIP_ROWS
KEYS = PREFIX + LOCAL
QW = HEADS * HEAD_DIM // 2
KW = KV_HEADS * HEAD_DIM // 2
MESH = pl.DeviceIdType.MESH
BF = jnp.bfloat16
F32 = jnp.float32
NEG = -1e30
NEAR = 4
PARTS = 2 * NEAR
LIMIT = 40
RS_AT = 2


def remote(src, dst, send, recv, z, c):
    return pltpu.make_async_remote_copy(
        src_ref=src, dst_ref=dst, send_sem=send, recv_sem=recv, device_id=(z, c), device_id_type=MESH
    )


def arrived(ref, sem):
    pltpu.make_async_copy(ref, ref, sem).wait()


def each(count, body):
    def step(k, carry):
        body(k)
        return carry

    lax.fori_loop(0, count, step, 0)


def send_all(count, me, copy, local):
    each(count - 1, lambda k: copy(lax.rem(me + 1 + k, count)).start())
    local(me).start()


def sent_all(count, me, copy):
    each(count - 1, lambda k: copy(lax.rem(me + 1 + k, count)).wait_send())


def send_but(count, me, copy, local):
    def body(k):
        @pl.when(k != me)
        def _():
            copy(k).start()

        @pl.when(k == me)
        def _():
            local(k).start()

    each(count, body)


def sent_but(count, me, copy):
    def body(k):
        @pl.when(k != me)
        def _():
            copy(k).wait_send()

    each(count, body)


def greet(z, c):
    barrier = pltpu.get_barrier_semaphore()
    i = c // 2

    def column(k):
        for to in (lax.rem(z + 1 + k, GROUPS), lax.rem(z + GROUPS - 1 - k, GROUPS)):
            for core in (0, 1):
                pl.semaphore_signal(barrier, inc=1, device_id=(to, 2 * i + core), device_id_type=MESH)

    def plane(k):
        pl.semaphore_signal(
            barrier, inc=1, device_id=(z, lax.rem(c + 1 + k, SHARDS)), device_id_type=MESH
        )

    each(NEAR, column)
    each(SHARDS - 1, plane)


def greeted():
    pl.semaphore_wait(pltpu.get_barrier_semaphore(), SHARDS - 1 + 4 * NEAR)


def one_hot(rows, cols, source):
    o = lax.broadcasted_iota(jnp.int32, (rows, cols), 0)
    n = lax.broadcasted_iota(jnp.int32, (rows, cols), 1)
    return jnp.where(n == source(o), 1.0, 0.0).astype(BF)


def piece_rows():
    shape = (8, 48, 384)
    piece = lax.broadcasted_iota(jnp.int32, shape, 0)
    y = lax.broadcasted_iota(jnp.int32, shape, 1)
    n = lax.broadcasted_iota(jnp.int32, shape, 2)
    half = piece % 2
    of_kv = y < 16
    y = jnp.where(of_kv, y, y - 16)
    row = 2 * (piece // 2) + jnp.where(of_kv, y // 8, y // 16)
    block = jnp.where(of_kv, 32 + 8 * ((y // 4) % 2) + 4 * half + y % 4, 16 * half + y % 16)
    return jnp.where(n == 8 * block + row, 1.0, 0.0)


def kv_order(o):
    y = o // 16
    return (o % 16) * 8 + 4 * (y % 2) + 2 * (y // 4) + (y // 2) % 2


def kv_order_back(o):
    x = o % 8
    return ((x % 4) // 2 * 4 + x % 2 * 2 + x // 4) * 16 + o // 8


def q_order(o):
    return (o % 16) * 16 + o // 16


def kernel(
    seq_ref, vis_ref, len_ref, q, d, kv, img,
    gq, gkv, gimg,
    inv_ref, pieces, z1k, z1q, stage, z2k, z2q, kvp, qi, ta, tb, tm, ds, dnext, to_kv, to_q, kv_p, kv_pb, q_p,
    q2, d2, kvloc, kvimg, kvtxt, imgd,
    bias, ibias, valid, el, dwl, stat, sp, kp, vp, dkl, dvl,
    dq2, dkvloc, dkvimg, dkvtxt, heads,
    rsi, rst, hb0, hb1, hb2, dtx, rows, zbk, zbq, stage2, stage3, fin, tx, kvo, io,
    z1s, z2s, txs, sws, has, ags, ats, dss, dns, ris, rts, hrs, qrs, xs, y1s, y2s, ims,
    z1r, z2r, kir, y1r, y2r, klr, kfr,
    tar, tbr, q2r, d2r, ktr, d0r, dnr, rir, rtr, h0r, h1r, h2r, gqr, xr, lcr, far_sem,
):
    z = lax.axis_index("rollout")
    c = lax.axis_index("ctx")
    i = c // 2
    h = c % 2
    sib = 2 * i + 1 - h
    scale = 1.0 / math.sqrt(HEAD_DIM)
    to_log2 = scale * math.log2(math.e)
    vis = vis_ref[0]
    nt = (((1,), (1,)), ((), ()))
    load = pltpu.make_async_copy(img, io, lcr)
    load.start()
    greet(z, c)

    in_pieces = piece_rows()
    load.wait()
    blocks = jnp.concatenate([io[:, 128 * k : 128 * (k + 1)].astype(F32) for k in range(48)], axis=0).astype(BF)
    pieces[...] = jnp.dot(in_pieces.astype(BF).reshape(384, 384), blocks, preferred_element_type=F32).astype(BF).reshape(8, 48, 128)
    greeted()
    for to in (lax.rem(z + NEAR, GROUPS), lax.rem(z + GROUPS - NEAR, GROUPS)):
        for core in (0, 1):
            pl.semaphore_signal(far_sem, inc=1, device_id=(to, 2 * i + core), device_id_type=MESH)

    spans = (pl.ds(0, 16), pl.ds(16, 32))
    z1b, z2b, zbs = (z1k, z1q), (z2k, z2q), (zbk, zbq)

    def z1(p, n):
        j = lax.rem(z + GROUPS + 1 - NEAR + p, GROUPS)
        return remote(pieces.at[p // 2 * 2 + j % 2, spans[n]], z1b[n].at[p], z1s.at[n, p], z1r.at[n], j, c)

    def z1_here(n):
        p = NEAR - 1
        return pltpu.make_async_copy(
            pieces.at[p // 2 * 2 + z % 2, spans[n]], z1b[n].at[p], z1r.at[n]
        )

    others = [p for p in range(PARTS) if p != NEAR - 1]
    for n in (0, 1):
        for p in others:
            z1(p, n).start()
        z1_here(n).start()

    def text_src(k):
        ii, hh = k // 2, k % 2
        b = ii % 8
        return kv.at[
            b // 4,
            pl.ds(pl.multiple_of(32 * (ii // 8), 32), 32),
            pl.ds(pl.multiple_of(KW * hh + 128 * (b % 4), 128), 128),
        ]

    for place, buf, sem in ((0, ta, tar), (2, tb, tbr)):
        @pl.when(c == place)
        def _():
            send_all(
                SHARDS, c,
                lambda k: remote(text_src(k), buf, txs.at[k], sem, z, k),
                lambda k: pltpu.make_async_copy(text_src(k), buf, sem),
            )

    def cols(core, width):
        return pl.ds(pl.multiple_of(width * core, width), width)

    def rows_of(core, first):
        return pl.ds(pl.multiple_of(first + ROWS * core, 64), ROWS)

    def block(k):
        return pl.ds(pl.multiple_of(16 * k, 16), 16)

    def half_of(k):
        return pl.ds(pl.multiple_of(32 * (k // 8), 32), 32)

    def ahead(n):
        return lax.rem(i + n, CHIPS)

    my_rows = rows_of(h, 0)
    own_rows = rows_of(h, HALO)
    near_rows = rows_of(h, 64)

    def kv_cols(core, e):
        return pl.ds(pl.multiple_of(KW * core + 128 * e, 128), 128)

    sends_near = (i >= 1) & (i < CHIPS - 1)
    sends_far = (i >= 2) & (i < CHIPS - 1)
    has_near = i >= 2
    has_far = i >= 3
    far_rows = pl.ds(0, 64)

    def own_in(e):
        return remote(
            kv.at[:, :, kv_cols(1 - h, e)], kvloc.at[e, :, own_rows, :], has.at[2, e], klr.at[e], z, sib
        )

    def near_in(e):
        return [
            remote(
                kv.at[:, :, kv_cols(hh, e)], kvloc.at[e, :, near_rows, :], has.at[hh, e], klr.at[e], z,
                2 * ahead(1) + hh,
            )
            for hh in (0, 1)
        ]

    def far_in(e):
        return remote(
            kvloc.at[e, :, pl.ds(HALO - 64, 64), :], kvloc.at[e, :, far_rows, :], has.at[3, e], kfr.at[e], z,
            2 * ahead(1) + h,
        )

    def halo_start(e):
        @pl.when(sends_near)
        def _():
            for copy in near_in(e):
                copy.start()

        own_in(e).start()
        pltpu.make_async_copy(kv.at[:, :, kv_cols(h, e)], kvloc.at[e, :, own_rows, :], klr.at[e]).start()

    def near_come(e):
        @pl.when(has_near)
        def _():
            arrived(kvloc.at[e, :, pl.ds(64, LOCAL - 64), :], klr.at[e])

        @pl.when(i < 2)
        def _():
            arrived(kvloc.at[e, :, pl.ds(HALO, CHIP_ROWS), :], klr.at[e])
            kvloc[e, :, 64:HALO, :] = jnp.zeros((2, HALO - 64, 128), BF)

        @pl.when(sends_far)
        def _():
            far_in(e).start()

    def far_come(e):
        @pl.when(has_far)
        def _():
            arrived(kvloc.at[e, :, far_rows, :], kfr.at[e])

        @pl.when(i < 3)
        def _():
            kvloc[e, :, 0:64, :] = jnp.zeros((2, 64, 128), BF)

    swaps = [
        remote(d.at[:, cols(1 - h, QW)], d2.at[my_rows, :], sws.at[0], d2r, z, sib),
        remote(q.at[:, cols(1 - h, QW)], q2.at[my_rows, :], sws.at[1], q2r, z, sib),
    ]
    halo_start(0)
    for copy in swaps:
        copy.start()
    pltpu.make_async_copy(d.at[:, cols(h, QW)], d2.at[my_rows, :], d2r).start()
    pltpu.make_async_copy(q.at[:, cols(h, QW)], q2.at[my_rows, :], q2r).start()
    halo_start(1)

    def dnear(hh):
        return remote(d.at[pl.ds(0, 64), pl.ds(QW * hh, QW)], dnext, dns.at[hh], dnr, z, hh)

    def dsend(k):
        return remote(ds.at[block(k), :], imgd, dss.at[k], d0r, z, 2 * k + h)

    @pl.when(c == 2)
    def _():
        for hh in (0, 1):
            dnear(hh).start()

    def rest_of_image():
        arrived(dnext, dnr)
        shift = one_hot(64, CHIP_ROWS, lambda r: r + 192 + vis)
        more = one_hot(64, 64, lambda r: r + 192 + vis - CHIP_ROWS)
        for part in range(4):
            w = pl.ds(part * 512, 512)
            rows_d = jnp.dot(shift, d2[:, w], preferred_element_type=F32)
            rows_d = rows_d + jnp.dot(more, dnext[:, w], preferred_element_type=F32)
            ds[192:, w] = rows_d.astype(BF)
        each(4, lambda k: dsend(k + 12).start())

    to_kv[...] = in_pieces[:, :16, 256:].astype(BF).reshape(128, 128).T
    to_q[...] = in_pieces[:, 16:, :256].astype(BF).reshape(256, 256).T
    kv_p[...] = one_hot(128, 128, kv_order)
    kv_pb[...] = one_hot(128, 128, kv_order_back)
    q_p[...] = one_hot(256, 256, q_order)
    for o in range(GROUPS):
        user = jnp.int32(0)
        for g in range(GROUPS):
            user = jnp.where(seq_ref[g] == o, g, user)
        inv_ref[o] = user

    def slot_positions(lanes):
        r = lax.broadcasted_iota(jnp.int32, (PREFIX, lanes), 0)
        text = r - VIS
        return jnp.where(r < VIS, vis + r, jnp.where(text < vis, text, r))

    pos = CHIP_ROWS * i + lax.broadcasted_iota(jnp.int32, (1, CHIP_ROWS), 1)
    begin = jnp.full((1, CHIP_ROWS), PREFIX, jnp.int32)
    edge = jnp.int32(PREFIX)
    for k in range(16):
        edge = edge + len_ref[0, k]
        begin = jnp.where(pos >= edge, edge, begin)
    begin = jnp.where(pos < PREFIX, pos + 1, begin)
    valid[...] = jnp.where((pos >= vis) & (pos < vis + VIS), 0.0, 1.0)
    bias[:PREFIX, :] = jnp.where(slot_positions(CHIP_ROWS) <= pos, 0.0, NEG)
    at = CHIP_ROWS * i - HALO + lax.broadcasted_iota(jnp.int32, (LOCAL, CHIP_ROWS), 0)
    bias[PREFIX:, :] = jnp.where((at >= begin) & (at <= pos), 0.0, NEG)
    ipos = vis + 16 * i + lax.broadcasted_iota(jnp.int32, (1, 64), 1) % 16
    ibias[...] = jnp.where(slot_positions(64) <= ipos, 0.0, NEG)

    to_core = z % 2
    slot = 8 * h + z // 2
    here = jnp.where(to_core == h, z, GROUPS)
    here_back = jnp.where(to_core == h, slot, GROUPS)

    def part_of(o, j):
        return jnp.minimum((j - o + NEAR - 1) & (GROUPS - 1), PARTS - 1)

    def z2(g, n):
        return remote(
            stage.at[g, spans[n]], z2b[n].at[slot], z2s.at[n, g], z2r.at[n], g, 2 * i + to_core
        )

    def z2_here(g, n):
        return pltpu.make_async_copy(stage.at[g, spans[n]], z2b[n].at[slot], z2r.at[n])

    for n in (0, 1):
        arrived(z1b[n], z1r.at[n])

        def pick(g):
            stage[g, spans[n]] = z1b[n][part_of(seq_ref[g], z)]

        each(GROUPS, pick)
        if n == 0:
            pl.semaphore_wait(far_sem, 4)
        send_but(GROUPS, here, lambda g: z2(g, n), lambda g: z2_here(g, n))

    @pl.when(i == 0)
    def _():
        arrived(d2, d2r)
        shift = one_hot(192, CHIP_ROWS, lambda r: r + vis)
        for part in range(4):
            w = pl.ds(part * 512, 512)
            ds[:192, w] = jnp.dot(shift, d2[:, w], preferred_element_type=F32).astype(BF)
        pltpu.make_async_copy(ds.at[block(0), :], imgd, d0r).start()
        each(11, lambda k: dsend(k + 1).start())

    halo_start(2)
    halo_start(3)

    image = seq_ref[z]

    def slot_of(s, rp):
        even = (image + 1 - NEAR + 2 * rp) & (GROUPS - 1)
        j = jnp.where((even & 1) == h, even, (even + 1) & (GROUPS - 1))
        return 8 * s + j // 2

    def come(n):
        return jnp.concatenate([z2b[n][slot_of(s, rp)] for s in (0, 1) for rp in range(4)], axis=0)

    def aim(half, k):
        return remote(kvp.at[half], kvimg.at[half, :, block(i), :], ags.at[half, k], kir.at[half], z, 2 * k + h)

    def hand_round():
        arrived(z2b[0], z2r.at[0])
        kvp[...] = jnp.dot(kv_p[...], come(0), preferred_element_type=F32).astype(BF).reshape(2, 4, 16, 128)

        for half in (0, 1):
            send_all(
                CHIPS, i, lambda k: aim(half, k),
                lambda k: pltpu.make_async_copy(kvp.at[half], kvimg.at[half, :, block(i), :], kir.at[half]),
            )

    arrived(q2, q2r)

    @pl.when(i > 0)
    def _():
        arrived(d2, d2r)


    def head_cols(e, k):
        return pl.ds(pl.multiple_of(512 * e + 128 * k, 128), 128)

    def local_scores(e):
        far_come(e)
        k_rows = kvloc[e, 0]
        v_rows = kvloc[e, 1]
        for k in range(4):
            w128 = head_cols(e, k)
            n = 4 * e + k
            top = lax.dot_general(k_rows, q2[:, w128], nt, preferred_element_type=F32) * to_log2 + bias[PREFIX:, :]
            peak = jnp.max(top, axis=0, keepdims=True)
            ex = jnp.exp2(top - peak)
            dw = lax.dot_general(v_rows, d2[:, w128], nt, preferred_element_type=F32)
            el[n] = ex
            dwl[n] = dw
            lanes = pl.ds(CHIP_ROWS * k, CHIP_ROWS)
            stat[e, 0:1, lanes] = peak
            stat[e, 1:2, lanes] = jnp.sum(ex, axis=0, keepdims=True)
            stat[e, 2:3, lanes] = jnp.sum(ex * dw, axis=0, keepdims=True)

    def prefix_come():
        arrived(z2b[1], z2r.at[1])
        qi[...] = jnp.dot(q_p[...], come(1), preferred_element_type=F32).astype(BF).reshape(16, 16, 128)
        arrived(kvtxt, ktr)
        arrived(imgd, d0r)

    def rimg(half, k):
        return remote(dkvimg.at[half, :, block(k), :], rsi.at[i, half], ris.at[half, k], rir, z, 2 * k + h)

    def rtxt(k):
        return remote(dkvtxt.at[k % 8, half_of(k), :], rst.at[i], rts.at[k], rtr, z, 2 * k + h)

    def four(x):
        return jnp.concatenate([x] * 4, axis=1)

    def prefix_grads(e):
        place = 2 * (e % 2)

        @pl.when(e == 0)
        def _():
            prefix_come()

        @pl.when(e % 2 == 0)
        def _():
            arrived(kvimg.at[e // 2], kir.at[e // 2])

        kp[:VIS, :] = kvimg[e // 2, place]
        kp[VIS:, :] = kvtxt[e]
        vp[:VIS, :] = kvimg[e // 2, place + 1]
        vp[VIS:, :] = kvtxt[4 + e]
        k_rows = kp[...]
        v_rows = vp[...]

        def scores(q_rows, d_rows, mask):
            top = lax.dot_general(k_rows, q_rows, nt, preferred_element_type=F32) * to_log2 + mask
            dw = lax.dot_general(v_rows, d_rows, nt, preferred_element_type=F32)
            return top, jnp.max(top, axis=0, keepdims=True), dw

        q_rows = qi[pl.ds(4 * e, 4)].reshape(64, 128)
        wide = pl.ds(pl.multiple_of(512 * e, 512), 512)
        d_rows = imgd[:, wide]
        d_rows = jnp.concatenate([d_rows[:, 128 * k : 128 * (k + 1)] for k in range(4)], axis=0)
        top, peak, dw = scores(q_rows, d_rows, ibias[...])
        ex = jnp.exp2(top - peak)
        inv = 1.0 / jnp.sum(ex, axis=0, keepdims=True)
        delta = jnp.sum(ex * dw, axis=0, keepdims=True) * inv
        w = ex * inv
        s = (w * (dw - delta)).astype(BF)
        dk = jnp.dot(s, q_rows, preferred_element_type=F32)
        dv = jnp.dot(w.astype(BF), d_rows, preferred_element_type=F32)
        dqi = lax.dot_general(s, k_rows, (((0,), (0,)), ((), ())), preferred_element_type=F32) * scale
        heads[pl.ds(4 * e, 4)] = dqi.astype(BF).reshape(4, 16, 128)

        q_rows = jnp.concatenate([q2[:, head_cols(e, k)] for k in range(4)], axis=0)
        d_rows = jnp.concatenate([d2[:, head_cols(e, k)] for k in range(4)], axis=0)
        top, peak, dw = scores(q_rows, d_rows, four(bias[:PREFIX, :]))
        low = stat[e, 0:1, :]
        peak = jnp.maximum(peak, low)
        ex = jnp.exp2(top - peak)
        shrink = jnp.exp2(low - peak)
        inv = 1.0 / (jnp.sum(ex, axis=0, keepdims=True) + stat[e, 1:2, :] * shrink)
        delta = (jnp.sum(ex * dw, axis=0, keepdims=True) + stat[e, 2:3, :] * shrink) * inv
        inv = inv * four(valid[...])
        w = ex * inv
        s = (w * (dw - delta)).astype(BF)
        dk = dk + jnp.dot(s, q_rows, preferred_element_type=F32)
        dv = dv + jnp.dot(w.astype(BF), d_rows, preferred_element_type=F32)
        sp[e] = s
        stat[e, 0:1, :] = shrink * inv
        stat[e, 1:2, :] = delta
        dk = (dk * scale).astype(BF)
        dv = dv.astype(BF)
        dkvimg[e // 2, place] = dk[:VIS]
        dkvimg[e // 2, place + 1] = dv[:VIS]
        dkvtxt[e] = dk[VIS:]
        dkvtxt[4 + e] = dv[VIS:]

        @pl.when(e % 2 == 1)
        def _():
            half = e // 2
            send_all(
                CHIPS, i,
                lambda k: rimg(half, k),
                lambda k: pltpu.make_async_copy(dkvimg.at[half, :, block(k), :], rsi.at[i, half], rir),
            )

    def z1_back(t, n):
        return remote(
            stage2.at[t, spans[n]], zbs[n].at[z], y1s.at[n, t], y1r.at[n], 2 * (t % 8) + h, 2 * i + t // 8
        )

    def back_to_rows(n, value):
        rows[:, spans[n]] = value.astype(BF).reshape(8, 16 * (n + 1), 128)

        def pick(t):
            stage2[t, spans[n]] = rows[4 * (t // 8) + part_of(image, 2 * (t % 8) + h) // 2, spans[n]]

        each(16, pick)
        send_but(
            16, here_back, lambda t: z1_back(t, n),
            lambda t: pltpu.make_async_copy(stage2.at[t, spans[n]], zbs[n].at[z], y1r.at[n]),
        )

    def z2_back(p, n):
        o = lax.rem(z + GROUPS + NEAR - 1 - p, GROUPS)
        return remote(
            stage3.at[p, spans[n]], fin.at[p // 2 * 2 + z % 2, spans[n]], y2s.at[n, p], y2r.at[n], o, c
        )

    def second_back(n):
        arrived(zbs[n], y1r.at[n])

        def pick(p):
            stage3[p, spans[n]] = zbs[n][inv_ref[lax.rem(z + GROUPS + NEAR - 1 - p, GROUPS)]]

        each(PARTS, pick)
        for p in others:
            z2_back(p, n).start()
        p = NEAR - 1
        pltpu.make_async_copy(
            stage3.at[p, spans[n]], fin.at[p // 2 * 2 + z % 2, spans[n]], y2r.at[n]
        ).start()

    near_come(0)

    @pl.when(i == 0)
    def _():
        rest_of_image()

    hand_round()

    arrived(ta, tar)
    arrived(tb, tbr)
    t = 32 * (i // 8) + lax.broadcasted_iota(jnp.int32, (32, 128), 0)
    tm[...] = jnp.where(t < vis, ta[...].astype(F32), tb[...].astype(F32)).astype(BF)
    txt_part = kvtxt.at[i % 8, half_of(i), :]

    def atx(k):
        return remote(tm, txt_part, ats.at[k], ktr, z, 2 * k + h)

    send_all(CHIPS, i, atx, lambda k: pltpu.make_async_copy(tm, txt_part, ktr))
    near_come(1)

    def step(n):
        @pl.when((n != 2) & (n < 4))
        def _():
            local_scores(n)

        @pl.when(n == 1)
        def _():
            near_come(2)
            near_come(3)

        @pl.when(n > 0)
        def _():
            prefix_grads(n - 1)

        @pl.when(n == 2)
        def _():
            local_scores(n)

    each(5, step)
    back_to_rows(1, jnp.dot(q_p[...], heads[...].reshape(256, 128), preferred_element_type=F32))
    send_all(CHIPS, i, rtxt, lambda k: pltpu.make_async_copy(dkvtxt.at[k % 8, half_of(k), :], rst.at[i], rtr))

    def near_back(e):
        return [
            remote(
                dkvloc.at[e, :, rows_of(s, 64), :], hb1.at[h, e], hrs.at[s, e], h1r, z, 2 * ahead(CHIPS - 1) + s
            )
            for s in (0, 1)
        ]

    def far_back(e):
        return remote(
            dkvloc.at[e, :, far_rows, :], hb2.at[h, e], hrs.at[2, e], h2r, z, 2 * ahead(CHIPS - 2) + 1
        )

    def own_back(e):
        return [
            remote(dkvloc.at[e, :, rows_of(1 - h, HALO), :], hb0.at[h, e], hrs.at[3, e], h0r, z, sib),
            remote(dq2.at[e, rows_of(1 - h, 0), :], gq.at[:, out_cols(e)], qrs.at[e], gqr, z, sib),
        ]

    def back_start(e):
        @pl.when(has_near)
        def _():
            for copy in near_back(e):
                copy.start()

        @pl.when(has_far)
        def _():
            far_back(e).start()

        for copy in own_back(e):
            copy.start()

    def back_left(e):
        @pl.when(has_near)
        def _():
            for copy in near_back(e):
                copy.wait_send()

        @pl.when(has_far)
        def _():
            far_back(e).wait_send()

        for copy in own_back(e):
            copy.wait_send()

    def out_cols(e):
        return pl.ds(pl.multiple_of(QW * h + 512 * e, 512), 512)

    def local_grads(e):
        k_rows = kvloc[e, 0]
        kt = k_rows.T
        kp[:VIS, :] = kvimg[e // 2, 2 * (e % 2)]
        kp[VIS:, :] = kvtxt[e]
        kpt = kp[...].T
        for k in range(4):
            n = 4 * e + k
            q_rows = q2[:, head_cols(e, k)]
            d_rows = d2[:, head_cols(e, k)]
            lanes = pl.ds(CHIP_ROWS * k, CHIP_ROWS)
            w = el[n] * stat[e, 0:1, lanes]
            s = (w * (dwl[n] - stat[e, 1:2, lanes])).astype(BF)
            part = jnp.dot(s, q_rows, preferred_element_type=F32)
            dkl[...] = part if k == 0 else dkl[...] + part
            part = jnp.dot(w.astype(BF), d_rows, preferred_element_type=F32)
            dvl[...] = part if k == 0 else dvl[...] + part
            dqt = jnp.dot(kt, s, preferred_element_type=F32) + jnp.dot(kpt, sp[e, :, lanes], preferred_element_type=F32)
            dq2[e, :, 128 * k : 128 * (k + 1)] = (dqt * scale).T.astype(BF)
        dkvloc[e, 0] = (dkl[...] * scale).astype(BF)
        dkvloc[e, 1] = dvl[...].astype(BF)
        back_start(e)
        pltpu.make_async_copy(dkvloc.at[e, :, rows_of(h, HALO), :], hb0.at[h, e], h0r).start()
        pltpu.make_async_copy(dq2.at[e, rows_of(h, 0), :], gq.at[:, out_cols(e)], gqr).start()

    txt_slot = dtx.at[h, i % 8, half_of(i), :]

    def reduce_prefix():
        arrived(rsi, rir)
        total = rsi[0].astype(F32)
        for k in range(1, CHIPS):
            total = total + rsi[k].astype(F32)
        total = total.astype(BF).reshape(128, 128)
        back_to_rows(0, jnp.dot(kv_pb[...], total, preferred_element_type=F32))
        arrived(rst, rtr)
        total = rst[0].astype(F32)
        for k in range(1, CHIPS):
            total = total + rst[k].astype(F32)
        tx[...] = total.astype(BF)
        for n, place in ((0, 0), (1, 2)):
            @pl.when(c != place)
            def _():
                remote(tx, txt_slot, xs.at[n], xr, z, place).start()

            @pl.when(c == place)
            def _():
                pltpu.make_async_copy(tx, txt_slot, xr).start()

    def rest(e):
        local_grads(e)

        @pl.when(e == RS_AT)
        def _():
            reduce_prefix()

    each(4, rest)

    second_back(1)

    for n in (0, 1):
        for p in others:
            z1(p, n).wait_send()
        sent_but(GROUPS, here, lambda g: z2(g, n))
    for place, buf, sem in ((0, ta, tar), (2, tb, tbr)):
        @pl.when(c == place)
        def _():
            sent_all(SHARDS, c, lambda k: remote(text_src(k), buf, txs.at[k], sem, z, k))

    for copy in swaps:
        copy.wait_send()

    def halo_left(e):
        own_in(e).wait_send()

        @pl.when(sends_near)
        def _():
            for copy in near_in(e):
                copy.wait_send()

        @pl.when(sends_far)
        def _():
            far_in(e).wait_send()

    each(4, halo_left)

    sent_all(CHIPS, i, atx)
    for half in (0, 1):
        sent_all(CHIPS, i, lambda k: aim(half, k))

    @pl.when(i == 0)
    def _():
        each(15, lambda k: dsend(k + 1).wait_send())

    @pl.when(c == 2)
    def _():
        for hh in (0, 1):
            dnear(hh).wait_send()

    second_back(0)

    def assemble(n, order):
        blocks = jnp.dot(order[...], fin[:, spans[n]].reshape(-1, 128), preferred_element_type=F32)
        begin, width = ((2 * QW, 4 * KW), (0, 2 * QW))[n]
        for k in range(width // 128):
            io[:, begin + 128 * k : begin + 128 * (k + 1)] = blocks[8 * k : 8 * (k + 1)].astype(BF)
        span = pl.ds(begin, width)
        copy = pltpu.make_async_copy(io.at[:, span], gimg.at[:, span], ims.at[n])
        copy.start()
        return copy

    arrived(fin.at[:, spans[1]], y2r.at[1])
    first = assemble(1, to_q)

    for half in (0, 1):
        sent_all(CHIPS, i, lambda k: rimg(half, k))
    sent_all(CHIPS, i, rtxt)
    for n in (0, 1):
        sent_but(16, here_back, lambda t: z1_back(t, n))
    for n, place in ((0, 0), (1, 2)):
        @pl.when(c != place)
        def _():
            remote(tx, txt_slot, xs.at[n], xr, z, place).wait_send()

    arrived(hb0, h0r)
    @pl.when(sends_near)
    def _():
        arrived(hb1, h1r)

    gives_far = (h == 1) & (i >= 1) & (i < CHIPS - 2)

    @pl.when(gives_far)
    def _():
        arrived(hb2, h2r)

    for hh in (0, 1):
        for e in range(4):
            for n in (0, 1):
                w = pl.ds(KW * hh + 128 * e, 128)
                near = hb0[hh, e, n].astype(F32) + jnp.where(sends_near, hb1[hh, e, n].astype(F32), 0.0)
                kvo[n, :64, w] = near[:64].astype(BF)
                more = jnp.where(gives_far, hb2[hh, e, n].astype(F32), 0.0)
                kvo[n, 64:, w] = (near[64:] + more).astype(BF)

    t64 = lax.broadcasted_iota(jnp.int32, (PROMPT, 128), 0)
    for place in (0, 2):
        @pl.when(c == place)
        def _():
            arrived(dtx, xr)
            keep = t64 < vis if place == 0 else t64 >= vis
            for hh in (0, 1):
                for b in range(8):
                    kvo[b // 4, :64, pl.ds(KW * hh + 128 * (b % 4), 128)] = jnp.where(
                        keep, dtx[hh, b].astype(F32), 0.0
                    ).astype(BF)

    out = pltpu.make_async_copy(kvo, gkv, lcr)
    out.start()
    each(4, back_left)
    arrived(gq, gqr)
    out.wait()
    arrived(fin.at[:, spans[0]], y2r.at[0])
    last = assemble(0, to_kv)
    for n in (0, 1):
        for p in others:
            z2_back(p, n).wait_send()
    first.wait()
    last.wait()


ANY = pl.BlockSpec(memory_space=pl.ANY)
SMEM = pl.BlockSpec(memory_space=pltpu.SMEM)
DMA = pltpu.SemaphoreType.DMA


def sds(*shape):
    return jax.ShapeDtypeStruct(shape, BF)


def vm(*shape, dtype=BF):
    return pltpu.VMEM(shape, dtype)


def per_device(queries, keys_values, image_rows, cotangent, seq_image, vis_start, comp_lengths):
    gq, gkv, gimg = pl.pallas_call(
        kernel,
        out_shape=[sds(ROWS, 2 * QW), sds(2, ROWS, 2 * KW), sds(8, 2 * QW + 4 * KW)],
        in_specs=[SMEM] * 3 + [ANY] * 4,
        out_specs=[ANY] * 3,
        scratch_shapes=[
            pltpu.SMEM((16,), jnp.int32),
            vm(8, 48, 128), vm(8, 16, 128), vm(8, 32, 128), vm(16, 48, 128), vm(16, 16, 128), vm(16, 32, 128),
            vm(2, 4, 16, 128), vm(16, 16, 128),
            vm(32, 128), vm(32, 128), vm(32, 128), vm(VIS, QW), vm(64, QW), vm(128, 128), vm(256, 256),
            vm(128, 128), vm(128, 128), vm(256, 256),
            vm(CHIP_ROWS, QW), vm(CHIP_ROWS, QW), vm(4, 2, LOCAL, 128), vm(2, 4, VIS, 128), vm(8, PROMPT, 128),
            vm(16, QW),
            vm(KEYS, CHIP_ROWS, dtype=F32), vm(PREFIX, 64, dtype=F32), vm(1, CHIP_ROWS, dtype=F32),
            vm(16, LOCAL, CHIP_ROWS, dtype=F32), vm(16, LOCAL, CHIP_ROWS, dtype=F32),
            vm(4, 8, 4 * CHIP_ROWS, dtype=F32), vm(4, PREFIX, 4 * CHIP_ROWS),
            vm(PREFIX, 128), vm(PREFIX, 128), vm(LOCAL, 128, dtype=F32), vm(LOCAL, 128, dtype=F32),
            vm(4, CHIP_ROWS, 512), vm(4, 2, LOCAL, 128), vm(2, 4, VIS, 128), vm(8, PROMPT, 128), vm(16, 16, 128),
            vm(16, 2, 4, 16, 128), vm(16, 32, 128), vm(2, 4, 2, ROWS, 128), vm(2, 4, 2, ROWS, 128),
            vm(2, 4, 2, 64, 128), vm(2, 8, 64, 128), vm(8, 48, 128), vm(16, 16, 128), vm(16, 32, 128),
            vm(16, 48, 128), vm(8, 48, 128), vm(8, 48, 128), vm(32, 128), vm(2, ROWS, 2 * KW), vm(8, 2 * QW + 4 * KW),
            DMA((2, 8)), DMA((2, 16)), DMA((32,)), DMA((2,)), DMA((4, 4)), DMA((2, 16)), DMA((16,)), DMA((16,)), DMA((2,)),
            DMA((2, 16)), DMA((16,)), DMA((4, 4)), DMA((4,)), DMA((2,)), DMA((2, 16)), DMA((2, 8)),
            DMA((2,)),
            DMA((2,)), DMA((2,)), DMA((2,)), DMA((2,)), DMA((2,)), DMA((4,)), DMA((4,)),
        ] + [DMA(())] * 15 + [pltpu.SemaphoreType.REGULAR],
        compiler_params=pltpu.CompilerParams(
            collective_id=0, has_side_effects=True, vmem_limit_bytes=LIMIT * 2**20
        ),
        name="grads",
    )(
        pltpu.with_memory_space_constraint(seq_image, pltpu.HBM), vis_start,
        pltpu.with_memory_space_constraint(comp_lengths, pltpu.HBM),
        *(pltpu.with_memory_space_constraint(x[0], pltpu.HBM) for x in (queries, cotangent, keys_values, image_rows)),
    )
    return (gq[None], gkv[None], gimg[None])


def solution(mesh):
    placed = (
        P("rollout", "ctx", None),
        P("rollout", None, "ctx", None),
        P("rollout", "ctx", None),
        P("rollout", "ctx", None),
        P(),
        P("rollout"),
        P("rollout", None),
    )
    return jax.shard_map(
        per_device,
        mesh=mesh,
        in_specs=placed,
        out_specs=(
            P("rollout", "ctx", None),
            P("rollout", None, "ctx", None),
            P("rollout", "ctx", None),
        ),
        check_vma=False,
    )
```

```python
import functools
import math

import jax
import jax.numpy as jnp
from jax import lax
from jax.experimental import pallas as pl
from jax.experimental.pallas import tpu as pltpu
from jax.sharding import PartitionSpec as P

HEADS = 32
KV_HEADS = 8
HEAD_DIM = 128
VIS = 256
PROMPT = 64
PREFIX = VIS + PROMPT
GROUPS = 16
SHARDS = 32
CHIPS = 16
ROWS = 128
CHIP_ROWS = 256
HALO = 320
LOCAL = HALO + CHIP_ROWS
KEYS = PREFIX + LOCAL
QW = HEADS * HEAD_DIM // 2
KW = KV_HEADS * HEAD_DIM // 2
MESH = pl.DeviceIdType.MESH
BF = jnp.bfloat16
F32 = jnp.float32
NEG = -1e30
NEAR = 4
PARTS = 2 * NEAR
LIMIT = 40
RS_AT = 2


def remote(src, dst, send, recv, z, c):
    return pltpu.make_async_remote_copy(
        src_ref=src, dst_ref=dst, send_sem=send, recv_sem=recv, device_id=(z, c), device_id_type=MESH
    )


def arrived(ref, sem):
    pltpu.make_async_copy(ref, ref, sem).wait()


def each(count, body):
    def step(k, carry):
        body(k)
        return carry

    lax.fori_loop(0, count, step, 0)


def send_all(count, me, copy, local):
    each(count - 1, lambda k: copy(lax.rem(me + 1 + k, count)).start())
    local(me).start()


def sent_all(count, me, copy):
    each(count - 1, lambda k: copy(lax.rem(me + 1 + k, count)).wait_send())


def send_but(count, me, copy, local):
    def body(k):
        @pl.when(k != me)
        def _():
            copy(k).start()

        @pl.when(k == me)
        def _():
            local(k).start()

    each(count, body)


def sent_but(count, me, copy):
    def body(k):
        @pl.when(k != me)
        def _():
            copy(k).wait_send()

    each(count, body)


def greet(z, c):
    barrier = pltpu.get_barrier_semaphore()
    i = c // 2

    def column(k):
        for to in (lax.rem(z + 1 + k, GROUPS), lax.rem(z + GROUPS - 1 - k, GROUPS)):
            for core in (0, 1):
                pl.semaphore_signal(barrier, inc=1, device_id=(to, 2 * i + core), device_id_type=MESH)

    def plane(k):
        pl.semaphore_signal(
            barrier, inc=1, device_id=(z, lax.rem(c + 1 + k, SHARDS)), device_id_type=MESH
        )

    each(NEAR, column)
    each(SHARDS - 1, plane)


def greeted():
    pl.semaphore_wait(pltpu.get_barrier_semaphore(), SHARDS - 1 + 4 * NEAR)


def one_hot(rows, cols, source):
    o = lax.broadcasted_iota(jnp.int32, (rows, cols), 0)
    n = lax.broadcasted_iota(jnp.int32, (rows, cols), 1)
    return jnp.where(n == source(o), 1.0, 0.0).astype(BF)


def piece_rows():
    shape = (8, 48, 384)
    piece = lax.broadcasted_iota(jnp.int32, shape, 0)
    y = lax.broadcasted_iota(jnp.int32, shape, 1)
    n = lax.broadcasted_iota(jnp.int32, shape, 2)
    half = piece % 2
    of_kv = y < 16
    y = jnp.where(of_kv, y, y - 16)
    row = 2 * (piece // 2) + jnp.where(of_kv, y // 8, y // 16)
    block = jnp.where(of_kv, 32 + 8 * ((y // 4) % 2) + 4 * half + y % 4, 16 * half + y % 16)
    return jnp.where(n == 8 * block + row, 1.0, 0.0)


def kv_order(o):
    y = o // 16
    return (o % 16) * 8 + 4 * (y % 2) + 2 * (y // 4) + (y // 2) % 2


def kv_order_back(o):
    x = o % 8
    return ((x % 4) // 2 * 4 + x % 2 * 2 + x // 4) * 16 + o // 8


def q_order(o):
    return (o % 16) * 16 + o // 16


def kernel(
    seq_ref, vis_ref, len_ref, q, d, kv, img,
    gq, gkv, gimg,
    inv_ref, pieces, z1k, z1q, stage, z2k, z2q, kvp, qi, ta, tb, tm, ds, dnext, to_kv, to_q, kv_p, kv_pb, q_p,
    q2, d2, kvloc, kvimg, kvtxt, imgd,
    bias, ibias, valid, el, dwl, stat, sp, kp, vp, dkl, dvl,
    dq2, dkvloc, dkvimg, dkvtxt, heads,
    rsi, rst, hb0, hb1, hb2, dtx, rows, zbk, zbq, stage2, stage3, fin, tx, kvo, io,
    z1s, z2s, txs, sws, has, ags, ats, dss, dns, ris, rts, hrs, qrs, xs, y1s, y2s, ims,
    z1r, z2r, kir, y1r, y2r, klr, kfr,
    tar, tbr, q2r, d2r, ktr, d0r, dnr, rir, rtr, h0r, h1r, h2r, gqr, xr, lcr, far_sem,
):
    z = lax.axis_index("rollout")
    c = lax.axis_index("ctx")
    i = c // 2
    h = c % 2
    sib = 2 * i + 1 - h
    scale = 1.0 / math.sqrt(HEAD_DIM)
    to_log2 = scale * math.log2(math.e)
    vis = vis_ref[0]
    nt = (((1,), (1,)), ((), ()))
    load = pltpu.make_async_copy(img, io, lcr)
    load.start()
    greet(z, c)

    in_pieces = piece_rows()
    load.wait()
    blocks = jnp.concatenate([io[:, 128 * k : 128 * (k + 1)].astype(F32) for k in range(48)], axis=0).astype(BF)
    pieces[...] = jnp.dot(in_pieces.astype(BF).reshape(384, 384), blocks, preferred_element_type=F32).astype(BF).reshape(8, 48, 128)
    greeted()
    for to in (lax.rem(z + NEAR, GROUPS), lax.rem(z + GROUPS - NEAR, GROUPS)):
        for core in (0, 1):
            pl.semaphore_signal(far_sem, inc=1, device_id=(to, 2 * i + core), device_id_type=MESH)

    spans = (pl.ds(0, 16), pl.ds(16, 32))
    z1b, z2b, zbs = (z1k, z1q), (z2k, z2q), (zbk, zbq)

    def z1(p, n):
        j = lax.rem(z + GROUPS + 1 - NEAR + p, GROUPS)
        return remote(pieces.at[p // 2 * 2 + j % 2, spans[n]], z1b[n].at[p], z1s.at[n, p], z1r.at[n], j, c)

    def z1_here(n):
        p = NEAR - 1
        return pltpu.make_async_copy(
            pieces.at[p // 2 * 2 + z % 2, spans[n]], z1b[n].at[p], z1r.at[n]
        )

    others = [p for p in range(PARTS) if p != NEAR - 1]
    for n in (0, 1):
        for p in others:
            z1(p, n).start()
        z1_here(n).start()

    def text_src(k):
        ii, hh = k // 2, k % 2
        b = ii % 8
        return kv.at[
            b // 4,
            pl.ds(pl.multiple_of(32 * (ii // 8), 32), 32),
            pl.ds(pl.multiple_of(KW * hh + 128 * (b % 4), 128), 128),
        ]

    for place, buf, sem in ((0, ta, tar), (2, tb, tbr)):
        @pl.when(c == place)
        def _():
            send_all(
                SHARDS, c,
                lambda k: remote(text_src(k), buf, txs.at[k], sem, z, k),
                lambda k: pltpu.make_async_copy(text_src(k), buf, sem),
            )

    def cols(core, width):
        return pl.ds(pl.multiple_of(width * core, width), width)

    def rows_of(core, first):
        return pl.ds(pl.multiple_of(first + ROWS * core, 64), ROWS)

    def block(k):
        return pl.ds(pl.multiple_of(16 * k, 16), 16)

    def half_of(k):
        return pl.ds(pl.multiple_of(32 * (k // 8), 32), 32)

    def ahead(n):
        return lax.rem(i + n, CHIPS)

    my_rows = rows_of(h, 0)
    own_rows = rows_of(h, HALO)
    near_rows = rows_of(h, 64)

    def kv_cols(core, e):
        return pl.ds(pl.multiple_of(KW * core + 128 * e, 128), 128)

    sends_near = (i >= 1) & (i < CHIPS - 1)
    sends_far = (i >= 2) & (i < CHIPS - 1)
    has_near = i >= 2
    has_far = i >= 3
    far_rows = pl.ds(0, 64)

    def own_in(e):
        return remote(
            kv.at[:, :, kv_cols(1 - h, e)], kvloc.at[e, :, own_rows, :], has.at[2, e], klr.at[e], z, sib
        )

    def near_in(e):
        return [
            remote(
                kv.at[:, :, kv_cols(hh, e)], kvloc.at[e, :, near_rows, :], has.at[hh, e], klr.at[e], z,
                2 * ahead(1) + hh,
            )
            for hh in (0, 1)
        ]

    def far_in(e):
        return remote(
            kvloc.at[e, :, pl.ds(HALO - 64, 64), :], kvloc.at[e, :, far_rows, :], has.at[3, e], kfr.at[e], z,
            2 * ahead(1) + h,
        )

    def halo_start(e):
        @pl.when(sends_near)
        def _():
            for copy in near_in(e):
                copy.start()

        own_in(e).start()
        pltpu.make_async_copy(kv.at[:, :, kv_cols(h, e)], kvloc.at[e, :, own_rows, :], klr.at[e]).start()

    def near_come(e):
        @pl.when(has_near)
        def _():
            arrived(kvloc.at[e, :, pl.ds(64, LOCAL - 64), :], klr.at[e])

        @pl.when(i < 2)
        def _():
            arrived(kvloc.at[e, :, pl.ds(HALO, CHIP_ROWS), :], klr.at[e])
            kvloc[e, :, 64:HALO, :] = jnp.zeros((2, HALO - 64, 128), BF)

        @pl.when(sends_far)
        def _():
            far_in(e).start()

    def far_come(e):
        @pl.when(has_far)
        def _():
            arrived(kvloc.at[e, :, far_rows, :], kfr.at[e])

        @pl.when(i < 3)
        def _():
            kvloc[e, :, 0:64, :] = jnp.zeros((2, 64, 128), BF)

    swaps = [
        remote(d.at[:, cols(1 - h, QW)], d2.at[my_rows, :], sws.at[0], d2r, z, sib),
        remote(q.at[:, cols(1 - h, QW)], q2.at[my_rows, :], sws.at[1], q2r, z, sib),
    ]
    halo_start(0)
    for copy in swaps:
        copy.start()
    pltpu.make_async_copy(d.at[:, cols(h, QW)], d2.at[my_rows, :], d2r).start()
    pltpu.make_async_copy(q.at[:, cols(h, QW)], q2.at[my_rows, :], q2r).start()
    halo_start(1)

    def dnear(hh):
        return remote(d.at[pl.ds(0, 64), pl.ds(QW * hh, QW)], dnext, dns.at[hh], dnr, z, hh)

    def dsend(k):
        return remote(ds.at[block(k), :], imgd, dss.at[k], d0r, z, 2 * k + h)

    @pl.when(c == 2)
    def _():
        for hh in (0, 1):
            dnear(hh).start()

    def rest_of_image():
        arrived(dnext, dnr)
        shift = one_hot(64, CHIP_ROWS, lambda r: r + 192 + vis)
        more = one_hot(64, 64, lambda r: r + 192 + vis - CHIP_ROWS)
        for part in range(4):
            w = pl.ds(part * 512, 512)
            rows_d = jnp.dot(shift, d2[:, w], preferred_element_type=F32)
            rows_d = rows_d + jnp.dot(more, dnext[:, w], preferred_element_type=F32)
            ds[192:, w] = rows_d.astype(BF)
        each(4, lambda k: dsend(k + 12).start())

    to_kv[...] = in_pieces[:, :16, 256:].astype(BF).reshape(128, 128).T
    to_q[...] = in_pieces[:, 16:, :256].astype(BF).reshape(256, 256).T
    kv_p[...] = one_hot(128, 128, kv_order)
    kv_pb[...] = one_hot(128, 128, kv_order_back)
    q_p[...] = one_hot(256, 256, q_order)
    for o in range(GROUPS):
        user = jnp.int32(0)
        for g in range(GROUPS):
            user = jnp.where(seq_ref[g] == o, g, user)
        inv_ref[o] = user

    def slot_positions(lanes):
        r = lax.broadcasted_iota(jnp.int32, (PREFIX, lanes), 0)
        text = r - VIS
        return jnp.where(r < VIS, vis + r, jnp.where(text < vis, text, r))

    pos = CHIP_ROWS * i + lax.broadcasted_iota(jnp.int32, (1, CHIP_ROWS), 1)
    begin = jnp.full((1, CHIP_ROWS), PREFIX, jnp.int32)
    edge = jnp.int32(PREFIX)
    for k in range(16):
        edge = edge + len_ref[0, k]
        begin = jnp.where(pos >= edge, edge, begin)
    begin = jnp.where(pos < PREFIX, pos + 1, begin)
    valid[...] = jnp.where((pos >= vis) & (pos < vis + VIS), 0.0, 1.0)
    bias[:PREFIX, :] = jnp.where(slot_positions(CHIP_ROWS) <= pos, 0.0, NEG)
    at = CHIP_ROWS * i - HALO + lax.broadcasted_iota(jnp.int32, (LOCAL, CHIP_ROWS), 0)
    bias[PREFIX:, :] = jnp.where((at >= begin) & (at <= pos), 0.0, NEG)
    ipos = vis + 16 * i + lax.broadcasted_iota(jnp.int32, (1, 64), 1) % 16
    ibias[...] = jnp.where(slot_positions(64) <= ipos, 0.0, NEG)

    to_core = z % 2
    slot = 8 * h + z // 2
    here = jnp.where(to_core == h, z, GROUPS)
    here_back = jnp.where(to_core == h, slot, GROUPS)

    def part_of(o, j):
        return jnp.minimum((j - o + NEAR - 1) & (GROUPS - 1), PARTS - 1)

    def z2(g, n):
        return remote(
            stage.at[g, spans[n]], z2b[n].at[slot], z2s.at[n, g], z2r.at[n], g, 2 * i + to_core
        )

    def z2_here(g, n):
        return pltpu.make_async_copy(stage.at[g, spans[n]], z2b[n].at[slot], z2r.at[n])

    for n in (0, 1):
        arrived(z1b[n], z1r.at[n])

        def pick(g):
            stage[g, spans[n]] = z1b[n][part_of(seq_ref[g], z)]

        each(GROUPS, pick)
        if n == 0:
            pl.semaphore_wait(far_sem, 4)
        send_but(GROUPS, here, lambda g: z2(g, n), lambda g: z2_here(g, n))

    @pl.when(i == 0)
    def _():
        arrived(d2, d2r)
        shift = one_hot(192, CHIP_ROWS, lambda r: r + vis)
        for part in range(4):
            w = pl.ds(part * 512, 512)
            ds[:192, w] = jnp.dot(shift, d2[:, w], preferred_element_type=F32).astype(BF)
        pltpu.make_async_copy(ds.at[block(0), :], imgd, d0r).start()
        each(11, lambda k: dsend(k + 1).start())

    halo_start(2)
    halo_start(3)

    image = seq_ref[z]

    def slot_of(s, rp):
        even = (image + 1 - NEAR + 2 * rp) & (GROUPS - 1)
        j = jnp.where((even & 1) == h, even, (even + 1) & (GROUPS - 1))
        return 8 * s + j // 2

    def come(n):
        return jnp.concatenate([z2b[n][slot_of(s, rp)] for s in (0, 1) for rp in range(4)], axis=0)

    def aim(half, k):
        return remote(kvp.at[half], kvimg.at[half, :, block(i), :], ags.at[half, k], kir.at[half], z, 2 * k + h)

    def hand_round():
        arrived(z2b[0], z2r.at[0])
        kvp[...] = jnp.dot(kv_p[...], come(0), preferred_element_type=F32).astype(BF).reshape(2, 4, 16, 128)

        for half in (0, 1):
            send_all(
                CHIPS, i, lambda k: aim(half, k),
                lambda k: pltpu.make_async_copy(kvp.at[half], kvimg.at[half, :, block(i), :], kir.at[half]),
            )

    arrived(q2, q2r)

    @pl.when(i > 0)
    def _():
        arrived(d2, d2r)


    def head_cols(e, k):
        return pl.ds(pl.multiple_of(512 * e + 128 * k, 128), 128)

    def local_scores(e):
        far_come(e)
        k_rows = kvloc[e, 0]
        v_rows = kvloc[e, 1]
        for k in range(4):
            w128 = head_cols(e, k)
            n = 4 * e + k
            top = lax.dot_general(k_rows, q2[:, w128], nt, preferred_element_type=F32) * to_log2 + bias[PREFIX:, :]
            peak = jnp.max(top, axis=0, keepdims=True)
            ex = jnp.exp2(top - peak)
            dw = lax.dot_general(v_rows, d2[:, w128], nt, preferred_element_type=F32)
            el[n] = ex
            dwl[n] = dw
            lanes = pl.ds(CHIP_ROWS * k, CHIP_ROWS)
            stat[e, 0:1, lanes] = peak
            stat[e, 1:2, lanes] = jnp.sum(ex, axis=0, keepdims=True)
            stat[e, 2:3, lanes] = jnp.sum(ex * dw, axis=0, keepdims=True)

    def prefix_come():
        arrived(z2b[1], z2r.at[1])
        qi[...] = jnp.dot(q_p[...], come(1), preferred_element_type=F32).astype(BF).reshape(16, 16, 128)
        arrived(kvtxt, ktr)
        arrived(imgd, d0r)

    def rimg(half, k):
        return remote(dkvimg.at[half, :, block(k), :], rsi.at[i, half], ris.at[half, k], rir, z, 2 * k + h)

    def rtxt(k):
        return remote(dkvtxt.at[k % 8, half_of(k), :], rst.at[i], rts.at[k], rtr, z, 2 * k + h)

    def four(x):
        return jnp.concatenate([x] * 4, axis=1)

    def prefix_grads(e):
        place = 2 * (e % 2)

        @pl.when(e == 0)
        def _():
            prefix_come()

        @pl.when(e % 2 == 0)
        def _():
            arrived(kvimg.at[e // 2], kir.at[e // 2])

        kp[:VIS, :] = kvimg[e // 2, place]
        kp[VIS:, :] = kvtxt[e]
        vp[:VIS, :] = kvimg[e // 2, place + 1]
        vp[VIS:, :] = kvtxt[4 + e]
        k_rows = kp[...]
        v_rows = vp[...]

        def scores(q_rows, d_rows, mask):
            top = lax.dot_general(k_rows, q_rows, nt, preferred_element_type=F32) * to_log2 + mask
            dw = lax.dot_general(v_rows, d_rows, nt, preferred_element_type=F32)
            return top, jnp.max(top, axis=0, keepdims=True), dw

        q_rows = qi[pl.ds(4 * e, 4)].reshape(64, 128)
        wide = pl.ds(pl.multiple_of(512 * e, 512), 512)
        d_rows = imgd[:, wide]
        d_rows = jnp.concatenate([d_rows[:, 128 * k : 128 * (k + 1)] for k in range(4)], axis=0)
        top, peak, dw = scores(q_rows, d_rows, ibias[...])
        ex = jnp.exp2(top - peak)
        inv = 1.0 / jnp.sum(ex, axis=0, keepdims=True)
        delta = jnp.sum(ex * dw, axis=0, keepdims=True) * inv
        w = ex * inv
        s = (w * (dw - delta)).astype(BF)
        dk = jnp.dot(s, q_rows, preferred_element_type=F32)
        dv = jnp.dot(w.astype(BF), d_rows, preferred_element_type=F32)
        dqi = lax.dot_general(s, k_rows, (((0,), (0,)), ((), ())), preferred_element_type=F32) * scale
        heads[pl.ds(4 * e, 4)] = dqi.astype(BF).reshape(4, 16, 128)

        q_rows = jnp.concatenate([q2[:, head_cols(e, k)] for k in range(4)], axis=0)
        d_rows = jnp.concatenate([d2[:, head_cols(e, k)] for k in range(4)], axis=0)
        top, peak, dw = scores(q_rows, d_rows, four(bias[:PREFIX, :]))
        low = stat[e, 0:1, :]
        peak = jnp.maximum(peak, low)
        ex = jnp.exp2(top - peak)
        shrink = jnp.exp2(low - peak)
        inv = 1.0 / (jnp.sum(ex, axis=0, keepdims=True) + stat[e, 1:2, :] * shrink)
        delta = (jnp.sum(ex * dw, axis=0, keepdims=True) + stat[e, 2:3, :] * shrink) * inv
        inv = inv * four(valid[...])
        w = ex * inv
        s = (w * (dw - delta)).astype(BF)
        dk = dk + jnp.dot(s, q_rows, preferred_element_type=F32)
        dv = dv + jnp.dot(w.astype(BF), d_rows, preferred_element_type=F32)
        sp[e] = s
        stat[e, 0:1, :] = shrink * inv
        stat[e, 1:2, :] = delta
        dk = (dk * scale).astype(BF)
        dv = dv.astype(BF)
        dkvimg[e // 2, place] = dk[:VIS]
        dkvimg[e // 2, place + 1] = dv[:VIS]
        dkvtxt[e] = dk[VIS:]
        dkvtxt[4 + e] = dv[VIS:]

        @pl.when(e % 2 == 1)
        def _():
            half = e // 2
            send_all(
                CHIPS, i,
                lambda k: rimg(half, k),
                lambda k: pltpu.make_async_copy(dkvimg.at[half, :, block(k), :], rsi.at[i, half], rir),
            )

    def z1_back(t, n):
        return remote(
            stage2.at[t, spans[n]], zbs[n].at[z], y1s.at[n, t], y1r.at[n], 2 * (t % 8) + h, 2 * i + t // 8
        )

    def back_to_rows(n, value):
        rows[:, spans[n]] = value.astype(BF).reshape(8, 16 * (n + 1), 128)

        def pick(t):
            stage2[t, spans[n]] = rows[4 * (t // 8) + part_of(image, 2 * (t % 8) + h) // 2, spans[n]]

        each(16, pick)
        send_but(
            16, here_back, lambda t: z1_back(t, n),
            lambda t: pltpu.make_async_copy(stage2.at[t, spans[n]], zbs[n].at[z], y1r.at[n]),
        )

    def z2_back(p, n):
        o = lax.rem(z + GROUPS + NEAR - 1 - p, GROUPS)
        return remote(
            stage3.at[p, spans[n]], fin.at[p // 2 * 2 + z % 2, spans[n]], y2s.at[n, p], y2r.at[n], o, c
        )

    def second_back(n):
        arrived(zbs[n], y1r.at[n])

        def pick(p):
            stage3[p, spans[n]] = zbs[n][inv_ref[lax.rem(z + GROUPS + NEAR - 1 - p, GROUPS)]]

        each(PARTS, pick)
        for p in others:
            z2_back(p, n).start()
        p = NEAR - 1
        pltpu.make_async_copy(
            stage3.at[p, spans[n]], fin.at[p // 2 * 2 + z % 2, spans[n]], y2r.at[n]
        ).start()

    near_come(0)

    @pl.when(i == 0)
    def _():
        rest_of_image()

    hand_round()

    arrived(ta, tar)
    arrived(tb, tbr)
    t = 32 * (i // 8) + lax.broadcasted_iota(jnp.int32, (32, 128), 0)
    tm[...] = jnp.where(t < vis, ta[...].astype(F32), tb[...].astype(F32)).astype(BF)
    txt_part = kvtxt.at[i % 8, half_of(i), :]

    def atx(k):
        return remote(tm, txt_part, ats.at[k], ktr, z, 2 * k + h)

    send_all(CHIPS, i, atx, lambda k: pltpu.make_async_copy(tm, txt_part, ktr))
    near_come(1)

    def step(n):
        @pl.when((n != 2) & (n < 4))
        def _():
            local_scores(n)

        @pl.when(n == 1)
        def _():
            near_come(2)
            near_come(3)

        @pl.when(n > 0)
        def _():
            prefix_grads(n - 1)

        @pl.when(n == 2)
        def _():
            local_scores(n)

    each(5, step)
    back_to_rows(1, jnp.dot(q_p[...], heads[...].reshape(256, 128), preferred_element_type=F32))
    send_all(CHIPS, i, rtxt, lambda k: pltpu.make_async_copy(dkvtxt.at[k % 8, half_of(k), :], rst.at[i], rtr))

    def near_back(e):
        return [
            remote(
                dkvloc.at[e, :, rows_of(s, 64), :], hb1.at[h, e], hrs.at[s, e], h1r, z, 2 * ahead(CHIPS - 1) + s
            )
            for s in (0, 1)
        ]

    def far_back(e):
        return remote(
            dkvloc.at[e, :, far_rows, :], hb2.at[h, e], hrs.at[2, e], h2r, z, 2 * ahead(CHIPS - 2) + 1
        )

    def own_back(e):
        return [
            remote(dkvloc.at[e, :, rows_of(1 - h, HALO), :], hb0.at[h, e], hrs.at[3, e], h0r, z, sib),
            remote(dq2.at[e, rows_of(1 - h, 0), :], gq.at[:, out_cols(e)], qrs.at[e], gqr, z, sib),
        ]

    def back_start(e):
        @pl.when(has_near)
        def _():
            for copy in near_back(e):
                copy.start()

        @pl.when(has_far)
        def _():
            far_back(e).start()

        for copy in own_back(e):
            copy.start()

    def back_left(e):
        @pl.when(has_near)
        def _():
            for copy in near_back(e):
                copy.wait_send()

        @pl.when(has_far)
        def _():
            far_back(e).wait_send()

        for copy in own_back(e):
            copy.wait_send()

    def out_cols(e):
        return pl.ds(pl.multiple_of(QW * h + 512 * e, 512), 512)

    def local_grads(e):
        k_rows = kvloc[e, 0]
        kt = k_rows.T
        kp[:VIS, :] = kvimg[e // 2, 2 * (e % 2)]
        kp[VIS:, :] = kvtxt[e]
        kpt = kp[...].T
        for k in range(4):
            n = 4 * e + k
            q_rows = q2[:, head_cols(e, k)]
            d_rows = d2[:, head_cols(e, k)]
            lanes = pl.ds(CHIP_ROWS * k, CHIP_ROWS)
            w = el[n] * stat[e, 0:1, lanes]
            s = (w * (dwl[n] - stat[e, 1:2, lanes])).astype(BF)
            part = jnp.dot(s, q_rows, preferred_element_type=F32)
            dkl[...] = part if k == 0 else dkl[...] + part
            part = jnp.dot(w.astype(BF), d_rows, preferred_element_type=F32)
            dvl[...] = part if k == 0 else dvl[...] + part
            dqt = jnp.dot(kt, s, preferred_element_type=F32) + jnp.dot(kpt, sp[e, :, lanes], preferred_element_type=F32)
            dq2[e, :, 128 * k : 128 * (k + 1)] = (dqt * scale).T.astype(BF)
        dkvloc[e, 0] = (dkl[...] * scale).astype(BF)
        dkvloc[e, 1] = dvl[...].astype(BF)
        back_start(e)
        pltpu.make_async_copy(dkvloc.at[e, :, rows_of(h, HALO), :], hb0.at[h, e], h0r).start()
        pltpu.make_async_copy(dq2.at[e, rows_of(h, 0), :], gq.at[:, out_cols(e)], gqr).start()

    txt_slot = dtx.at[h, i % 8, half_of(i), :]

    def reduce_prefix():
        arrived(rsi, rir)
        total = rsi[0].astype(F32)
        for k in range(1, CHIPS):
            total = total + rsi[k].astype(F32)
        total = total.astype(BF).reshape(128, 128)
        back_to_rows(0, jnp.dot(kv_pb[...], total, preferred_element_type=F32))
        arrived(rst, rtr)
        total = rst[0].astype(F32)
        for k in range(1, CHIPS):
            total = total + rst[k].astype(F32)
        tx[...] = total.astype(BF)
        for n, place in ((0, 0), (1, 2)):
            @pl.when(c != place)
            def _():
                remote(tx, txt_slot, xs.at[n], xr, z, place).start()

            @pl.when(c == place)
            def _():
                pltpu.make_async_copy(tx, txt_slot, xr).start()

    def rest(e):
        local_grads(e)

        @pl.when(e == RS_AT)
        def _():
            reduce_prefix()

    each(4, rest)

    second_back(1)

    for n in (0, 1):
        for p in others:
            z1(p, n).wait_send()
        sent_but(GROUPS, here, lambda g: z2(g, n))
    for place, buf, sem in ((0, ta, tar), (2, tb, tbr)):
        @pl.when(c == place)
        def _():
            sent_all(SHARDS, c, lambda k: remote(text_src(k), buf, txs.at[k], sem, z, k))

    for copy in swaps:
        copy.wait_send()

    def halo_left(e):
        own_in(e).wait_send()

        @pl.when(sends_near)
        def _():
            for copy in near_in(e):
                copy.wait_send()

        @pl.when(sends_far)
        def _():
            far_in(e).wait_send()

    each(4, halo_left)

    sent_all(CHIPS, i, atx)
    for half in (0, 1):
        sent_all(CHIPS, i, lambda k: aim(half, k))

    @pl.when(i == 0)
    def _():
        each(15, lambda k: dsend(k + 1).wait_send())

    @pl.when(c == 2)
    def _():
        for hh in (0, 1):
            dnear(hh).wait_send()

    second_back(0)

    def assemble(n, order):
        blocks = jnp.dot(order[...], fin[:, spans[n]].reshape(-1, 128), preferred_element_type=F32)
        begin, width = ((2 * QW, 4 * KW), (0, 2 * QW))[n]
        for k in range(width // 128):
            io[:, begin + 128 * k : begin + 128 * (k + 1)] = blocks[8 * k : 8 * (k + 1)].astype(BF)
        span = pl.ds(begin, width)
        copy = pltpu.make_async_copy(io.at[:, span], gimg.at[:, span], ims.at[n])
        copy.start()
        return copy

    arrived(fin.at[:, spans[1]], y2r.at[1])
    first = assemble(1, to_q)

    for half in (0, 1):
        sent_all(CHIPS, i, lambda k: rimg(half, k))
    sent_all(CHIPS, i, rtxt)
    for n in (0, 1):
        sent_but(16, here_back, lambda t: z1_back(t, n))
    for n, place in ((0, 0), (1, 2)):
        @pl.when(c != place)
        def _():
            remote(tx, txt_slot, xs.at[n], xr, z, place).wait_send()

    arrived(hb0, h0r)
    @pl.when(sends_near)
    def _():
        arrived(hb1, h1r)

    gives_far = (h == 1) & (i >= 1) & (i < CHIPS - 2)

    @pl.when(gives_far)
    def _():
        arrived(hb2, h2r)

    for hh in (0, 1):
        for e in range(4):
            for n in (0, 1):
                w = pl.ds(KW * hh + 128 * e, 128)
                near = hb0[hh, e, n].astype(F32) + jnp.where(sends_near, hb1[hh, e, n].astype(F32), 0.0)
                kvo[n, :64, w] = near[:64].astype(BF)
                more = jnp.where(gives_far, hb2[hh, e, n].astype(F32), 0.0)
                kvo[n, 64:, w] = (near[64:] + more).astype(BF)

    t64 = lax.broadcasted_iota(jnp.int32, (PROMPT, 128), 0)
    for place in (0, 2):
        @pl.when(c == place)
        def _():
            arrived(dtx, xr)
            keep = t64 < vis if place == 0 else t64 >= vis
            for hh in (0, 1):
                for b in range(8):
                    kvo[b // 4, :64, pl.ds(KW * hh + 128 * (b % 4), 128)] = jnp.where(
                        keep, dtx[hh, b].astype(F32), 0.0
                    ).astype(BF)

    out = pltpu.make_async_copy(kvo, gkv, lcr)
    out.start()
    each(4, back_left)
    arrived(gq, gqr)
    out.wait()
    for n in (0, 1):
        for p in others:
            z2_back(p, n).wait_send()
    first.wait()
    arrived(fin.at[:, spans[0]], y2r.at[0])
    assemble(0, to_kv).wait()


ANY = pl.BlockSpec(memory_space=pl.ANY)
SMEM = pl.BlockSpec(memory_space=pltpu.SMEM)
DMA = pltpu.SemaphoreType.DMA


def sds(*shape):
    return jax.ShapeDtypeStruct(shape, BF)


def vm(*shape, dtype=BF):
    return pltpu.VMEM(shape, dtype)


def per_device(queries, keys_values, image_rows, cotangent, seq_image, vis_start, comp_lengths):
    gq, gkv, gimg = pl.pallas_call(
        kernel,
        out_shape=[sds(ROWS, 2 * QW), sds(2, ROWS, 2 * KW), sds(8, 2 * QW + 4 * KW)],
        in_specs=[SMEM] * 3 + [ANY] * 4,
        out_specs=[ANY] * 3,
        scratch_shapes=[
            pltpu.SMEM((16,), jnp.int32),
            vm(8, 48, 128), vm(8, 16, 128), vm(8, 32, 128), vm(16, 48, 128), vm(16, 16, 128), vm(16, 32, 128),
            vm(2, 4, 16, 128), vm(16, 16, 128),
            vm(32, 128), vm(32, 128), vm(32, 128), vm(VIS, QW), vm(64, QW), vm(128, 128), vm(256, 256),
            vm(128, 128), vm(128, 128), vm(256, 256),
            vm(CHIP_ROWS, QW), vm(CHIP_ROWS, QW), vm(4, 2, LOCAL, 128), vm(2, 4, VIS, 128), vm(8, PROMPT, 128),
            vm(16, QW),
            vm(KEYS, CHIP_ROWS, dtype=F32), vm(PREFIX, 64, dtype=F32), vm(1, CHIP_ROWS, dtype=F32),
            vm(16, LOCAL, CHIP_ROWS, dtype=F32), vm(16, LOCAL, CHIP_ROWS, dtype=F32),
            vm(4, 8, 4 * CHIP_ROWS, dtype=F32), vm(4, PREFIX, 4 * CHIP_ROWS),
            vm(PREFIX, 128), vm(PREFIX, 128), vm(LOCAL, 128, dtype=F32), vm(LOCAL, 128, dtype=F32),
            vm(4, CHIP_ROWS, 512), vm(4, 2, LOCAL, 128), vm(2, 4, VIS, 128), vm(8, PROMPT, 128), vm(16, 16, 128),
            vm(16, 2, 4, 16, 128), vm(16, 32, 128), vm(2, 4, 2, ROWS, 128), vm(2, 4, 2, ROWS, 128),
            vm(2, 4, 2, 64, 128), vm(2, 8, 64, 128), vm(8, 48, 128), vm(16, 16, 128), vm(16, 32, 128),
            vm(16, 48, 128), vm(8, 48, 128), vm(8, 48, 128), vm(32, 128), vm(2, ROWS, 2 * KW), vm(8, 2 * QW + 4 * KW),
            DMA((2, 8)), DMA((2, 16)), DMA((32,)), DMA((2,)), DMA((4, 4)), DMA((2, 16)), DMA((16,)), DMA((16,)), DMA((2,)),
            DMA((2, 16)), DMA((16,)), DMA((4, 4)), DMA((4,)), DMA((2,)), DMA((2, 16)), DMA((2, 8)),
            DMA((2,)),
            DMA((2,)), DMA((2,)), DMA((2,)), DMA((2,)), DMA((2,)), DMA((4,)), DMA((4,)),
        ] + [DMA(())] * 15 + [pltpu.SemaphoreType.REGULAR],
        compiler_params=pltpu.CompilerParams(
            collective_id=0, has_side_effects=True, vmem_limit_bytes=LIMIT * 2**20
        ),
        name="grads",
    )(
        pltpu.with_memory_space_constraint(seq_image, pltpu.HBM), vis_start,
        pltpu.with_memory_space_constraint(comp_lengths, pltpu.HBM),
        *(pltpu.with_memory_space_constraint(x[0], pltpu.HBM) for x in (queries, cotangent, keys_values, image_rows)),
    )
    return (gq[None], gkv[None], gimg[None])


def solution(mesh):
    placed = (
        P("rollout", "ctx", None),
        P("rollout", None, "ctx", None),
        P("rollout", "ctx", None),
        P("rollout", "ctx", None),
        P(),
        P("rollout"),
        P("rollout", None),
    )
    return jax.shard_map(
        per_device,
        mesh=mesh,
        in_specs=placed,
        out_specs=(
            P("rollout", "ctx", None),
            P("rollout", None, "ctx", None),
            P("rollout", "ctx", None),
        ),
        check_vma=False,
    )
```
